256 devices in a mesh: row: 64 (over z, x, y_lo), col: 4 (over y_hi, core).
Axes of the slice: x: 4, y: 4 (y_hi: 2, y_lo: 2; y = y_hi * 2 + y_lo), z: 8, core: 2. Of those that a mesh axis runs over, the one named last changes fastest.
Arguments:
- features: float32 [98304, 256], P(('row', 'col')), may hold values from -6 to 6
- w_qkv: bfloat16 [256, 768], replicated, may hold values from -0.375 to 0.375
- w_out: bfloat16 [256, 256], replicated, may hold values from -0.375 to 0.375
- head_bias: float32 [4], replicated, may hold values from -3 to 1
- out_gain: float32 [256], replicated, may hold values from 0.1 to 1.9
- tile_rows: int32 [256, 256], P(('row', 'col')), may hold values from 0 to 767, as said below
- tile_cols: int32 [256, 256], P(('row', 'col')), may hold values from 0 to 767, as said below
- tile_masks: int32 [256, 256, 2048], P(('row', 'col')), may hold values from 0 to 255
- tile_count: int32 [256], P(('row', 'col')), may hold values from 1 to 256, as said below
Outputs:
- updated: float32 [98304, 256], P(('row', 'col'))
The draws below stay inside these ranges and needn't reach their ends.
Inputs may be any that keep to these rules, and one draw needn't show every extreme that they name: `tile_rows`: list d = r * 4 + c names only destination tiles of blocks r * 4 to r * 4 + 4 - 1 and only source tiles of blocks whose index modulo 4 is c; within one list no tile appears twice. `tile_cols`: see tile_rows. `tile_count`: some list has all 256 slots live.
All inputs are finite; a program needn't handle non-finite values.
Results may differ from the reference program's by a relative error of at most 0.0042.
Values may be sent and summed in bfloat16 or wider, within the bound.
A program may use at most 192 MiB of HBM per device.

```python
import math
import jax
import jax.numpy as jnp
from jax import lax

D = 256
HEADS = 4
TILE = 128
ND = 384
TILES_DEV = 256
NODES = 98304
N_ROW = 64
N_COL = 4
DEVICES = 256


def tile_places(key):
    row_tiles = N_COL * ND // TILE
    col_tiles = N_ROW * ND // TILE
    block_tiles = ND // TILE
    device_keys = jax.random.split(key, DEVICES)
    places = jax.vmap(lambda sub_key: jax.random.permutation(sub_key, row_tiles * col_tiles)[:TILES_DEV])(device_keys).astype(jnp.int32)
    device_index = jnp.arange(DEVICES, dtype=jnp.int32)[:, None]
    block_row = device_index // N_COL
    block_col = device_index % N_COL
    rows_global = block_row * row_tiles + places // col_tiles
    local_col = places % col_tiles
    cols_global = (local_col // block_tiles * N_COL + block_col) * block_tiles + local_col % block_tiles
    return (rows_global.astype(jnp.int32), cols_global.astype(jnp.int32))


def draw_tile_rows(key, part):
    return tile_places(key)[0]


def draw_tile_cols(key, part):
    return tile_places(key)[1]


def draw_tile_count(key, part):
    key = jax.random.fold_in(key, 7)
    first_key, second_key, third_key = jax.random.split(key, 3)
    halving = jax.random.randint(first_key, (DEVICES,), 0, 4)
    base_count = jnp.right_shift(jnp.full((DEVICES,), TILES_DEV, jnp.int32), halving.astype(jnp.int32))
    trimmed = jax.random.randint(second_key, (DEVICES,), 0, max(1, TILES_DEV // 8))
    counts = jnp.maximum(1, base_count - trimmed)
    chosen = jax.random.randint(third_key, (), 0, DEVICES)
    return jnp.where(jnp.arange(DEVICES) == chosen, TILES_DEV, counts).astype(jnp.int32)


def touch_ends(array, key, low, largest):
    extent = array.shape
    spot = [jax.random.randint(jax.random.fold_in(key, axis), (), 0, extent[axis]) for axis in range(len(extent))]
    array = array.at[tuple(spot)].set(low)
    longest = extent.index(max(extent))
    spot[longest] = (spot[longest] + 1) % extent[longest]
    return array.at[tuple(spot)].set(largest)


def block_scale(rng, shape, cuts, least, high):
    loudness, own = 1.0, jax.random.fold_in(rng, 6)
    for axis_at, shards_of in cuts:
        steps = jnp.exp(jax.random.uniform(jax.random.fold_in(own, axis_at), (shards_of,), jnp.float32, least / len(cuts), high / len(cuts)))
        loudness = loudness * jnp.repeat(steps, shape[axis_at] // shards_of).reshape([-1 if axis == axis_at else 1 for axis in range(len(shape))])
    return loudness


def scatter_about(stream_key, dims, spread, bound, cuts=(), held_as=jnp.bfloat16):
    result = spread * jax.random.normal(stream_key, dims, jnp.float32)
    if cuts:
        result = result * block_scale(stream_key, dims, cuts, -0.22, 0.18)
    return jnp.clip(result, -bound, bound).astype(held_as)


def setup_inputs(seed: int = 0) -> dict:
    key_list = jax.random.split(jax.random.key(seed), 10)
    features = scatter_about(key_list[0], (NODES, D), 1.0, 6.0, ((0, 256),), jnp.float32)
    w_qkv = scatter_about(key_list[1], (D, 3 * D), D ** -0.5, 0.375)
    w_out = scatter_about(key_list[2], (D, D), D ** -0.5, 0.375)
    head_bias = jnp.clip(jax.random.uniform(key_list[3], (HEADS,), jnp.float32, -3.0, 1.0), -3.0, 1.0)
    out_gain = jnp.clip(1.0 + 0.18 * jax.random.normal(key_list[4], (D,), jnp.float32), 0.1, 1.9)
    tile_rows = draw_tile_rows(jax.random.fold_in(key_list[9], 71), 0)
    tile_cols = draw_tile_cols(jax.random.fold_in(key_list[9], 71), 0)
    tile_masks = touch_ends(jax.random.randint(key_list[7], (DEVICES, TILES_DEV, TILE * TILE // 8), 0, 256), jax.random.fold_in(key_list[7], 1), 0, 255).astype(jnp.int32)
    tile_count = draw_tile_count(jax.random.fold_in(key_list[9], 71), 0)
    return {"features": features, "w_qkv": w_qkv, "w_out": w_out, "head_bias": head_bias, "out_gain": out_gain, "tile_rows": tile_rows, "tile_cols": tile_cols, "tile_masks": tile_masks, "tile_count": tile_count}


def tile_group(q_tiles, k_tiles, v_tiles, rows_group, cols_group, mask_words, live_slot, head_bias, score_scale):
    group_size = mask_words.shape[0]
    tile_size = TILE
    bit_shift = jnp.arange(8, dtype=jnp.int32)
    words_shaped = mask_words.reshape(group_size, tile_size, tile_size // 8)
    edge_bits = jnp.bitwise_and(jnp.right_shift(words_shaped[..., None], bit_shift), 1)
    edge_mask = edge_bits.reshape(group_size, tile_size, tile_size).astype(jnp.float32)
    edge_mask = edge_mask * live_slot[:, None, None].astype(jnp.float32)
    queries = q_tiles[rows_group].astype(jnp.float32)
    keys = k_tiles[cols_group].astype(jnp.float32)
    values = v_tiles[cols_group].astype(jnp.float32)
    scores = jnp.einsum('gihe,gjhe->ghij', queries, keys, precision=lax.Precision.HIGHEST)
    weights = jax.nn.sigmoid(scores * score_scale + head_bias[None, :, None, None]) * edge_mask[:, None]
    packed = weights.astype(jnp.bfloat16).astype(jnp.float32)
    partial_value = jnp.einsum('ghij,gjhe->gihe', packed, values, precision=lax.Precision.HIGHEST)
    return (partial_value, lax.optimization_barrier(jnp.sum(weights, axis=3)))

def reference(features, w_qkv, w_out, head_bias, out_gain, tile_rows, tile_cols, tile_masks, tile_count):
    node_total = features.shape[0]
    head_size = D // HEADS
    tile_total = node_total // TILE
    projections = jnp.dot(features.astype(jnp.bfloat16), w_qkv, preferred_element_type=jnp.float32).astype(jnp.bfloat16)
    q_tiles = projections[:, :D].reshape(tile_total, TILE, HEADS, head_size)
    k_tiles = projections[:, D:2 * D].reshape(tile_total, TILE, HEADS, head_size)
    v_tiles = projections[:, 2 * D:].reshape(tile_total, TILE, HEADS, head_size)
    group_size = math.gcd(16, TILES_DEV)
    score_scale = 1.0 / math.sqrt(head_size)

    def per_device(totals, device_tiles):
        rows_device, cols_device, words_device, count_device = device_tiles

        def group_step(turn_index, inner):
            numerator, denominator = inner
            first_slot = turn_index * group_size
            rows_group = lax.dynamic_slice_in_dim(rows_device, first_slot, group_size)
            cols_group = lax.dynamic_slice_in_dim(cols_device, first_slot, group_size)
            words_group = lax.dynamic_slice_in_dim(words_device, first_slot, group_size, 0)
            live_slot = first_slot + jnp.arange(group_size, dtype=jnp.int32) < count_device
            partial_value, weight_sums = tile_group(q_tiles, k_tiles, v_tiles, rows_group, cols_group, words_group, live_slot, head_bias, score_scale)
            numerator = numerator.at[rows_group].add(partial_value)
            denominator = denominator.at[:, rows_group].add(jnp.transpose(weight_sums, (1, 0, 2)))
            return (numerator, denominator)
        turns = (count_device + group_size - 1) // group_size
        return (lax.fori_loop(jnp.int32(0), turns.astype(jnp.int32), group_step, totals), None)
    start = (jnp.zeros((tile_total, TILE, HEADS, head_size), jnp.float32), jnp.zeros((HEADS, tile_total, TILE), jnp.float32))
    totals, _ = lax.scan(per_device, start, (tile_rows, tile_cols, tile_masks, tile_count))
    numerator = totals[0].reshape(node_total, HEADS, head_size)
    denominator = 1.0 + totals[1].reshape(HEADS, node_total)
    mixed = (numerator / jnp.transpose(denominator)[:, :, None]).reshape(node_total, D).astype(jnp.bfloat16)
    projected = jnp.dot(mixed, w_out, preferred_element_type=jnp.float32)
    inverse = lax.rsqrt(lax.optimization_barrier(jnp.mean(projected * projected, axis=1, keepdims=True)) + 1e-05)
    return features + out_gain * projected * inverse
```

```python
import functools

import jax
import jax.numpy as jnp
from jax import lax
from jax.experimental import pallas as pl
from jax.experimental.pallas import tpu as pltpu
from jax.sharding import PartitionSpec as P

TILE = 128
HEADS = 4
HEAD = 64
D = 256
STRIP = 16
TABLE = 384
NX, NY, NZ = 4, 4, 8
SITES = NX * NZ
NODES = 384
FIRST = 160
SECOND = NODES - FIRST
BLOCK = NODES // TILE
MESH = pl.DeviceIdType.MESH
NT = (((1,), (1,)), ((), ()))


def position():
    row, col = lax.axis_index("row"), lax.axis_index("col")
    return row // 8, row // 2 % 4, col // 2 * 2 + row % 2, col % 2


def device(z, x, y, core):
    return ((z * NX + x) * 2 + y % 2, y // 2 * 2 + core)


def meet(partners):
    barrier = pltpu.get_barrier_semaphore()
    for partner in partners:
        pl.semaphore_signal(barrier, inc=1, device_id=partner, device_id_type=MESH)
    pl.semaphore_wait(barrier, len(partners))


def site_partners(z, x, y, core):
    found = [device(z, x, y, 1 - core)]
    for d in range(1, NY):
        found += [device(z, x, (y + d) % NY, core), device(z, x, (y + d) % NY, 1 - core)]
    return found


def lane_order():
    node = lax.broadcasted_iota(jnp.int32, (TILE, TILE), 0)
    lane = lax.broadcasted_iota(jnp.int32, (TILE, TILE), 1)
    return node, lane % 16 * 8 + lane // 16


def exchange_kernel(
    features_ref, masks_ref, rows_ref, cols_ref, count_ref, weights_ref,
    gathered, values, stationary, words, table,
    queries, own, own_queries, wq, wv, bits, landed, sorted_slots, diagonal,
    query_send, query_recv, list_send, list_recv,
    ring_send, first_x, first_z, second_z, second_x, sibling_send, sibling_recv,
):
    z, x, y, core = position()
    y_lo, y_hi = y % 2, y // 2
    site = z * NX + x
    own[...] = features_ref[...].astype(jnp.bfloat16)
    meet(
        site_partners(z, x, y, core)
        + [device(z, (x + d) % NX, y, core) for d in (1, 2, 3)]
        + [device((z + d) % NZ, x, y, core) for d in (1, 7)]
    )

    my_list = y_hi * 2 + core
    home = y_lo == core
    partner = device(z, x, y_hi * 2 + core, y_lo)

    def to_partner(src, dst, k):
        return pltpu.make_async_remote_copy(
            src_ref=src, dst_ref=dst, send_sem=list_send.at[k], recv_sem=list_recv.at[k],
            device_id=partner, device_id_type=MESH,
        )

    def hand_over(src, dst, k):
        @pl.when(home)
        def _():
            pltpu.make_async_copy(src, dst, list_recv.at[k]).start()

        @pl.when(jnp.logical_not(home))
        def _():
            to_partner(src, dst, k).start()

    def handed(ref, k):
        pltpu.make_async_copy(ref, ref, list_recv.at[k]).wait()

    def rows(a_site, parity, low, count):
        return pl.ds(pl.multiple_of((a_site * 2 + parity) * NODES + low, 16), count)

    def remote(src, dst, send, recv, target):
        pltpu.make_async_remote_copy(
            src_ref=src, dst_ref=dst, send_sem=send, recv_sem=recv,
            device_id=target, device_id_type=MESH,
        ).start()

    def arrived(a_site, low, count, sem):
        here = gathered.at[rows(a_site, core, low, count)]
        pltpu.make_async_copy(here, here, sem).wait()

    def forward(a_site, low, count, send, recv, target):
        here = gathered.at[rows(a_site, core, low, count)]
        remote(here, here, send, recv, target)

    up, down = device((z + 1) % NZ, x, y, core), device((z + 7) % NZ, x, y, core)
    right, left = device(z, (x + 1) % NX, y, core), device(z, (x + 3) % NX, y, core)
    across = device(z, (x + 2) % NX, y, core)
    other = device(z, x, y, 1 - core)
    z_to, x_to = (up, down), (right, left)

    def share(a_site, low, count):
        forward(a_site, low, count, sibling_send.at[0], sibling_recv.at[0], other)

    def site_of(dz, dx):
        return (z + dz + NZ) % NZ * NX + (x + dx + NX) % NX

    hand_over(own, gathered.at[rows(site, y_lo, 0, NODES)], 0)
    handed(gathered.at[rows(site, core, 0, NODES)], 0)
    for s in range(2):
        forward(site, FIRST, SECOND, ring_send.at[s], second_z.at[s, 0], z_to[s])
        forward(site, 0, FIRST, ring_send.at[2 + s], first_x.at[s], x_to[s])
    forward(site, 0, FIRST, ring_send.at[4], first_x.at[2], across)
    for s in range(2):
        forward(site, FIRST, SECOND, ring_send.at[2 + s], second_x.at[0, s, 0], x_to[s])
        forward(site, 0, FIRST, ring_send.at[s], first_z.at[s, 0, 0], z_to[s])
    share(site, 0, NODES)

    wq[...] = jnp.transpose(weights_ref[:, 0:D])
    wv[...] = jnp.transpose(weights_ref[:, 2 * D : 3 * D])
    node, lane_node = lane_order()
    to_lanes = jnp.where(node == lane_node, 1.0, 0.0).astype(jnp.bfloat16)
    q = lax.dot_general(wq[...], own[...], NT, preferred_element_type=jnp.float32)
    q = q.astype(jnp.bfloat16) * jnp.bfloat16(0.0625)
    for t in range(BLOCK):
        own_queries[t] = jnp.dot(
            q[:, t * TILE : (t + 1) * TILE], to_lanes, preferred_element_type=jnp.float32
        ).astype(jnp.bfloat16)

    def to_queries(d):
        return pltpu.make_async_remote_copy(
            src_ref=own_queries, dst_ref=queries.at[my_list],
            send_sem=query_send.at[d], recv_sem=query_recv.at[my_list],
            device_id=device(z, x, (y_hi * 2 + core + d) % NY, y_lo), device_id_type=MESH,
        )

    @pl.when(home)
    def _():
        pltpu.make_async_copy(own_queries, queries.at[my_list], query_recv.at[my_list]).start()

    @pl.when(jnp.logical_not(home))
    def _():
        to_queries(0).start()

    for d in (1, 2, 3):
        to_queries(d).start()
    bits[...] = masks_ref[...].astype(jnp.float32).astype(jnp.bfloat16)
    hand_over(bits, landed, 1)
    diagonal[...] = jnp.zeros_like(diagonal)

    def fold(c):
        pltpu.make_async_copy(queries.at[c], queries.at[c], query_recv.at[c]).wait()
        for t in range(BLOCK):
            for h in range(HEADS):
                diagonal[h * HEAD : (h + 1) * HEAD, h * TILE : (h + 1) * TILE] = (
                    queries[c, t, h * HEAD : (h + 1) * HEAD, :]
                )
            stationary[c * BLOCK + t] = jnp.dot(
                weights_ref[:, D : 2 * D], diagonal[...], preferred_element_type=jnp.float32
            ).astype(jnp.bfloat16)

    def spread(c):
        words[c] = landed[:, c * TILE : (c + 1) * TILE].astype(jnp.float32).astype(jnp.int32)

    def swap_bit(b):
        step = 1 << b
        slots = words.shape[1]
        upper = (lax.broadcasted_iota(jnp.int32, (slots, TILE), 1) // step) % 2 == 1
        for c in range(words.shape[0]):
            if c & step == 0:
                low, high = words[c], words[c + step]
                words[c] = jnp.where(upper, pltpu.roll(high, step, 1), low)
                words[c + step] = jnp.where(upper, high, pltpu.roll(low, TILE - step, 1))

    def start_words():
        handed(landed, 1)
        for c in range(words.shape[0]):
            spread(c)

    def sort_slots():
        slots = rows_ref.shape[1]
        row_tiles = NY * BLOCK
        to, source = rows_ref[...].astype(jnp.float32), cols_ref[...].astype(jnp.float32)
        count = jnp.full((1, slots), count_ref[0], jnp.int32).astype(jnp.float32)
        slot = lax.broadcasted_iota(jnp.int32, (1, slots), 1).astype(jnp.float32)
        a = to - row_tiles * jnp.floor((to + 0.5) * (1.0 / row_tiles))
        b = BLOCK * jnp.floor((source + 0.5) * (1.0 / row_tiles)) + (
            source - BLOCK * jnp.floor((source + 0.5) * (1.0 / BLOCK))
        )
        a = jnp.where(slot < count, a, float(row_tiles))
        base = jnp.zeros_like(a)
        total = jnp.zeros((1, 1), jnp.float32)
        for tile in range(row_tiles):
            number = jnp.sum(jnp.where(a == tile, 1.0, 0.0), axis=1, keepdims=True)
            number = 2.0 * jnp.floor((number + 1.5) * 0.5)
            base += jnp.where(a > tile, number, 0.0)
            total += number
        across_lanes = jnp.broadcast_to(a, (slots, slots))
        down = jnp.transpose(across_lanes)
        earlier = lax.broadcasted_iota(jnp.int32, (slots, slots), 0) < lax.broadcasted_iota(
            jnp.int32, (slots, slots), 1
        )
        rank = jnp.sum(
            jnp.where((across_lanes == down) & earlier, 1.0, 0.0), axis=0, keepdims=True
        )
        at = jnp.where(a < row_tiles, base + rank, float(TABLE))
        at_down = jnp.transpose(jnp.broadcast_to(at, (TABLE, slots)))
        hit = at_down == lax.broadcasted_iota(jnp.int32, (slots, TABLE), 1).astype(jnp.float32)

        def pick(value):
            down = jnp.transpose(jnp.broadcast_to(value, (TABLE, slots)))
            return jnp.sum(jnp.where(hit, down, 0.0), axis=0, keepdims=True)

        sorted_slots[0:1, :] = (pick(slot + 1.0) - 1.0).astype(jnp.int32)
        sorted_slots[1:2, :] = pick(a).astype(jnp.int32)
        sorted_slots[2:3, :] = pick(b).astype(jnp.int32)
        sorted_slots[3:4, :] = jnp.broadcast_to(total * 0.5, (1, TABLE)).astype(jnp.int32)
        sorted_slots[4:8, :] = jnp.zeros((4, TABLE), jnp.int32)
        hand_over(sorted_slots, table, 2)

    X_OFF = (0, -1, 1, 2)
    Z_OFF = (0, -1, 1, -2, 2, -3, 3, 4)
    HALF1, HALF2 = FIRST // 2, SECOND // 2

    def second_z_step(t):
        for s in range(2):
            sign = -1 if s == 0 else 1
            if t < 4:
                a = site_of(sign * t, 0)
                arrived(a, FIRST, SECOND, second_z.at[s, t - 1])
                if t < 3:
                    forward(a, FIRST, SECOND, ring_send.at[s], second_z.at[s, t], z_to[s])
                else:
                    forward(a, FIRST + s * HALF2, HALF2, ring_send.at[s], second_z.at[s, 3], z_to[s])
                k = Z_OFF.index(sign * t)
                for e in range(2):
                    forward(a, FIRST, SECOND, ring_send.at[2 + e], second_x.at[k, e, 0], x_to[e])
                share(a, FIRST, SECOND)
        if t == 4:
            a = site_of(4, 0)
            for s in range(2):
                arrived(a, FIRST + s * HALF2, HALF2, second_z.at[s, 3])
            for e in range(2):
                forward(a, FIRST, SECOND, ring_send.at[2 + e], second_x.at[7, e, 0], x_to[e])
            share(a, FIRST, SECOND)

    def first_x_step():
        for k in range(3):
            a = site_of(0, X_OFF[k + 1])
            arrived(a, 0, FIRST, first_x.at[k])
            for s in range(2):
                forward(a, 0, FIRST, ring_send.at[s], first_z.at[s, 0, k + 1], z_to[s])
            share(a, 0, FIRST)

    def first_z_step(t, k):
        if t < 4:
            for s in range(2):
                sign = -1 if s == 0 else 1
                a = site_of(sign * t, X_OFF[k])
                arrived(a, 0, FIRST, first_z.at[s, t - 1, k])
                if t < 3:
                    forward(a, 0, FIRST, ring_send.at[s], first_z.at[s, t, k], z_to[s])
                else:
                    forward(a, s * HALF1, HALF1, ring_send.at[s], first_z.at[s, 3, k], z_to[s])
                share(a, 0, FIRST)
        else:
            a = site_of(4, X_OFF[k])
            for s in range(2):
                arrived(a, s * HALF1, HALF1, first_z.at[s, 3, k])
            share(a, 0, FIRST)

    def second_x_step(k):
        for e in range(2):
            sign = -1 if e == 0 else 1
            a = site_of(Z_OFF[k], sign)
            arrived(a, FIRST, SECOND, second_x.at[k, e, 0])
            forward(a, FIRST + e * HALF2, HALF2, ring_send.at[2 + e], second_x.at[k, e, 1], x_to[e])
            share(a, FIRST, SECOND)

    def second_x_end(k):
        a = site_of(Z_OFF[k], 2)
        for e in range(2):
            arrived(a, FIRST + e * HALF2, HALF2, second_x.at[k, e, 1])
        share(a, FIRST, SECOND)

    def project(depth, m):
        a = site_of(jnp.where(m < NX, depth, -depth), m % NX)
        start = pl.multiple_of((a * 2 + core) * NODES, NODES)
        tile = (a * 2 + core) * BLOCK
        v = lax.dot_general(
            wv[...], gathered[pl.ds(start, NODES), :], NT, preferred_element_type=jnp.float32
        ).astype(jnp.bfloat16)
        for t in range(BLOCK):
            values[tile + t] = v[:, t * TILE : (t + 1) * TILE]
        done = values.at[pl.ds(tile, BLOCK)]
        remote(done, done, sibling_send.at[1], sibling_recv.at[1], other)

    def drain(count, sem):
        pltpu.make_async_copy(gathered.at[pl.ds(0, count)], gathered.at[pl.ds(0, count)], sem).wait()

    def project_round(r):
        lax.fori_loop(0, NX if r in (0, 4) else 2 * NX, lambda m, _: (project(r, m), 0)[1], 0)

    sort_slots()
    second_z_step(1)
    first_x_step()
    second_z_step(2)
    second_x_step(0)
    fold(0)
    fold(1)
    second_z_step(3)
    fold(2)
    second_x_end(0)
    project_round(0)
    for r in range(1, 4):
        for k in range(NX):
            first_z_step(r, k)
        if r == 1:
            second_z_step(4)
        second_x_step(2 * r - 1)
        second_x_step(2 * r)
        second_x_end(2 * r - 1)
        second_x_end(2 * r)
        project_round(r)
        if r == 1:
            fold(3)
            start_words()
        elif r == 2:
            swap_bit(0)
            swap_bit(1)
        else:
            swap_bit(2)
            swap_bit(3)
    second_x_step(7)
    for k in range(NX):
        first_z_step(4, k)
    second_x_end(7)
    project_round(4)

    half_values = values.at[pl.ds(0, SITES * BLOCK)]
    pltpu.make_async_copy(half_values, half_values, sibling_recv.at[1]).wait()
    pltpu.make_async_copy(half_values, half_values, sibling_send.at[1]).wait()
    drain(SITES * NODES, sibling_recv.at[0])
    drain(SITES * NODES, sibling_send.at[0])
    z_rows = 3 * SECOND + HALF2 + NX * (3 * FIRST + HALF1)
    x_rows = FIRST + NZ * (SECOND + HALF2)
    for s in range(2):
        drain(z_rows, ring_send.at[s])
        drain(x_rows, ring_send.at[2 + s])
    drain(FIRST, ring_send.at[4])
    for d in range(1, NY):
        to_queries(d).wait_send()
    handed(table, 2)

    @pl.when(jnp.logical_not(home))
    def _():
        to_queries(0).wait_send()
        to_partner(own, gathered.at[rows(site, y_lo, 0, NODES)], 0).wait_send()
        to_partner(bits, landed, 1).wait_send()
        to_partner(sorted_slots, table, 2).wait_send()


def exchange(features, masks, tile_rows, tile_cols, tile_count, weights):
    slots, length = masks.shape
    vmem = pl.BlockSpec(memory_space=pltpu.VMEM)
    smem = pl.BlockSpec(memory_space=pltpu.SMEM)
    dma = pltpu.SemaphoreType.DMA
    half = jnp.bfloat16
    return pl.pallas_call(
        exchange_kernel,
        out_shape=(
            jax.ShapeDtypeStruct((SITES * 2 * NODES, D), half),
            jax.ShapeDtypeStruct((SITES * 2 * BLOCK, D, TILE), half),
            jax.ShapeDtypeStruct((NY * BLOCK, D, HEADS * TILE), half),
            jax.ShapeDtypeStruct((length // TILE, slots, TILE), jnp.int32),
            jax.ShapeDtypeStruct((8, TABLE), jnp.int32),
        ),
        in_specs=[vmem, vmem, vmem, vmem, smem, vmem],
        out_specs=(vmem,) * 5,
        scratch_shapes=[
            pltpu.VMEM((NY, BLOCK, D, TILE), half),
            pltpu.VMEM((NODES, D), half),
            pltpu.VMEM((BLOCK, D, TILE), half),
            pltpu.VMEM((D, D), half),
            pltpu.VMEM((D, D), half),
            pltpu.VMEM((slots, length), half),
            pltpu.VMEM((slots, length), half),
            pltpu.VMEM((8, TABLE), jnp.int32),
            pltpu.VMEM((D, HEADS * TILE), half),
            dma((NY,)), dma((NY,)), dma((3,)), dma((3,)),
            dma((5,)), dma((3,)), dma((2, 4, NX)), dma((2, 4)), dma((NZ, 2, 2)), dma((2,)), dma((2,)),
        ],
        compiler_params=pltpu.CompilerParams(
            collective_id=0, has_side_effects=True, vmem_limit_bytes=16 * 1024 * 1024
        ),
        name="exchange",
    )(features, masks, tile_rows, tile_cols, tile_count, weights)


def attention_kernel(
    table_ref, bias_ref, gathered, values, stationary, words,
    num_ref, den_ref, num_acc, den_acc, even_scores, odd_scores, even_weights, odd_weights,
):
    pairs = table_ref[3, 0]
    num_acc[...] = jnp.zeros_like(num_acc)
    den_acc[...] = jnp.zeros_like(den_acc)
    odd_weights[...] = jnp.zeros_like(odd_weights)
    bit_of = jnp.left_shift(jnp.int32(1), lax.broadcasted_iota(jnp.int32, (8, TILE), 0))
    half_bias = [bias_ref[h] * 0.5 for h in range(HEADS)]

    def score(p, scores):
        a = table_ref[1, 2 * p]
        sources = jnp.concatenate(
            [
                gathered[pl.ds(pl.multiple_of(table_ref[2, 2 * p + u] * TILE, TILE), TILE), :]
                for u in range(2)
            ],
            axis=0,
        )

        def part(half):
            lanes = slice(half * 2 * TILE, (half + 1) * 2 * TILE)
            scores[:, lanes] = jnp.dot(
                sources, stationary[a, :, lanes], preferred_element_type=jnp.float32
            )

        return [functools.partial(part, half) for half in range(2)]

    def weigh(p, scores, weights):
        a = table_ref[1, 2 * p]
        total = [jnp.zeros((8, TILE), jnp.float32) for _ in range(HEADS)]

        def part(u, groups):
            s = table_ref[0, 2 * p + u]
            live = jnp.where(s >= 0, bit_of, 0)
            s = jnp.maximum(s, 0)
            for g in groups:
                edge = [
                    (jnp.broadcast_to(words[w, pl.ds(s, 1), :], (8, TILE)) & live) != 0
                    for w in (2 * g, 2 * g + 1)
                ]
                here = slice(u * TILE + g * STRIP, u * TILE + (g + 1) * STRIP)
                for h in range(HEADS):
                    lanes = slice(h * TILE, (h + 1) * TILE)
                    twice = jnp.tanh(scores[here, lanes] + half_bias[h]) + 1.0
                    low = jnp.where(edge[0], twice[0:8], 0.0)
                    high = jnp.where(edge[1], twice[8:16], 0.0)
                    total[h] += low + high
                    weights[here, lanes] = jnp.concatenate([low, high], axis=0).astype(jnp.bfloat16)

        def finish():
            for h in range(HEADS):
                den_acc[a, h] += total[h]

        half = TILE // STRIP // 2
        return [
            functools.partial(part, u, range(v * half, (v + 1) * half))
            for u in range(2) for v in range(2)
        ] + [finish]

    def mix(p, weights):
        a = table_ref[1, 2 * p]
        source = [table_ref[2, 2 * p + u] for u in range(2)]

        def part(half):
            rows = slice(half * TILE, (half + 1) * TILE)
            v = jnp.concatenate([values[b, rows, :] for b in source], axis=1)
            both = jnp.dot(
                v, weights[:, half * 2 * TILE : (half + 1) * 2 * TILE],
                preferred_element_type=jnp.float32,
            )
            for side in range(2):
                start = half * TILE + side * HEAD
                num_acc[a, start : start + HEAD, :] += both[
                    side * HEAD : (side + 1) * HEAD, side * TILE : (side + 1) * TILE
                ]

        return [functools.partial(part, half) for half in range(2)]

    def together(scored, mixed, weighed):
        for k in range(2):
            scored[k]()
            weighed[2 * k]()
            mixed[k]()
            weighed[2 * k + 1]()
        weighed[4]()

    for part in score(0, even_scores):
        part()

    def turn(t, _):
        p = 2 * t
        together(
            score(p + 1, odd_scores), mix(jnp.maximum(p - 1, 0), odd_weights),
            weigh(p, even_scores, even_weights),
        )
        together(
            score(p + 2, even_scores), mix(p, even_weights),
            weigh(p + 1, odd_scores, odd_weights),
        )
        return 0

    turns = (pairs + 1) // 2
    lax.fori_loop(0, turns, turn, 0)
    for part in mix(jnp.maximum(2 * turns - 1, 0), odd_weights):
        part()
    num_ref[...] = (num_acc[...] * 0.5).astype(num_ref.dtype)
    den_ref[...] = jnp.sum(den_acc[...], axis=2) * 0.5


def attention(table, bias, gathered, values, stationary, words):
    row_tiles = stationary.shape[0]
    smem = pl.BlockSpec(memory_space=pltpu.SMEM)
    vmem = pl.BlockSpec(memory_space=pltpu.VMEM)
    return pl.pallas_call(
        attention_kernel,
        out_shape=(
            jax.ShapeDtypeStruct((row_tiles, D, TILE), jnp.bfloat16),
            jax.ShapeDtypeStruct((row_tiles, HEADS, TILE), jnp.float32),
        ),
        in_specs=[smem] * 2 + [vmem] * 4,
        out_specs=(vmem, vmem),
        scratch_shapes=[
            pltpu.VMEM((row_tiles, D, TILE), jnp.float32),
            pltpu.VMEM((row_tiles, HEADS, 8, TILE), jnp.float32),
            pltpu.VMEM((2 * TILE, HEADS * TILE), jnp.float32),
            pltpu.VMEM((2 * TILE, HEADS * TILE), jnp.float32),
            pltpu.VMEM((2 * TILE, HEADS * TILE), jnp.bfloat16),
            pltpu.VMEM((2 * TILE, HEADS * TILE), jnp.bfloat16),
        ],
        compiler_params=pltpu.CompilerParams(vmem_limit_bytes=16 * 1024 * 1024),
        name="attention",
    )(table, bias, gathered, values, stationary, words)


def finish_kernel(
    features_ref, num_ref, den_ref, w_ref, gain_ref, out_ref,
    nums, dens, send, recv,
):
    z, x, y, core = position()
    y_lo = y % 2
    meet(site_partners(z, x, y, core))
    home = y_lo == core

    def part(d, src, dst, k):
        c = (y + d) % NY
        return pltpu.make_async_remote_copy(
            src_ref=src.at[c], dst_ref=dst.at[y], send_sem=send.at[k, d], recv_sem=recv.at[k, y],
            device_id=device(z, x, c // 2 * 2 + core, c % 2), device_id_type=MESH,
        )

    pairs = ((num_ref, nums), (den_ref, dens))
    for d in (1, 2, 3):
        for k, (src, dst) in enumerate(pairs):
            part(d, src, dst, k).start()
    for k, (src, dst) in enumerate(pairs):
        @pl.when(home)
        def _():
            pltpu.make_async_copy(src.at[y], dst.at[y], recv.at[k, y]).start()

        @pl.when(jnp.logical_not(home))
        def _():
            part(0, src, dst, k).start()

    for c in range(NY):
        for k, (src, dst) in enumerate(pairs):
            pltpu.make_async_copy(dst.at[c], dst.at[c], recv.at[k, c]).wait()
    total = sum(nums[c].astype(jnp.float32) for c in range(NY))
    weight = 1.0 + sum(dens[c] for c in range(NY))
    gain = gain_ref[...]
    node, lane_node = lane_order()
    to_nodes = jnp.transpose(jnp.where(node == lane_node, 1.0, 0.0)).astype(jnp.bfloat16)
    for t in range(NODES // TILE):
        mixed = total[t].reshape(HEADS, HEAD, TILE) / weight[t].reshape(HEADS, 1, TILE)
        mixed = mixed.reshape(D, TILE).astype(jnp.bfloat16)
        mixed = jnp.dot(mixed, to_nodes, preferred_element_type=jnp.float32).astype(jnp.bfloat16)
        projected = lax.dot_general(
            mixed, w_ref[...], (((0,), (0,)), ((), ())), preferred_element_type=jnp.float32
        )
        square = jnp.mean(projected * projected, axis=1, keepdims=True)
        here = pl.ds(t * TILE, TILE)
        out_ref[here, :] = features_ref[here, :] + gain * projected * lax.rsqrt(square + 1e-05)
    for d in range(NY):
        for k, (src, dst) in enumerate(pairs):
            if d:
                part(d, src, dst, k).wait_send()
            else:
                @pl.when(jnp.logical_not(home))
                def _():
                    part(d, src, dst, k).wait_send()


def finish(features, numerator, denominator, w_out, gain):
    vmem = pl.BlockSpec(memory_space=pltpu.VMEM)
    hbm = pl.BlockSpec(memory_space=pl.ANY)
    dma = pltpu.SemaphoreType.DMA
    return pl.pallas_call(
        finish_kernel,
        out_shape=jax.ShapeDtypeStruct(features.shape, jnp.float32),
        in_specs=[vmem, hbm, hbm, vmem, vmem],
        out_specs=vmem,
        scratch_shapes=[
            pltpu.VMEM(numerator.shape, numerator.dtype),
            pltpu.VMEM(denominator.shape, denominator.dtype),
            dma((2, NY)), dma((2, NY)),
        ],
        compiler_params=pltpu.CompilerParams(
            collective_id=1, has_side_effects=True, vmem_limit_bytes=32 * 1024 * 1024
        ),
        name="finish",
    )(features, numerator, denominator, w_out, gain)


def local(
    features, w_qkv, w_out, head_bias, out_gain, tile_rows, tile_cols, tile_masks, tile_count
):
    block_tiles = features.shape[0] // TILE
    gathered, values, stationary, words, table = exchange(
        features, tile_masks[0], tile_rows, tile_cols, tile_count, w_qkv
    )
    numerator, denominator = attention(
        table, head_bias, gathered, values, stationary, words
    )
    return finish(
        features,
        numerator.reshape(NY, block_tiles, D, TILE),
        denominator.reshape(NY, block_tiles, HEADS, TILE),
        w_out, out_gain[None, :],
    )


def solution(mesh):
    placed = (
        P(("row", "col"), None),
        P(),
        P(),
        P(),
        P(),
        P(("row", "col"), None),
        P(("row", "col"), None),
        P(("row", "col"), None, None),
        P(("row", "col")),
    )
    return jax.shard_map(
        local, mesh=mesh, in_specs=placed, out_specs=P(("row", "col"), None), check_vma=False
    )
```

```python
import functools

import jax
import jax.numpy as jnp
from jax import lax
from jax.experimental import pallas as pl
from jax.experimental.pallas import tpu as pltpu
from jax.sharding import PartitionSpec as P

TILE = 128
HEADS = 4
HEAD = 64
D = 256
STRIP = 16
TABLE = 384
NX, NY, NZ = 4, 4, 8
SITES = NX * NZ
NODES = 384
FIRST = 160
SECOND = NODES - FIRST
BLOCK = NODES // TILE
MESH = pl.DeviceIdType.MESH
NT = (((1,), (1,)), ((), ()))


def position():
    row, col = lax.axis_index("row"), lax.axis_index("col")
    return row // 8, row // 2 % 4, col // 2 * 2 + row % 2, col % 2


def device(z, x, y, core):
    return ((z * NX + x) * 2 + y % 2, y // 2 * 2 + core)


def meet(partners, meanwhile=None):
    barrier = pltpu.get_barrier_semaphore()
    for partner in partners:
        pl.semaphore_signal(barrier, inc=1, device_id=partner, device_id_type=MESH)
    if meanwhile is not None:
        meanwhile()
    pl.semaphore_wait(barrier, len(partners))


def site_partners(z, x, y, core):
    found = [device(z, x, y, 1 - core)]
    for d in range(1, NY):
        found += [device(z, x, (y + d) % NY, core), device(z, x, (y + d) % NY, 1 - core)]
    return found


def lane_order():
    node = lax.broadcasted_iota(jnp.int32, (TILE, TILE), 0)
    lane = lax.broadcasted_iota(jnp.int32, (TILE, TILE), 1)
    return node, lane % 16 * 8 + lane // 16


def exchange_kernel(
    features_ref, masks_ref, rows_ref, cols_ref, count_ref, weights_ref,
    gathered, values, stationary, words, table,
    queries, own, own_queries, wq, wv, bits, landed, sorted_slots, diagonal,
    query_send, query_recv, list_send, list_recv,
    ring_send, first_x, first_z, second_z, second_x, sibling_send, sibling_recv,
):
    z, x, y, core = position()
    y_lo, y_hi = y % 2, y // 2
    site = z * NX + x

    def setup():
        own[...] = features_ref[...].astype(jnp.bfloat16)
        wq[...] = jnp.transpose(weights_ref[:, 0:D])
        wv[...] = jnp.transpose(weights_ref[:, 2 * D : 3 * D])
        bits[...] = masks_ref[...].astype(jnp.float32).astype(jnp.bfloat16)
        diagonal[...] = jnp.zeros_like(diagonal)

    meet(
        site_partners(z, x, y, core)
        + [device(z, (x + d) % NX, y, core) for d in (1, 2, 3)]
        + [device((z + d) % NZ, x, y, core) for d in (1, 7)],
        setup,
    )

    my_list = y_hi * 2 + core
    home = y_lo == core
    partner = device(z, x, y_hi * 2 + core, y_lo)

    def to_partner(src, dst, k):
        return pltpu.make_async_remote_copy(
            src_ref=src, dst_ref=dst, send_sem=list_send.at[k], recv_sem=list_recv.at[k],
            device_id=partner, device_id_type=MESH,
        )

    def hand_over(src, dst, k):
        @pl.when(home)
        def _():
            pltpu.make_async_copy(src, dst, list_recv.at[k]).start()

        @pl.when(jnp.logical_not(home))
        def _():
            to_partner(src, dst, k).start()

    def handed(ref, k):
        pltpu.make_async_copy(ref, ref, list_recv.at[k]).wait()

    def rows(a_site, parity, low, count):
        return pl.ds(pl.multiple_of((a_site * 2 + parity) * NODES + low, 16), count)

    def remote(src, dst, send, recv, target):
        pltpu.make_async_remote_copy(
            src_ref=src, dst_ref=dst, send_sem=send, recv_sem=recv,
            device_id=target, device_id_type=MESH,
        ).start()

    def arrived(a_site, low, count, sem):
        here = gathered.at[rows(a_site, core, low, count)]
        pltpu.make_async_copy(here, here, sem).wait()

    def forward(a_site, low, count, send, recv, target):
        here = gathered.at[rows(a_site, core, low, count)]
        remote(here, here, send, recv, target)

    up, down = device((z + 1) % NZ, x, y, core), device((z + 7) % NZ, x, y, core)
    right, left = device(z, (x + 1) % NX, y, core), device(z, (x + 3) % NX, y, core)
    across = device(z, (x + 2) % NX, y, core)
    other = device(z, x, y, 1 - core)
    z_to, x_to = (up, down), (right, left)

    def site_of(dz, dx):
        return (z + dz + NZ) % NZ * NX + (x + dx + NX) % NX

    def to_queries(d):
        return pltpu.make_async_remote_copy(
            src_ref=own_queries, dst_ref=queries.at[my_list],
            send_sem=query_send.at[d], recv_sem=query_recv.at[my_list],
            device_id=device(z, x, (y_hi * 2 + core + d) % NY, y_lo), device_id_type=MESH,
        )

    def prepare():
        node, lane_node = lane_order()
        to_lanes = jnp.where(node == lane_node, 1.0, 0.0).astype(jnp.bfloat16)
        q = lax.dot_general(wq[...], own[...], NT, preferred_element_type=jnp.float32)
        q = q.astype(jnp.bfloat16) * jnp.bfloat16(0.0625)
        for t in range(BLOCK):
            own_queries[t] = jnp.dot(
                q[:, t * TILE : (t + 1) * TILE], to_lanes, preferred_element_type=jnp.float32
            ).astype(jnp.bfloat16)
        sort_slots()

    def fold(c, t):
        if t == 0:
            pltpu.make_async_copy(queries.at[c], queries.at[c], query_recv.at[c]).wait()
        for h in range(HEADS):
            diagonal[h * HEAD : (h + 1) * HEAD, h * TILE : (h + 1) * TILE] = (
                queries[c, t, h * HEAD : (h + 1) * HEAD, :]
            )
        stationary[c * BLOCK + t] = jnp.dot(
            weights_ref[:, D : 2 * D], diagonal[...], preferred_element_type=jnp.float32
        ).astype(jnp.bfloat16)

    def spread(c):
        words[c] = landed[:, c * TILE : (c + 1) * TILE].astype(jnp.float32).astype(jnp.int32)

    def swap_bit(b):
        step = 1 << b
        slots = words.shape[1]
        upper = (lax.broadcasted_iota(jnp.int32, (slots, TILE), 1) // step) % 2 == 1
        for c in range(words.shape[0]):
            if c & step == 0:
                low, high = words[c], words[c + step]
                words[c] = jnp.where(upper, pltpu.roll(high, step, 1), low)
                words[c + step] = jnp.where(upper, high, pltpu.roll(low, TILE - step, 1))

    def start_words():
        handed(landed, 1)
        for c in range(words.shape[0]):
            spread(c)

    def sort_slots():
        slots = rows_ref.shape[1]
        row_tiles = NY * BLOCK
        to, source = rows_ref[...].astype(jnp.float32), cols_ref[...].astype(jnp.float32)
        count = jnp.full((1, slots), count_ref[0], jnp.int32).astype(jnp.float32)
        slot = lax.broadcasted_iota(jnp.int32, (1, slots), 1).astype(jnp.float32)
        a = to - row_tiles * jnp.floor((to + 0.5) * (1.0 / row_tiles))
        b = BLOCK * jnp.floor((source + 0.5) * (1.0 / row_tiles)) + (
            source - BLOCK * jnp.floor((source + 0.5) * (1.0 / BLOCK))
        )
        a = jnp.where(slot < count, a, float(row_tiles))
        base = jnp.zeros_like(a)
        total = jnp.zeros((1, 1), jnp.float32)
        for tile in range(row_tiles):
            number = jnp.sum(jnp.where(a == tile, 1.0, 0.0), axis=1, keepdims=True)
            number = 2.0 * jnp.floor((number + 1.5) * 0.5)
            base += jnp.where(a > tile, number, 0.0)
            total += number
        across_lanes = jnp.broadcast_to(a, (slots, slots))
        down = jnp.transpose(across_lanes)
        earlier = lax.broadcasted_iota(jnp.int32, (slots, slots), 0) < lax.broadcasted_iota(
            jnp.int32, (slots, slots), 1
        )
        rank = jnp.sum(
            jnp.where((across_lanes == down) & earlier, 1.0, 0.0), axis=0, keepdims=True
        )
        at = jnp.where(a < row_tiles, base + rank, float(TABLE))
        at_down = jnp.transpose(jnp.broadcast_to(at, (TABLE, slots)))
        hit = at_down == lax.broadcasted_iota(jnp.int32, (slots, TABLE), 1).astype(jnp.float32)

        def pick(value):
            down = jnp.transpose(jnp.broadcast_to(value, (TABLE, slots)))
            return jnp.sum(jnp.where(hit, down, 0.0), axis=0, keepdims=True)

        sorted_slots[0:1, :] = (pick(slot + 1.0) - 1.0).astype(jnp.int32)
        sorted_slots[1:2, :] = pick(a).astype(jnp.int32)
        sorted_slots[2:3, :] = pick(b).astype(jnp.int32)
        sorted_slots[3:4, :] = jnp.broadcast_to(total * 0.5, (1, TABLE)).astype(jnp.int32)
        sorted_slots[4:8, :] = jnp.zeros((4, TABLE), jnp.int32)

    hand_over(own, gathered.at[rows(site, y_lo, 0, NODES)], 0)

    @pl.when(jnp.logical_not(home))
    def _():
        prepare()

    handed(gathered.at[rows(site, core, 0, NODES)], 0)
    for s in range(2):
        forward(site, FIRST, SECOND, ring_send.at[s], second_z.at[s, 0], z_to[s])
        forward(site, 0, FIRST, ring_send.at[2 + s], first_x.at[s], x_to[s])
    forward(site, 0, FIRST, ring_send.at[4], first_x.at[2], across)
    for s in range(2):
        forward(site, FIRST, SECOND, ring_send.at[2 + s], second_x.at[0, s, 0], x_to[s])
        forward(site, 0, FIRST, ring_send.at[s], first_z.at[s, 0, 0], z_to[s])

    @pl.when(home)
    def _():
        prepare()
        pltpu.make_async_copy(own_queries, queries.at[my_list], query_recv.at[my_list]).start()

    @pl.when(jnp.logical_not(home))
    def _():
        to_queries(0).start()

    for d in (1, 2, 3):
        to_queries(d).start()
    hand_over(bits, landed, 1)
    hand_over(sorted_slots, table, 2)

    X_OFF = (0, -1, 1, 2)
    Z_OFF = (0, -1, 1, -2, 2, -3, 3, 4)
    HALF1, HALF2 = FIRST // 2, SECOND // 2

    def second_z_step(t):
        for s in range(2):
            sign = -1 if s == 0 else 1
            if t < 4:
                a = site_of(sign * t, 0)
                arrived(a, FIRST, SECOND, second_z.at[s, t - 1])
                if t < 3:
                    forward(a, FIRST, SECOND, ring_send.at[s], second_z.at[s, t], z_to[s])
                else:
                    forward(a, FIRST + s * HALF2, HALF2, ring_send.at[s], second_z.at[s, 3], z_to[s])
                k = Z_OFF.index(sign * t)
                for e in range(2):
                    forward(a, FIRST, SECOND, ring_send.at[2 + e], second_x.at[k, e, 0], x_to[e])
        if t == 4:
            a = site_of(4, 0)
            for s in range(2):
                arrived(a, FIRST + s * HALF2, HALF2, second_z.at[s, 3])
            for e in range(2):
                forward(a, FIRST, SECOND, ring_send.at[2 + e], second_x.at[7, e, 0], x_to[e])

    def first_x_step():
        for k in range(3):
            a = site_of(0, X_OFF[k + 1])
            arrived(a, 0, FIRST, first_x.at[k])
            for s in range(2):
                forward(a, 0, FIRST, ring_send.at[s], first_z.at[s, 0, k + 1], z_to[s])

    def first_z_step(t, k):
        if t < 4:
            for s in range(2):
                sign = -1 if s == 0 else 1
                a = site_of(sign * t, X_OFF[k])
                arrived(a, 0, FIRST, first_z.at[s, t - 1, k])
                if t < 3:
                    forward(a, 0, FIRST, ring_send.at[s], first_z.at[s, t, k], z_to[s])
                else:
                    forward(a, s * HALF1, HALF1, ring_send.at[s], first_z.at[s, 3, k], z_to[s])
        else:
            a = site_of(4, X_OFF[k])
            for s in range(2):
                arrived(a, s * HALF1, HALF1, first_z.at[s, 3, k])

    def second_x_step(k):
        for e in range(2):
            sign = -1 if e == 0 else 1
            a = site_of(Z_OFF[k], sign)
            arrived(a, FIRST, SECOND, second_x.at[k, e, 0])
            forward(a, FIRST + e * HALF2, HALF2, ring_send.at[2 + e], second_x.at[k, e, 1], x_to[e])

    def second_x_end(k):
        a = site_of(Z_OFF[k], 2)
        for e in range(2):
            arrived(a, FIRST + e * HALF2, HALF2, second_x.at[k, e, 1])

    plan = [
        [
            [(second_z_step, 1)], [(first_x_step,)], [(second_z_step, 2)], [(second_x_step, 0)],
            [(second_z_step, 3)], [(second_x_end, 0)],
        ],
        [
            [(first_z_step, 1, 0), (second_x_step, 1)],
            [(first_z_step, 1, 1), (second_z_step, 4), (second_x_step, 2)],
            [(first_z_step, 1, 2), (second_x_end, 1)],
            [(first_z_step, 1, 3), (second_x_end, 2)],
        ],
    ]
    for t in (2, 3):
        k = 2 * t - 1
        plan.append([
            [(first_z_step, t, 0)], [(second_x_step, k)], [(first_z_step, t, 1)],
            [(second_x_step, k + 1)], [(first_z_step, t, 2)], [(second_x_end, k)],
            [(first_z_step, t, 3)], [(second_x_end, k + 1)],
        ])
    plan.append([
        [(first_z_step, 4, 0)], [(second_x_step, 7)], [(first_z_step, 4, 1)], [],
        [(first_z_step, 4, 2)], [(second_x_end, 7)], [(first_z_step, 4, 3)], [],
    ])

    folds = [(fold, c, t) for c in range(NY) for t in range(BLOCK)]
    for n, extra in enumerate(folds):
        plan[2 + n // 8][n % 8].append(extra)
    for at, extra in (
        ((3, 4), (start_words,)), ((3, 6), (swap_bit, 0)), ((4, 0), (swap_bit, 1)),
        ((4, 2), (swap_bit, 2)), ((4, 4), (swap_bit, 3)),
    ):
        plan[at[0]][at[1]].append(extra)

    def project(depth, m):
        a = site_of(jnp.where(m < NX, depth, -depth), m % NX)
        start = pl.multiple_of((a * 2 + core) * NODES, NODES)
        tile = (a * 2 + core) * BLOCK
        forward(a, 0, NODES, sibling_send.at[0], sibling_recv.at[0], other)
        v = lax.dot_general(
            wv[...], gathered[pl.ds(start, NODES), :], NT, preferred_element_type=jnp.float32
        ).astype(jnp.bfloat16)
        for t in range(BLOCK):
            values[tile + t] = v[:, t * TILE : (t + 1) * TILE]
        done = values.at[pl.ds(tile, BLOCK)]
        remote(done, done, sibling_send.at[1], sibling_recv.at[1], other)

    def turn(r, i):
        for j, todo in enumerate(plan[r] if r < len(plan) else []):
            if todo:
                @pl.when(i == j)
                def _():
                    for step in todo:
                        step[0](*step[1:])

        if r:
            project(r - 1, i)
        return 0

    def drain(count, sem):
        pltpu.make_async_copy(gathered.at[pl.ds(0, count)], gathered.at[pl.ds(0, count)], sem).wait()

    for todo in plan[0]:
        for step in todo:
            step[0](*step[1:])
    for r in range(1, 6):
        blocks = NX if r in (1, 5) else 2 * NX
        lax.fori_loop(0, blocks, lambda i, _: turn(r, i), 0)

    half_values = values.at[pl.ds(0, SITES * BLOCK)]
    pltpu.make_async_copy(half_values, half_values, sibling_recv.at[1]).wait()
    pltpu.make_async_copy(half_values, half_values, sibling_send.at[1]).wait()
    drain(SITES * NODES, sibling_recv.at[0])
    drain(SITES * NODES, sibling_send.at[0])
    z_rows = 3 * SECOND + HALF2 + NX * (3 * FIRST + HALF1)
    x_rows = FIRST + NZ * (SECOND + HALF2)
    for s in range(2):
        drain(z_rows, ring_send.at[s])
        drain(x_rows, ring_send.at[2 + s])
    drain(FIRST, ring_send.at[4])
    for d in range(1, NY):
        to_queries(d).wait_send()
    handed(table, 2)

    @pl.when(jnp.logical_not(home))
    def _():
        to_queries(0).wait_send()
        to_partner(own, gathered.at[rows(site, y_lo, 0, NODES)], 0).wait_send()
        to_partner(bits, landed, 1).wait_send()
        to_partner(sorted_slots, table, 2).wait_send()


def exchange(features, masks, tile_rows, tile_cols, tile_count, weights):
    slots, length = masks.shape
    vmem = pl.BlockSpec(memory_space=pltpu.VMEM)
    smem = pl.BlockSpec(memory_space=pltpu.SMEM)
    dma = pltpu.SemaphoreType.DMA
    half = jnp.bfloat16
    return pl.pallas_call(
        exchange_kernel,
        out_shape=(
            jax.ShapeDtypeStruct((SITES * 2 * NODES, D), half),
            jax.ShapeDtypeStruct((SITES * 2 * BLOCK, D, TILE), half),
            jax.ShapeDtypeStruct((NY * BLOCK, D, HEADS * TILE), half),
            jax.ShapeDtypeStruct((length // TILE, slots, TILE), jnp.int32),
            jax.ShapeDtypeStruct((8, TABLE), jnp.int32),
        ),
        in_specs=[vmem, vmem, vmem, vmem, smem, vmem],
        out_specs=(vmem,) * 5,
        scratch_shapes=[
            pltpu.VMEM((NY, BLOCK, D, TILE), half),
            pltpu.VMEM((NODES, D), half),
            pltpu.VMEM((BLOCK, D, TILE), half),
            pltpu.VMEM((D, D), half),
            pltpu.VMEM((D, D), half),
            pltpu.VMEM((slots, length), half),
            pltpu.VMEM((slots, length), half),
            pltpu.VMEM((8, TABLE), jnp.int32),
            pltpu.VMEM((D, HEADS * TILE), half),
            dma((NY,)), dma((NY,)), dma((3,)), dma((3,)),
            dma((5,)), dma((3,)), dma((2, 4, NX)), dma((2, 4)), dma((NZ, 2, 2)), dma((2,)), dma((2,)),
        ],
        compiler_params=pltpu.CompilerParams(
            collective_id=0, has_side_effects=True, vmem_limit_bytes=16 * 1024 * 1024
        ),
        name="exchange",
    )(features, masks, tile_rows, tile_cols, tile_count, weights)


def attention_kernel(
    table_ref, bias_ref, gathered, values, stationary, words,
    num_ref, den_ref, num_acc, den_acc, even_scores, odd_scores, even_weights, odd_weights,
):
    pairs = table_ref[3, 0]
    num_acc[...] = jnp.zeros_like(num_acc)
    den_acc[...] = jnp.zeros_like(den_acc)
    odd_weights[...] = jnp.zeros_like(odd_weights)
    bit_of = jnp.left_shift(jnp.int32(1), lax.broadcasted_iota(jnp.int32, (8, TILE), 0))
    half_bias = [bias_ref[h] * 0.5 for h in range(HEADS)]

    def score(p, scores):
        a = table_ref[1, 2 * p]
        sources = jnp.concatenate(
            [
                gathered[pl.ds(pl.multiple_of(table_ref[2, 2 * p + u] * TILE, TILE), TILE), :]
                for u in range(2)
            ],
            axis=0,
        )

        def part(half):
            lanes = slice(half * 2 * TILE, (half + 1) * 2 * TILE)
            scores[:, lanes] = jnp.dot(
                sources, stationary[a, :, lanes], preferred_element_type=jnp.float32
            )

        return [functools.partial(part, half) for half in range(2)]

    def weigh(p, scores, weights):
        a = table_ref[1, 2 * p]
        total = [jnp.zeros((8, TILE), jnp.float32) for _ in range(HEADS)]

        def part(u, groups):
            s = table_ref[0, 2 * p + u]
            live = jnp.where(s >= 0, bit_of, 0)
            s = jnp.maximum(s, 0)
            for g in groups:
                edge = [
                    (jnp.broadcast_to(words[w, pl.ds(s, 1), :], (8, TILE)) & live) != 0
                    for w in (2 * g, 2 * g + 1)
                ]
                here = slice(u * TILE + g * STRIP, u * TILE + (g + 1) * STRIP)
                for h in range(HEADS):
                    lanes = slice(h * TILE, (h + 1) * TILE)
                    twice = jnp.tanh(scores[here, lanes] + half_bias[h]) + 1.0
                    low = jnp.where(edge[0], twice[0:8], 0.0)
                    high = jnp.where(edge[1], twice[8:16], 0.0)
                    total[h] += low + high
                    weights[here, lanes] = jnp.concatenate([low, high], axis=0).astype(jnp.bfloat16)

        def finish():
            for h in range(HEADS):
                den_acc[a, h] += total[h]

        half = TILE // STRIP // 2
        return [
            functools.partial(part, u, range(v * half, (v + 1) * half))
            for u in range(2) for v in range(2)
        ] + [finish]

    def mix(p, weights):
        a = table_ref[1, 2 * p]
        source = [table_ref[2, 2 * p + u] for u in range(2)]

        def part(half):
            rows = slice(half * TILE, (half + 1) * TILE)
            v = jnp.concatenate([values[b, rows, :] for b in source], axis=1)
            both = jnp.dot(
                v, weights[:, half * 2 * TILE : (half + 1) * 2 * TILE],
                preferred_element_type=jnp.float32,
            )
            for side in range(2):
                start = half * TILE + side * HEAD
                num_acc[a, start : start + HEAD, :] += both[
                    side * HEAD : (side + 1) * HEAD, side * TILE : (side + 1) * TILE
                ]

        return [functools.partial(part, half) for half in range(2)]

    def together(scored, mixed, weighed):
        for k in range(2):
            scored[k]()
            mixed[k]()
        for k in range(4):
            weighed[k]()
        weighed[4]()

    for part in score(0, even_scores):
        part()

    def turn(t, _):
        p = 2 * t
        together(
            score(p + 1, odd_scores), mix(jnp.maximum(p - 1, 0), odd_weights),
            weigh(p, even_scores, even_weights),
        )
        together(
            score(p + 2, even_scores), mix(p, even_weights),
            weigh(p + 1, odd_scores, odd_weights),
        )
        return 0

    turns = (pairs + 1) // 2
    lax.fori_loop(0, turns, turn, 0)
    for part in mix(jnp.maximum(2 * turns - 1, 0), odd_weights):
        part()
    num_ref[...] = (num_acc[...] * 0.5).astype(num_ref.dtype)
    den_ref[...] = jnp.sum(den_acc[...], axis=2) * 0.5


def attention(table, bias, gathered, values, stationary, words):
    row_tiles = stationary.shape[0]
    smem = pl.BlockSpec(memory_space=pltpu.SMEM)
    vmem = pl.BlockSpec(memory_space=pltpu.VMEM)
    return pl.pallas_call(
        attention_kernel,
        out_shape=(
            jax.ShapeDtypeStruct((row_tiles, D, TILE), jnp.bfloat16),
            jax.ShapeDtypeStruct((row_tiles, HEADS, TILE), jnp.float32),
        ),
        in_specs=[smem] * 2 + [vmem] * 4,
        out_specs=(vmem, vmem),
        scratch_shapes=[
            pltpu.VMEM((row_tiles, D, TILE), jnp.float32),
            pltpu.VMEM((row_tiles, HEADS, 8, TILE), jnp.float32),
            pltpu.VMEM((2 * TILE, HEADS * TILE), jnp.float32),
            pltpu.VMEM((2 * TILE, HEADS * TILE), jnp.float32),
            pltpu.VMEM((2 * TILE, HEADS * TILE), jnp.bfloat16),
            pltpu.VMEM((2 * TILE, HEADS * TILE), jnp.bfloat16),
        ],
        compiler_params=pltpu.CompilerParams(vmem_limit_bytes=16 * 1024 * 1024),
        name="attention",
    )(table, bias, gathered, values, stationary, words)


def finish_kernel(
    features_ref, num_ref, den_ref, w_ref, gain_ref, out_ref,
    nums, dens, send, recv,
):
    z, x, y, core = position()
    y_lo = y % 2
    meet(site_partners(z, x, y, core))
    home = y_lo == core

    def part(d, src, dst, k):
        c = (y + d) % NY
        return pltpu.make_async_remote_copy(
            src_ref=src.at[c], dst_ref=dst.at[y], send_sem=send.at[k, d], recv_sem=recv.at[k, y],
            device_id=device(z, x, c // 2 * 2 + core, c % 2), device_id_type=MESH,
        )

    pairs = ((num_ref, nums), (den_ref, dens))
    for d in (1, 2, 3):
        for k, (src, dst) in enumerate(pairs):
            part(d, src, dst, k).start()
    for k, (src, dst) in enumerate(pairs):
        @pl.when(home)
        def _():
            pltpu.make_async_copy(src.at[y], dst.at[y], recv.at[k, y]).start()

        @pl.when(jnp.logical_not(home))
        def _():
            part(0, src, dst, k).start()

    for c in range(NY):
        for k, (src, dst) in enumerate(pairs):
            pltpu.make_async_copy(dst.at[c], dst.at[c], recv.at[k, c]).wait()
    total = sum(nums[c].astype(jnp.float32) for c in range(NY))
    weight = 1.0 + sum(dens[c] for c in range(NY))
    gain = gain_ref[...]
    node, lane_node = lane_order()
    to_nodes = jnp.transpose(jnp.where(node == lane_node, 1.0, 0.0)).astype(jnp.bfloat16)
    for t in range(NODES // TILE):
        mixed = total[t].reshape(HEADS, HEAD, TILE) / weight[t].reshape(HEADS, 1, TILE)
        mixed = mixed.reshape(D, TILE).astype(jnp.bfloat16)
        mixed = jnp.dot(mixed, to_nodes, preferred_element_type=jnp.float32).astype(jnp.bfloat16)
        projected = lax.dot_general(
            mixed, w_ref[...], (((0,), (0,)), ((), ())), preferred_element_type=jnp.float32
        )
        square = jnp.mean(projected * projected, axis=1, keepdims=True)
        here = pl.ds(t * TILE, TILE)
        out_ref[here, :] = features_ref[here, :] + gain * projected * lax.rsqrt(square + 1e-05)
    for d in range(NY):
        for k, (src, dst) in enumerate(pairs):
            if d:
                part(d, src, dst, k).wait_send()
            else:
                @pl.when(jnp.logical_not(home))
                def _():
                    part(d, src, dst, k).wait_send()


def finish(features, numerator, denominator, w_out, gain):
    vmem = pl.BlockSpec(memory_space=pltpu.VMEM)
    hbm = pl.BlockSpec(memory_space=pl.ANY)
    dma = pltpu.SemaphoreType.DMA
    return pl.pallas_call(
        finish_kernel,
        out_shape=jax.ShapeDtypeStruct(features.shape, jnp.float32),
        in_specs=[vmem, hbm, hbm, vmem, vmem],
        out_specs=vmem,
        scratch_shapes=[
            pltpu.VMEM(numerator.shape, numerator.dtype),
            pltpu.VMEM(denominator.shape, denominator.dtype),
            dma((2, NY)), dma((2, NY)),
        ],
        compiler_params=pltpu.CompilerParams(
            collective_id=1, has_side_effects=True, vmem_limit_bytes=32 * 1024 * 1024
        ),
        name="finish",
    )(features, numerator, denominator, w_out, gain)


def local(
    features, w_qkv, w_out, head_bias, out_gain, tile_rows, tile_cols, tile_masks, tile_count
):
    block_tiles = features.shape[0] // TILE
    gathered, values, stationary, words, table = exchange(
        features, tile_masks[0], tile_rows, tile_cols, tile_count, w_qkv
    )
    numerator, denominator = attention(
        table, head_bias, gathered, values, stationary, words
    )
    return finish(
        features,
        numerator.reshape(NY, block_tiles, D, TILE),
        denominator.reshape(NY, block_tiles, HEADS, TILE),
        w_out, out_gain[None, :],
    )


def solution(mesh):
    placed = (
        P(("row", "col"), None),
        P(),
        P(),
        P(),
        P(),
        P(("row", "col"), None),
        P(("row", "col"), None),
        P(("row", "col"), None, None),
        P(("row", "col")),
    )
    return jax.shard_map(
        local, mesh=mesh, in_specs=placed, out_specs=P(("row", "col"), None), check_vma=False
    )
```

```python
import functools

import jax
import jax.numpy as jnp
from jax import lax
from jax.experimental import pallas as pl
from jax.experimental.pallas import tpu as pltpu
from jax.sharding import PartitionSpec as P

TILE = 128
HEADS = 4
HEAD = 64
D = 256
STRIP = 16
TABLE = 384
NX, NY, NZ = 4, 4, 8
SITES = NX * NZ
NODES = 384
FIRST = 160
SECOND = NODES - FIRST
BLOCK = NODES // TILE
MESH = pl.DeviceIdType.MESH
NT = (((1,), (1,)), ((), ()))


def position():
    row, col = lax.axis_index("row"), lax.axis_index("col")
    return row // 8, row // 2 % 4, col // 2 * 2 + row % 2, col % 2


def device(z, x, y, core):
    return ((z * NX + x) * 2 + y % 2, y // 2 * 2 + core)


def meet(partners, meanwhile=None):
    barrier = pltpu.get_barrier_semaphore()
    for partner in partners:
        pl.semaphore_signal(barrier, inc=1, device_id=partner, device_id_type=MESH)
    if meanwhile is not None:
        meanwhile()
    pl.semaphore_wait(barrier, len(partners))


def site_partners(z, x, y, core):
    found = [device(z, x, y, 1 - core)]
    for d in range(1, NY):
        found += [device(z, x, (y + d) % NY, core), device(z, x, (y + d) % NY, 1 - core)]
    return found


def lane_order():
    node = lax.broadcasted_iota(jnp.int32, (TILE, TILE), 0)
    lane = lax.broadcasted_iota(jnp.int32, (TILE, TILE), 1)
    return node, lane % 16 * 8 + lane // 16


def exchange_kernel(
    features_ref, masks_ref, rows_ref, cols_ref, count_ref, weights_ref,
    gathered, values, stationary, words, table,
    queries, own, own_queries, wq, wv, bits, landed, sorted_slots, diagonal,
    query_send, query_recv, list_send, list_recv,
    ring_send, first_x, first_z, second_z, second_x, sibling_send, sibling_recv,
):
    z, x, y, core = position()
    y_lo, y_hi = y % 2, y // 2
    site = z * NX + x

    def setup():
        own[...] = features_ref[...].astype(jnp.bfloat16)
        wq[...] = jnp.transpose(weights_ref[:, 0:D])
        wv[...] = jnp.transpose(weights_ref[:, 2 * D : 3 * D])
        bits[...] = masks_ref[...].astype(jnp.float32).astype(jnp.bfloat16)
        diagonal[...] = jnp.zeros_like(diagonal)

    meet(
        site_partners(z, x, y, core)
        + [device(z, (x + d) % NX, y, core) for d in (1, 2, 3)]
        + [device((z + d) % NZ, x, y, core) for d in (1, 7)],
        setup,
    )

    my_list = y_hi * 2 + core
    home = y_lo == core
    partner = device(z, x, y_hi * 2 + core, y_lo)

    def to_partner(src, dst, k):
        return pltpu.make_async_remote_copy(
            src_ref=src, dst_ref=dst, send_sem=list_send.at[k], recv_sem=list_recv.at[k],
            device_id=partner, device_id_type=MESH,
        )

    def hand_over(src, dst, k):
        @pl.when(home)
        def _():
            pltpu.make_async_copy(src, dst, list_recv.at[k]).start()

        @pl.when(jnp.logical_not(home))
        def _():
            to_partner(src, dst, k).start()

    def handed(ref, k):
        pltpu.make_async_copy(ref, ref, list_recv.at[k]).wait()

    def rows(a_site, parity, low, count):
        return pl.ds(pl.multiple_of((a_site * 2 + parity) * NODES + low, 16), count)

    def remote(src, dst, send, recv, target):
        pltpu.make_async_remote_copy(
            src_ref=src, dst_ref=dst, send_sem=send, recv_sem=recv,
            device_id=target, device_id_type=MESH,
        ).start()

    def arrived(a_site, low, count, sem):
        here = gathered.at[rows(a_site, core, low, count)]
        pltpu.make_async_copy(here, here, sem).wait()

    def forward(a_site, low, count, send, recv, target):
        here = gathered.at[rows(a_site, core, low, count)]
        remote(here, here, send, recv, target)

    up, down = device((z + 1) % NZ, x, y, core), device((z + 7) % NZ, x, y, core)
    right, left = device(z, (x + 1) % NX, y, core), device(z, (x + 3) % NX, y, core)
    across = device(z, (x + 2) % NX, y, core)
    other = device(z, x, y, 1 - core)
    z_to, x_to = (up, down), (right, left)

    def site_of(dz, dx):
        return (z + dz + NZ) % NZ * NX + (x + dx + NX) % NX

    def to_queries(d):
        return pltpu.make_async_remote_copy(
            src_ref=own_queries, dst_ref=queries.at[my_list],
            send_sem=query_send.at[d], recv_sem=query_recv.at[my_list],
            device_id=device(z, x, (y_hi * 2 + core + d) % NY, y_lo), device_id_type=MESH,
        )

    def prepare():
        node, lane_node = lane_order()
        to_lanes = jnp.where(node == lane_node, 1.0, 0.0).astype(jnp.bfloat16)
        q = lax.dot_general(wq[...], own[...], NT, preferred_element_type=jnp.float32)
        q = q.astype(jnp.bfloat16) * jnp.bfloat16(0.0625)
        for t in range(BLOCK):
            own_queries[t] = jnp.dot(
                q[:, t * TILE : (t + 1) * TILE], to_lanes, preferred_element_type=jnp.float32
            ).astype(jnp.bfloat16)
        sort_slots()

    def fold(c, t):
        if t == 0:
            pltpu.make_async_copy(queries.at[c], queries.at[c], query_recv.at[c]).wait()
        for h in range(HEADS):
            diagonal[h * HEAD : (h + 1) * HEAD, h * TILE : (h + 1) * TILE] = (
                queries[c, t, h * HEAD : (h + 1) * HEAD, :]
            )
        stationary[c * BLOCK + t] = jnp.dot(
            weights_ref[:, D : 2 * D], diagonal[...], preferred_element_type=jnp.float32
        ).astype(jnp.bfloat16)

    def spread(c):
        words[c] = landed[:, c * TILE : (c + 1) * TILE].astype(jnp.float32).astype(jnp.int32)

    def swap_bit(b):
        step = 1 << b
        slots = words.shape[1]
        upper = (lax.broadcasted_iota(jnp.int32, (slots, TILE), 1) // step) % 2 == 1
        for c in range(words.shape[0]):
            if c & step == 0:
                low, high = words[c], words[c + step]
                words[c] = jnp.where(upper, pltpu.roll(high, step, 1), low)
                words[c + step] = jnp.where(upper, high, pltpu.roll(low, TILE - step, 1))

    def start_words():
        handed(landed, 1)
        for c in range(words.shape[0]):
            spread(c)

    def sort_slots():
        slots = rows_ref.shape[1]
        row_tiles = NY * BLOCK
        to, source = rows_ref[...].astype(jnp.float32), cols_ref[...].astype(jnp.float32)
        count = jnp.full((1, slots), count_ref[0], jnp.int32).astype(jnp.float32)
        slot = lax.broadcasted_iota(jnp.int32, (1, slots), 1).astype(jnp.float32)
        a = to - row_tiles * jnp.floor((to + 0.5) * (1.0 / row_tiles))
        b = BLOCK * jnp.floor((source + 0.5) * (1.0 / row_tiles)) + (
            source - BLOCK * jnp.floor((source + 0.5) * (1.0 / BLOCK))
        )
        a = jnp.where(slot < count, a, float(row_tiles))
        base = jnp.zeros_like(a)
        total = jnp.zeros((1, 1), jnp.float32)
        for tile in range(row_tiles):
            number = jnp.sum(jnp.where(a == tile, 1.0, 0.0), axis=1, keepdims=True)
            number = 2.0 * jnp.floor((number + 1.5) * 0.5)
            base += jnp.where(a > tile, number, 0.0)
            total += number
        across_lanes = jnp.broadcast_to(a, (slots, slots))
        down = jnp.transpose(across_lanes)
        earlier = lax.broadcasted_iota(jnp.int32, (slots, slots), 0) < lax.broadcasted_iota(
            jnp.int32, (slots, slots), 1
        )
        rank = jnp.sum(
            jnp.where((across_lanes == down) & earlier, 1.0, 0.0), axis=0, keepdims=True
        )
        at = jnp.where(a < row_tiles, base + rank, float(TABLE))
        at_down = jnp.transpose(jnp.broadcast_to(at, (TABLE, slots)))
        hit = at_down == lax.broadcasted_iota(jnp.int32, (slots, TABLE), 1).astype(jnp.float32)

        def pick(value):
            down = jnp.transpose(jnp.broadcast_to(value, (TABLE, slots)))
            return jnp.sum(jnp.where(hit, down, 0.0), axis=0, keepdims=True)

        sorted_slots[0:1, :] = (pick(slot + 1.0) - 1.0).astype(jnp.int32)
        sorted_slots[1:2, :] = pick(a).astype(jnp.int32)
        sorted_slots[2:3, :] = pick(b).astype(jnp.int32)
        sorted_slots[3:4, :] = jnp.broadcast_to(total * 0.5, (1, TABLE)).astype(jnp.int32)
        sorted_slots[4:8, :] = jnp.zeros((4, TABLE), jnp.int32)

    hand_over(own, gathered.at[rows(site, y_lo, 0, NODES)], 0)

    @pl.when(jnp.logical_not(home))
    def _():
        prepare()

    handed(gathered.at[rows(site, core, 0, NODES)], 0)
    for s in range(2):
        forward(site, FIRST, SECOND, ring_send.at[s], second_z.at[s, 0], z_to[s])
        forward(site, 0, FIRST, ring_send.at[2 + s], first_x.at[s], x_to[s])
    forward(site, 0, FIRST, ring_send.at[4], first_x.at[2], across)
    for s in range(2):
        forward(site, FIRST, SECOND, ring_send.at[2 + s], second_x.at[0, s, 0], x_to[s])
        forward(site, 0, FIRST, ring_send.at[s], first_z.at[s, 0, 0], z_to[s])

    @pl.when(home)
    def _():
        prepare()
        pltpu.make_async_copy(own_queries, queries.at[my_list], query_recv.at[my_list]).start()

    @pl.when(jnp.logical_not(home))
    def _():
        to_queries(0).start()

    for d in (1, 2, 3):
        to_queries(d).start()
    hand_over(bits, landed, 1)
    hand_over(sorted_slots, table, 2)

    X_OFF = (0, -1, 1, 2)
    Z_OFF = (0, -1, 1, -2, 2, -3, 3, 4)
    HALF1, HALF2 = FIRST // 2, SECOND // 2

    def second_z_step(t):
        for s in range(2):
            sign = -1 if s == 0 else 1
            if t < 4:
                a = site_of(sign * t, 0)
                arrived(a, FIRST, SECOND, second_z.at[s, t - 1])
                if t < 3:
                    forward(a, FIRST, SECOND, ring_send.at[s], second_z.at[s, t], z_to[s])
                else:
                    forward(a, FIRST + s * HALF2, HALF2, ring_send.at[s], second_z.at[s, 3], z_to[s])
                k = Z_OFF.index(sign * t)
                for e in range(2):
                    forward(a, FIRST, SECOND, ring_send.at[2 + e], second_x.at[k, e, 0], x_to[e])
        if t == 4:
            a = site_of(4, 0)
            for s in range(2):
                arrived(a, FIRST + s * HALF2, HALF2, second_z.at[s, 3])
            for e in range(2):
                forward(a, FIRST, SECOND, ring_send.at[2 + e], second_x.at[7, e, 0], x_to[e])

    def first_x_step(*which):
        for k in which:
            a = site_of(0, X_OFF[k + 1])
            arrived(a, 0, FIRST, first_x.at[k])
            for s in range(2):
                forward(a, 0, FIRST, ring_send.at[s], first_z.at[s, 0, k + 1], z_to[s])

    def first_z_step(t, k):
        if t < 4:
            for s in range(2):
                sign = -1 if s == 0 else 1
                a = site_of(sign * t, X_OFF[k])
                arrived(a, 0, FIRST, first_z.at[s, t - 1, k])
                if t < 3:
                    forward(a, 0, FIRST, ring_send.at[s], first_z.at[s, t, k], z_to[s])
                else:
                    forward(a, s * HALF1, HALF1, ring_send.at[s], first_z.at[s, 3, k], z_to[s])
        else:
            a = site_of(4, X_OFF[k])
            for s in range(2):
                arrived(a, s * HALF1, HALF1, first_z.at[s, 3, k])

    def second_x_step(k):
        for e in range(2):
            sign = -1 if e == 0 else 1
            a = site_of(Z_OFF[k], sign)
            arrived(a, FIRST, SECOND, second_x.at[k, e, 0])
            forward(a, FIRST + e * HALF2, HALF2, ring_send.at[2 + e], second_x.at[k, e, 1], x_to[e])

    def second_x_end(k):
        a = site_of(Z_OFF[k], 2)
        for e in range(2):
            arrived(a, FIRST + e * HALF2, HALF2, second_x.at[k, e, 1])

    def project(dz, k):
        a = site_of(dz, X_OFF[k])
        start = pl.multiple_of((a * 2 + core) * NODES, NODES)
        tile = (a * 2 + core) * BLOCK
        forward(a, 0, NODES, sibling_send.at[0], sibling_recv.at[0], other)
        v = lax.dot_general(
            wv[...], gathered[pl.ds(start, NODES), :], NT, preferred_element_type=jnp.float32
        ).astype(jnp.bfloat16)
        for t in range(BLOCK):
            values[tile + t] = v[:, t * TILE : (t + 1) * TILE]
        done = values.at[pl.ds(tile, BLOCK)]
        remote(done, done, sibling_send.at[1], sibling_recv.at[1], other)

    def drain(count, sem):
        pltpu.make_async_copy(gathered.at[pl.ds(0, count)], gathered.at[pl.ds(0, count)], sem).wait()

    order = [
        (project, 0, 0), (first_z_step, 1, 0), (second_z_step, 1), (project, -1, 0), (project, 1, 0),
        (first_x_step, 0, 1), (first_x_step, 2), (second_x_step, 0), (project, 0, 1), (project, 0, 2),
        (first_z_step, 2, 0), (fold, 0, 0), (fold, 0, 1), (fold, 0, 2), (fold, 1, 0), (fold, 1, 1),
        (fold, 1, 2), (fold, 2, 0), (fold, 2, 1), (fold, 2, 2), (fold, 3, 0), (second_x_step, 1),
        (second_x_step, 2), (fold, 3, 1), (fold, 3, 2), (second_x_end, 0), (project, 0, 3),
        (second_z_step, 2), (project, -2, 0), (project, 2, 0), (first_z_step, 1, 1), (first_z_step, 1, 2),
        (first_z_step, 1, 3), (project, -1, 1), (project, -1, 2), (project, 1, 1), (first_z_step, 3, 0),
        (project, 1, 2), (start_words,), (second_x_end, 1), (project, -1, 3), (second_x_end, 2),
        (project, 1, 3), (swap_bit, 0), (swap_bit, 1), (swap_bit, 2), (swap_bit, 3), (second_z_step, 3),
        (project, -3, 0), (project, 3, 0), (second_x_step, 3), (second_x_step, 4), (first_z_step, 4, 0),
        (first_z_step, 2, 1), (project, -2, 1), (first_z_step, 2, 2), (first_z_step, 2, 3), (project, -2, 2),
        (project, 2, 1), (second_z_step, 4), (project, 2, 2), (project, 4, 0), (second_x_end, 3),
        (project, -2, 3), (second_x_end, 4), (project, 2, 3), (second_x_step, 5), (first_z_step, 3, 1),
        (second_x_step, 6), (project, -3, 1), (project, 3, 1), (first_z_step, 3, 2), (first_z_step, 3, 3),
        (project, -3, 2), (project, 3, 2), (second_x_step, 7), (first_z_step, 4, 1), (project, 4, 1),
        (second_x_end, 5), (project, -3, 3), (first_z_step, 4, 2), (project, 4, 2), (first_z_step, 4, 3),
        (second_x_end, 6), (project, 3, 3), (second_x_end, 7), (project, 4, 3),
    ]
    for step in order:
        step[0](*step[1:])

    half_values = values.at[pl.ds(0, SITES * BLOCK)]
    pltpu.make_async_copy(half_values, half_values, sibling_recv.at[1]).wait()
    pltpu.make_async_copy(half_values, half_values, sibling_send.at[1]).wait()
    drain(SITES * NODES, sibling_recv.at[0])
    drain(SITES * NODES, sibling_send.at[0])
    z_rows = 3 * SECOND + HALF2 + NX * (3 * FIRST + HALF1)
    x_rows = FIRST + NZ * (SECOND + HALF2)
    for s in range(2):
        drain(z_rows, ring_send.at[s])
        drain(x_rows, ring_send.at[2 + s])
    drain(FIRST, ring_send.at[4])
    for d in range(1, NY):
        to_queries(d).wait_send()
    handed(table, 2)

    @pl.when(jnp.logical_not(home))
    def _():
        to_queries(0).wait_send()
        to_partner(own, gathered.at[rows(site, y_lo, 0, NODES)], 0).wait_send()
        to_partner(bits, landed, 1).wait_send()
        to_partner(sorted_slots, table, 2).wait_send()


def exchange(features, masks, tile_rows, tile_cols, tile_count, weights):
    slots, length = masks.shape
    vmem = pl.BlockSpec(memory_space=pltpu.VMEM)
    smem = pl.BlockSpec(memory_space=pltpu.SMEM)
    dma = pltpu.SemaphoreType.DMA
    half = jnp.bfloat16
    return pl.pallas_call(
        exchange_kernel,
        out_shape=(
            jax.ShapeDtypeStruct((SITES * 2 * NODES, D), half),
            jax.ShapeDtypeStruct((SITES * 2 * BLOCK, D, TILE), half),
            jax.ShapeDtypeStruct((NY * BLOCK, D, HEADS * TILE), half),
            jax.ShapeDtypeStruct((length // TILE, slots, TILE), jnp.int32),
            jax.ShapeDtypeStruct((8, TABLE), jnp.int32),
        ),
        in_specs=[vmem, vmem, vmem, vmem, smem, vmem],
        out_specs=(vmem,) * 5,
        scratch_shapes=[
            pltpu.VMEM((NY, BLOCK, D, TILE), half),
            pltpu.VMEM((NODES, D), half),
            pltpu.VMEM((BLOCK, D, TILE), half),
            pltpu.VMEM((D, D), half),
            pltpu.VMEM((D, D), half),
            pltpu.VMEM((slots, length), half),
            pltpu.VMEM((slots, length), half),
            pltpu.VMEM((8, TABLE), jnp.int32),
            pltpu.VMEM((D, HEADS * TILE), half),
            dma((NY,)), dma((NY,)), dma((3,)), dma((3,)),
            dma((5,)), dma((3,)), dma((2, 4, NX)), dma((2, 4)), dma((NZ, 2, 2)), dma((2,)), dma((2,)),
        ],
        compiler_params=pltpu.CompilerParams(
            collective_id=0, has_side_effects=True, vmem_limit_bytes=16 * 1024 * 1024
        ),
        name="exchange",
    )(features, masks, tile_rows, tile_cols, tile_count, weights)


def attention_kernel(
    table_ref, bias_ref, gathered, values, stationary, words,
    num_ref, den_ref, num_acc, den_acc, even_weights, odd_weights,
):
    pairs = table_ref[3, 0]
    num_acc[...] = jnp.zeros_like(num_acc)
    den_acc[...] = jnp.zeros_like(den_acc)
    odd_weights[...] = jnp.zeros_like(odd_weights)
    bit_of = jnp.left_shift(jnp.int32(1), lax.broadcasted_iota(jnp.int32, (8, TILE), 0))
    half_bias = [bias_ref[h] * 0.5 for h in range(HEADS)]

    def weigh(p, weights):
        a = table_ref[1, 2 * p]
        slots = [table_ref[0, 2 * p + u] for u in range(2)]
        sources = jnp.concatenate(
            [
                gathered[pl.ds(pl.multiple_of(table_ref[2, 2 * p + u] * TILE, TILE), TILE), :]
                for u in range(2)
            ],
            axis=0,
        )

        def part(half):
            scores = jnp.dot(
                sources, stationary[a, :, half * 2 * TILE : (half + 1) * 2 * TILE],
                preferred_element_type=jnp.float32,
            )
            total = [jnp.zeros((8, TILE), jnp.float32) for _ in range(2)]
            for u, s in enumerate(slots):
                live = jnp.where(s >= 0, bit_of, 0)
                s = jnp.maximum(s, 0)
                for g in range(TILE // STRIP):
                    edge = [
                        (jnp.broadcast_to(words[w, pl.ds(s, 1), :], (8, TILE)) & live) != 0
                        for w in (2 * g, 2 * g + 1)
                    ]
                    here = slice(u * TILE + g * STRIP, u * TILE + (g + 1) * STRIP)
                    for side in range(2):
                        h = half * 2 + side
                        score = scores[here, side * TILE : (side + 1) * TILE]
                        twice = jnp.tanh(score + half_bias[h]) + 1.0
                        low = jnp.where(edge[0], twice[0:8], 0.0)
                        high = jnp.where(edge[1], twice[8:16], 0.0)
                        total[side] += low + high
                        weights[here, h * TILE : (h + 1) * TILE] = jnp.concatenate(
                            [low, high], axis=0
                        ).astype(jnp.bfloat16)
            for side in range(2):
                den_acc[a, half * 2 + side] += total[side]

        return [functools.partial(part, half) for half in range(2)]

    def mix(p, weights):
        a = table_ref[1, 2 * p]
        source = [table_ref[2, 2 * p + u] for u in range(2)]

        def part(half):
            rows = slice(half * TILE, (half + 1) * TILE)
            v = jnp.concatenate([values[b, rows, :] for b in source], axis=1)
            both = jnp.dot(
                v, weights[:, half * 2 * TILE : (half + 1) * 2 * TILE],
                preferred_element_type=jnp.float32,
            )
            for side in range(2):
                start = half * TILE + side * HEAD
                num_acc[a, start : start + HEAD, :] += both[
                    side * HEAD : (side + 1) * HEAD, side * TILE : (side + 1) * TILE
                ]

        return [functools.partial(part, half) for half in range(2)]

    def together(weighed, mixed):
        for k in range(2):
            weighed[k]()
            mixed[k]()

    def turn(t, _):
        p = 2 * t
        together(weigh(p, even_weights), mix(jnp.maximum(p - 1, 0), odd_weights))
        together(weigh(p + 1, odd_weights), mix(p, even_weights))
        return 0

    turns = (pairs + 1) // 2
    lax.fori_loop(0, turns, turn, 0)
    for part in mix(jnp.maximum(2 * turns - 1, 0), odd_weights):
        part()
    num_ref[...] = (num_acc[...] * 0.5).astype(num_ref.dtype)
    den_ref[...] = jnp.sum(den_acc[...], axis=2) * 0.5


def attention(table, bias, gathered, values, stationary, words):
    row_tiles = stationary.shape[0]
    smem = pl.BlockSpec(memory_space=pltpu.SMEM)
    vmem = pl.BlockSpec(memory_space=pltpu.VMEM)
    return pl.pallas_call(
        attention_kernel,
        out_shape=(
            jax.ShapeDtypeStruct((row_tiles, D, TILE), jnp.bfloat16),
            jax.ShapeDtypeStruct((row_tiles, HEADS, TILE), jnp.float32),
        ),
        in_specs=[smem] * 2 + [vmem] * 4,
        out_specs=(vmem, vmem),
        scratch_shapes=[
            pltpu.VMEM((row_tiles, D, TILE), jnp.float32),
            pltpu.VMEM((row_tiles, HEADS, 8, TILE), jnp.float32),
            pltpu.VMEM((2 * TILE, HEADS * TILE), jnp.bfloat16),
            pltpu.VMEM((2 * TILE, HEADS * TILE), jnp.bfloat16),
        ],
        compiler_params=pltpu.CompilerParams(vmem_limit_bytes=16 * 1024 * 1024),
        name="attention",
    )(table, bias, gathered, values, stationary, words)


def finish_kernel(
    features_ref, num_ref, den_ref, w_ref, gain_ref, out_ref,
    nums, dens, send, recv,
):
    z, x, y, core = position()
    y_lo = y % 2
    meet(site_partners(z, x, y, core))
    home = y_lo == core

    def part(d, src, dst, k):
        c = (y + d) % NY
        return pltpu.make_async_remote_copy(
            src_ref=src.at[c], dst_ref=dst.at[y], send_sem=send.at[k, d], recv_sem=recv.at[k, y],
            device_id=device(z, x, c // 2 * 2 + core, c % 2), device_id_type=MESH,
        )

    pairs = ((num_ref, nums), (den_ref, dens))
    for d in (1, 2, 3):
        for k, (src, dst) in enumerate(pairs):
            part(d, src, dst, k).start()
    for k, (src, dst) in enumerate(pairs):
        @pl.when(home)
        def _():
            pltpu.make_async_copy(src.at[y], dst.at[y], recv.at[k, y]).start()

        @pl.when(jnp.logical_not(home))
        def _():
            part(0, src, dst, k).start()

    for c in range(NY):
        for k, (src, dst) in enumerate(pairs):
            pltpu.make_async_copy(dst.at[c], dst.at[c], recv.at[k, c]).wait()
    total = sum(nums[c].astype(jnp.float32) for c in range(NY))
    weight = 1.0 + sum(dens[c] for c in range(NY))
    gain = gain_ref[...]
    node, lane_node = lane_order()
    to_nodes = jnp.transpose(jnp.where(node == lane_node, 1.0, 0.0)).astype(jnp.bfloat16)
    for t in range(NODES // TILE):
        mixed = total[t].reshape(HEADS, HEAD, TILE) / weight[t].reshape(HEADS, 1, TILE)
        mixed = mixed.reshape(D, TILE).astype(jnp.bfloat16)
        mixed = jnp.dot(mixed, to_nodes, preferred_element_type=jnp.float32).astype(jnp.bfloat16)
        projected = lax.dot_general(
            mixed, w_ref[...], (((0,), (0,)), ((), ())), preferred_element_type=jnp.float32
        )
        square = jnp.mean(projected * projected, axis=1, keepdims=True)
        here = pl.ds(t * TILE, TILE)
        out_ref[here, :] = features_ref[here, :] + gain * projected * lax.rsqrt(square + 1e-05)
    for d in range(NY):
        for k, (src, dst) in enumerate(pairs):
            if d:
                part(d, src, dst, k).wait_send()
            else:
                @pl.when(jnp.logical_not(home))
                def _():
                    part(d, src, dst, k).wait_send()


def finish(features, numerator, denominator, w_out, gain):
    vmem = pl.BlockSpec(memory_space=pltpu.VMEM)
    hbm = pl.BlockSpec(memory_space=pl.ANY)
    dma = pltpu.SemaphoreType.DMA
    return pl.pallas_call(
        finish_kernel,
        out_shape=jax.ShapeDtypeStruct(features.shape, jnp.float32),
        in_specs=[vmem, hbm, hbm, vmem, vmem],
        out_specs=vmem,
        scratch_shapes=[
            pltpu.VMEM(numerator.shape, numerator.dtype),
            pltpu.VMEM(denominator.shape, denominator.dtype),
            dma((2, NY)), dma((2, NY)),
        ],
        compiler_params=pltpu.CompilerParams(
            collective_id=1, has_side_effects=True, vmem_limit_bytes=32 * 1024 * 1024
        ),
        name="finish",
    )(features, numerator, denominator, w_out, gain)


def local(
    features, w_qkv, w_out, head_bias, out_gain, tile_rows, tile_cols, tile_masks, tile_count
):
    block_tiles = features.shape[0] // TILE
    gathered, values, stationary, words, table = exchange(
        features, tile_masks[0], tile_rows, tile_cols, tile_count, w_qkv
    )
    numerator, denominator = attention(
        table, head_bias, gathered, values, stationary, words
    )
    return finish(
        features,
        numerator.reshape(NY, block_tiles, D, TILE),
        denominator.reshape(NY, block_tiles, HEADS, TILE),
        w_out, out_gain[None, :],
    )


def solution(mesh):
    placed = (
        P(("row", "col"), None),
        P(),
        P(),
        P(),
        P(),
        P(("row", "col"), None),
        P(("row", "col"), None),
        P(("row", "col"), None, None),
        P(("row", "col")),
    )
    return jax.shard_map(
        local, mesh=mesh, in_specs=placed, out_specs=P(("row", "col"), None), check_vma=False
    )
```

```python
import functools

import jax
import jax.numpy as jnp
from jax import lax
from jax.experimental import pallas as pl
from jax.experimental.pallas import tpu as pltpu
from jax.sharding import PartitionSpec as P

TILE = 128
HEADS = 4
HEAD = 64
D = 256
STRIP = 16
UNROLL = 4
TABLE = 384
NX, NY, NZ = 4, 4, 8
SITES = NX * NZ
NODES = 384
FIRST = 160
SECOND = NODES - FIRST
BLOCK = NODES // TILE
MESH = pl.DeviceIdType.MESH
NT = (((1,), (1,)), ((), ()))


def position():
    row, col = lax.axis_index("row"), lax.axis_index("col")
    return row // 8, row // 2 % 4, col // 2 * 2 + row % 2, col % 2


def device(z, x, y, core):
    return ((z * NX + x) * 2 + y % 2, y // 2 * 2 + core)


def meet(partners, meanwhile=None):
    barrier = pltpu.get_barrier_semaphore()
    for partner in partners:
        pl.semaphore_signal(barrier, inc=1, device_id=partner, device_id_type=MESH)
    if meanwhile is not None:
        meanwhile()
    pl.semaphore_wait(barrier, len(partners))


def site_partners(z, x, y, core):
    found = [device(z, x, y, 1 - core)]
    for d in range(1, NY):
        found += [device(z, x, (y + d) % NY, core), device(z, x, (y + d) % NY, 1 - core)]
    return found


def lane_order():
    node = lax.broadcasted_iota(jnp.int32, (TILE, TILE), 0)
    lane = lax.broadcasted_iota(jnp.int32, (TILE, TILE), 1)
    return node, lane % 16 * 8 + lane // 16


def exchange_kernel(
    features_ref, masks_ref, rows_ref, cols_ref, count_ref, weights_ref,
    gathered, values, stationary, words, table,
    queries, own, own_queries, wq, wv, bits, landed, sorted_slots, diagonal,
    query_send, query_recv, list_send, list_recv,
    ring_send, first_x, first_z, second_z, second_x, sibling_send, sibling_recv,
):
    z, x, y, core = position()
    y_lo, y_hi = y % 2, y // 2
    site = z * NX + x

    def setup():
        own[...] = features_ref[...].astype(jnp.bfloat16)
        wq[...] = jnp.transpose(weights_ref[:, 0:D])
        wv[...] = jnp.transpose(weights_ref[:, 2 * D : 3 * D])
        bits[...] = masks_ref[...].astype(jnp.float32).astype(jnp.bfloat16)
        diagonal[...] = jnp.zeros_like(diagonal)

    meet(
        site_partners(z, x, y, core)
        + [device(z, (x + d) % NX, y, core) for d in (1, 2, 3)]
        + [device((z + d) % NZ, x, y, core) for d in (1, 7)],
        setup,
    )

    my_list = y_hi * 2 + core
    home = y_lo == core
    partner = device(z, x, y_hi * 2 + core, y_lo)

    def to_partner(src, dst, k):
        return pltpu.make_async_remote_copy(
            src_ref=src, dst_ref=dst, send_sem=list_send.at[k], recv_sem=list_recv.at[k],
            device_id=partner, device_id_type=MESH,
        )

    def hand_over(src, dst, k):
        @pl.when(home)
        def _():
            pltpu.make_async_copy(src, dst, list_recv.at[k]).start()

        @pl.when(jnp.logical_not(home))
        def _():
            to_partner(src, dst, k).start()

    def handed(ref, k):
        pltpu.make_async_copy(ref, ref, list_recv.at[k]).wait()

    def rows(a_site, parity, low, count):
        return pl.ds(pl.multiple_of((a_site * 2 + parity) * NODES + low, 16), count)

    def remote(src, dst, send, recv, target):
        pltpu.make_async_remote_copy(
            src_ref=src, dst_ref=dst, send_sem=send, recv_sem=recv,
            device_id=target, device_id_type=MESH,
        ).start()

    def arrived(a_site, low, count, sem):
        here = gathered.at[rows(a_site, core, low, count)]
        pltpu.make_async_copy(here, here, sem).wait()

    def forward(a_site, low, count, send, recv, target):
        here = gathered.at[rows(a_site, core, low, count)]
        remote(here, here, send, recv, target)

    up, down = device((z + 1) % NZ, x, y, core), device((z + 7) % NZ, x, y, core)
    right, left = device(z, (x + 1) % NX, y, core), device(z, (x + 3) % NX, y, core)
    across = device(z, (x + 2) % NX, y, core)
    other = device(z, x, y, 1 - core)
    z_to, x_to = (up, down), (right, left)

    def site_of(dz, dx):
        return (z + dz + NZ) % NZ * NX + (x + dx + NX) % NX

    def to_queries(d):
        return pltpu.make_async_remote_copy(
            src_ref=own_queries, dst_ref=queries.at[my_list],
            send_sem=query_send.at[d], recv_sem=query_recv.at[my_list],
            device_id=device(z, x, (y_hi * 2 + core + d) % NY, y_lo), device_id_type=MESH,
        )

    def prepare():
        node, lane_node = lane_order()
        to_lanes = jnp.where(node == lane_node, 1.0, 0.0).astype(jnp.bfloat16)
        q = lax.dot_general(wq[...], own[...], NT, preferred_element_type=jnp.float32)
        q = q.astype(jnp.bfloat16) * jnp.bfloat16(0.0625)
        for t in range(BLOCK):
            own_queries[t] = jnp.dot(
                q[:, t * TILE : (t + 1) * TILE], to_lanes, preferred_element_type=jnp.float32
            ).astype(jnp.bfloat16)
        sort_slots()

    def fold(c, t):
        if t == 0:
            pltpu.make_async_copy(queries.at[c], queries.at[c], query_recv.at[c]).wait()
        for h in range(HEADS):
            diagonal[h * HEAD : (h + 1) * HEAD, h * TILE : (h + 1) * TILE] = (
                queries[c, t, h * HEAD : (h + 1) * HEAD, :]
            )
        stationary[c * BLOCK + t] = jnp.dot(
            weights_ref[:, D : 2 * D], diagonal[...], preferred_element_type=jnp.float32
        ).astype(jnp.bfloat16)

    def spread(c):
        words[c] = landed[:, c * TILE : (c + 1) * TILE].astype(jnp.float32).astype(jnp.int32)

    def swap_bit(b):
        step = 1 << b
        slots = words.shape[1]
        upper = (lax.broadcasted_iota(jnp.int32, (slots, TILE), 1) // step) % 2 == 1
        for c in range(words.shape[0]):
            if c & step == 0:
                low, high = words[c], words[c + step]
                words[c] = jnp.where(upper, pltpu.roll(high, step, 1), low)
                words[c + step] = jnp.where(upper, high, pltpu.roll(low, TILE - step, 1))

    def start_words():
        handed(landed, 1)
        for c in range(words.shape[0]):
            spread(c)

    def sort_slots():
        slots = rows_ref.shape[1]
        row_tiles = NY * BLOCK
        to, source = rows_ref[...].astype(jnp.float32), cols_ref[...].astype(jnp.float32)
        count = jnp.full((1, slots), count_ref[0], jnp.int32).astype(jnp.float32)
        slot = lax.broadcasted_iota(jnp.int32, (1, slots), 1).astype(jnp.float32)
        a = to - row_tiles * jnp.floor((to + 0.5) * (1.0 / row_tiles))
        b = BLOCK * jnp.floor((source + 0.5) * (1.0 / row_tiles)) + (
            source - BLOCK * jnp.floor((source + 0.5) * (1.0 / BLOCK))
        )
        a = jnp.where(slot < count, a, float(row_tiles))
        base = jnp.zeros_like(a)
        total = jnp.zeros((1, 1), jnp.float32)
        for tile in range(row_tiles):
            number = jnp.sum(jnp.where(a == tile, 1.0, 0.0), axis=1, keepdims=True)
            number = 2.0 * jnp.floor((number + 1.5) * 0.5)
            base += jnp.where(a > tile, number, 0.0)
            total += number
        across_lanes = jnp.broadcast_to(a, (slots, slots))
        down = jnp.transpose(across_lanes)
        earlier = lax.broadcasted_iota(jnp.int32, (slots, slots), 0) < lax.broadcasted_iota(
            jnp.int32, (slots, slots), 1
        )
        rank = jnp.sum(
            jnp.where((across_lanes == down) & earlier, 1.0, 0.0), axis=0, keepdims=True
        )
        at = jnp.where(a < row_tiles, base + rank, float(TABLE))
        at_down = jnp.transpose(jnp.broadcast_to(at, (TABLE, slots)))
        hit = at_down == lax.broadcasted_iota(jnp.int32, (slots, TABLE), 1).astype(jnp.float32)

        def pick(value):
            down = jnp.transpose(jnp.broadcast_to(value, (TABLE, slots)))
            return jnp.sum(jnp.where(hit, down, 0.0), axis=0, keepdims=True)

        sorted_slots[0:1, :] = (pick(slot + 1.0) - 1.0).astype(jnp.int32)
        sorted_slots[1:2, :] = pick(a).astype(jnp.int32)
        sorted_slots[2:3, :] = pick(b).astype(jnp.int32)
        sorted_slots[3:4, :] = jnp.broadcast_to(total * 0.5, (1, TABLE)).astype(jnp.int32)
        sorted_slots[4:8, :] = jnp.zeros((4, TABLE), jnp.int32)

    hand_over(own, gathered.at[rows(site, y_lo, 0, NODES)], 0)

    @pl.when(jnp.logical_not(home))
    def _():
        prepare()

    handed(gathered.at[rows(site, core, 0, NODES)], 0)
    for s in range(2):
        forward(site, FIRST, SECOND, ring_send.at[s], second_z.at[s, 0], z_to[s])
        forward(site, 0, FIRST, ring_send.at[2 + s], first_x.at[s], x_to[s])
    forward(site, 0, FIRST, ring_send.at[4], first_x.at[2], across)
    for s in range(2):
        forward(site, FIRST, SECOND, ring_send.at[2 + s], second_x.at[0, s, 0], x_to[s])
        forward(site, 0, FIRST, ring_send.at[s], first_z.at[s, 0, 0], z_to[s])

    @pl.when(home)
    def _():
        prepare()
        pltpu.make_async_copy(own_queries, queries.at[my_list], query_recv.at[my_list]).start()

    @pl.when(jnp.logical_not(home))
    def _():
        to_queries(0).start()

    for d in (1, 2, 3):
        to_queries(d).start()
    hand_over(bits, landed, 1)
    hand_over(sorted_slots, table, 2)

    X_OFF = (0, -1, 1, 2)
    Z_OFF = (0, -1, 1, -2, 2, -3, 3, 4)
    HALF1, HALF2 = FIRST // 2, SECOND // 2

    def second_z_step(t):
        for s in range(2):
            sign = -1 if s == 0 else 1
            if t < 4:
                a = site_of(sign * t, 0)
                arrived(a, FIRST, SECOND, second_z.at[s, t - 1])
                if t < 3:
                    forward(a, FIRST, SECOND, ring_send.at[s], second_z.at[s, t], z_to[s])
                else:
                    forward(a, FIRST + s * HALF2, HALF2, ring_send.at[s], second_z.at[s, 3], z_to[s])
                k = Z_OFF.index(sign * t)
                for e in range(2):
                    forward(a, FIRST, SECOND, ring_send.at[2 + e], second_x.at[k, e, 0], x_to[e])
        if t == 4:
            a = site_of(4, 0)
            for s in range(2):
                arrived(a, FIRST + s * HALF2, HALF2, second_z.at[s, 3])
            for e in range(2):
                forward(a, FIRST, SECOND, ring_send.at[2 + e], second_x.at[7, e, 0], x_to[e])

    def first_x_step(*which):
        for k in which:
            a = site_of(0, X_OFF[k + 1])
            arrived(a, 0, FIRST, first_x.at[k])
            for s in range(2):
                forward(a, 0, FIRST, ring_send.at[s], first_z.at[s, 0, k + 1], z_to[s])

    def first_z_step(t, k):
        if t < 4:
            for s in range(2):
                sign = -1 if s == 0 else 1
                a = site_of(sign * t, X_OFF[k])
                arrived(a, 0, FIRST, first_z.at[s, t - 1, k])
                if t < 3:
                    forward(a, 0, FIRST, ring_send.at[s], first_z.at[s, t, k], z_to[s])
                else:
                    forward(a, s * HALF1, HALF1, ring_send.at[s], first_z.at[s, 3, k], z_to[s])
        else:
            a = site_of(4, X_OFF[k])
            for s in range(2):
                arrived(a, s * HALF1, HALF1, first_z.at[s, 3, k])

    def second_x_step(k):
        for e in range(2):
            sign = -1 if e == 0 else 1
            a = site_of(Z_OFF[k], sign)
            arrived(a, FIRST, SECOND, second_x.at[k, e, 0])
            forward(a, FIRST + e * HALF2, HALF2, ring_send.at[2 + e], second_x.at[k, e, 1], x_to[e])

    def second_x_end(k):
        a = site_of(Z_OFF[k], 2)
        for e in range(2):
            arrived(a, FIRST + e * HALF2, HALF2, second_x.at[k, e, 1])

    def project(dz, k):
        a = site_of(dz, X_OFF[k])
        start = pl.multiple_of((a * 2 + core) * NODES, NODES)
        tile = (a * 2 + core) * BLOCK
        forward(a, 0, NODES, sibling_send.at[0], sibling_recv.at[0], other)
        v = lax.dot_general(
            wv[...], gathered[pl.ds(start, NODES), :], NT, preferred_element_type=jnp.float32
        ).astype(jnp.bfloat16)
        for t in range(BLOCK):
            values[tile + t] = v[:, t * TILE : (t + 1) * TILE]
        done = values.at[pl.ds(tile, BLOCK)]
        remote(done, done, sibling_send.at[1], sibling_recv.at[1], other)

    def drain(count, sem):
        pltpu.make_async_copy(gathered.at[pl.ds(0, count)], gathered.at[pl.ds(0, count)], sem).wait()

    order = [
        (second_z_step, 1), (fold, 0, 0), (fold, 0, 1), (fold, 0, 2), (first_z_step, 1, 0), (first_x_step, 2),
        (second_x_step, 0), (first_x_step, 0, 1), (second_z_step, 2), (start_words,), (fold, 1, 0),
        (swap_bit, 0), (project, 0, 0), (project, 0, 1), (first_z_step, 2, 0), (first_z_step, 1, 1),
        (first_z_step, 1, 2), (second_x_step, 1), (project, -1, 1), (fold, 1, 1), (second_x_step, 2),
        (project, -2, 0), (fold, 1, 2), (project, 1, 2), (second_x_step, 4), (fold, 2, 0), (second_z_step, 3),
        (project, 1, 0), (fold, 2, 1), (first_z_step, 1, 3), (swap_bit, 1), (swap_bit, 2), (second_x_end, 2),
        (first_z_step, 3, 0), (second_x_end, 1), (project, 2, 0), (second_x_end, 0), (first_z_step, 2, 1),
        (project, -3, 0), (project, 1, 3), (fold, 2, 2), (fold, 3, 0), (first_z_step, 2, 2),
        (second_z_step, 4), (project, 2, 1), (second_x_end, 4), (project, 0, 2), (project, 1, 1),
        (second_x_step, 3), (project, 3, 0), (swap_bit, 3), (first_z_step, 2, 3), (first_z_step, 4, 0),
        (project, 4, 0), (project, 2, 2), (fold, 3, 1), (fold, 3, 2), (second_x_step, 6), (project, 0, 3),
        (project, -1, 2), (first_z_step, 3, 1), (project, -2, 2), (project, -1, 3), (second_x_step, 5),
        (first_z_step, 3, 2), (project, 3, 1), (project, -3, 2), (project, 2, 3), (project, -2, 1),
        (second_x_end, 3), (second_x_step, 7), (first_z_step, 3, 3), (project, -3, 1), (project, -2, 3),
        (second_x_end, 6), (project, 3, 3), (first_z_step, 4, 1), (first_z_step, 4, 2), (project, -1, 0),
        (second_x_end, 5), (project, 4, 2), (project, 3, 2), (project, 4, 1), (project, -3, 3),
        (first_z_step, 4, 3), (second_x_end, 7), (project, 4, 3),
    ]
    for step in order:
        step[0](*step[1:])

    half_values = values.at[pl.ds(0, SITES * BLOCK)]
    pltpu.make_async_copy(half_values, half_values, sibling_recv.at[1]).wait()
    pltpu.make_async_copy(half_values, half_values, sibling_send.at[1]).wait()
    drain(SITES * NODES, sibling_recv.at[0])
    drain(SITES * NODES, sibling_send.at[0])
    z_rows = 3 * SECOND + HALF2 + NX * (3 * FIRST + HALF1)
    x_rows = FIRST + NZ * (SECOND + HALF2)
    for s in range(2):
        drain(z_rows, ring_send.at[s])
        drain(x_rows, ring_send.at[2 + s])
    drain(FIRST, ring_send.at[4])
    for d in range(1, NY):
        to_queries(d).wait_send()
    handed(table, 2)

    @pl.when(jnp.logical_not(home))
    def _():
        to_queries(0).wait_send()
        to_partner(own, gathered.at[rows(site, y_lo, 0, NODES)], 0).wait_send()
        to_partner(bits, landed, 1).wait_send()
        to_partner(sorted_slots, table, 2).wait_send()


def exchange(features, masks, tile_rows, tile_cols, tile_count, weights):
    slots, length = masks.shape
    vmem = pl.BlockSpec(memory_space=pltpu.VMEM)
    smem = pl.BlockSpec(memory_space=pltpu.SMEM)
    dma = pltpu.SemaphoreType.DMA
    half = jnp.bfloat16
    return pl.pallas_call(
        exchange_kernel,
        out_shape=(
            jax.ShapeDtypeStruct((SITES * 2 * NODES, D), half),
            jax.ShapeDtypeStruct((SITES * 2 * BLOCK, D, TILE), half),
            jax.ShapeDtypeStruct((NY * BLOCK, D, HEADS * TILE), half),
            jax.ShapeDtypeStruct((length // TILE, slots, TILE), jnp.int32),
            jax.ShapeDtypeStruct((8, TABLE), jnp.int32),
        ),
        in_specs=[vmem, vmem, vmem, vmem, smem, vmem],
        out_specs=(vmem,) * 5,
        scratch_shapes=[
            pltpu.VMEM((NY, BLOCK, D, TILE), half),
            pltpu.VMEM((NODES, D), half),
            pltpu.VMEM((BLOCK, D, TILE), half),
            pltpu.VMEM((D, D), half),
            pltpu.VMEM((D, D), half),
            pltpu.VMEM((slots, length), half),
            pltpu.VMEM((slots, length), half),
            pltpu.VMEM((8, TABLE), jnp.int32),
            pltpu.VMEM((D, HEADS * TILE), half),
            dma((NY,)), dma((NY,)), dma((3,)), dma((3,)),
            dma((5,)), dma((3,)), dma((2, 4, NX)), dma((2, 4)), dma((NZ, 2, 2)), dma((2,)), dma((2,)),
        ],
        compiler_params=pltpu.CompilerParams(
            collective_id=0, has_side_effects=True, vmem_limit_bytes=16 * 1024 * 1024
        ),
        name="exchange",
    )(features, masks, tile_rows, tile_cols, tile_count, weights)


def attention_kernel(
    table_ref, bias_ref, gathered, values, stationary, words,
    num_ref, den_ref, num_acc, den_acc, even_scores, odd_scores, even_weights, odd_weights,
):
    pairs = table_ref[3, 0]
    num_acc[...] = jnp.zeros_like(num_acc)
    den_acc[...] = jnp.zeros_like(den_acc)
    odd_weights[...] = jnp.zeros_like(odd_weights)
    bit_of = jnp.left_shift(jnp.int32(1), lax.broadcasted_iota(jnp.int32, (8, TILE), 0))
    half_bias = [bias_ref[h] * 0.5 for h in range(HEADS)]
    ones = jnp.ones((STRIP, 2 * TILE), jnp.bfloat16)

    def score(p, scores):
        a = table_ref[1, 2 * p]
        sources = jnp.concatenate(
            [
                gathered[pl.ds(pl.multiple_of(table_ref[2, 2 * p + u] * TILE, TILE), TILE), :]
                for u in range(2)
            ],
            axis=0,
        )

        def part(half):
            lanes = slice(half * 2 * TILE, (half + 1) * 2 * TILE)
            scores[:, lanes] = jnp.dot(
                sources, stationary[a, :, lanes], preferred_element_type=jnp.float32
            )

        return [functools.partial(part, half) for half in range(2)]

    def weigh(p, scores, weights):
        def part(u, groups):
            s = table_ref[0, 2 * p + u]
            live = jnp.where(s >= 0, bit_of, 0)
            s = jnp.maximum(s, 0)
            for g in groups:
                edge = [
                    jnp.where(
                        (jnp.broadcast_to(words[w, pl.ds(s, 1), :], (8, TILE)) & live) != 0, 1.0, 0.0
                    )
                    for w in (2 * g, 2 * g + 1)
                ]
                edge = jnp.concatenate(edge, axis=0).astype(jnp.bfloat16)
                here = slice(u * TILE + g * STRIP, u * TILE + (g + 1) * STRIP)
                for h in range(HEADS):
                    lanes = slice(h * TILE, (h + 1) * TILE)
                    twice = jnp.tanh(scores[here, lanes] + half_bias[h]) + 1.0
                    weights[here, lanes] = twice.astype(jnp.bfloat16) * edge

        half = TILE // STRIP // 2
        return [
            functools.partial(part, u, range(v * half, (v + 1) * half))
            for u in range(2) for v in range(2)
        ]

    def mix(p, weights):
        a = table_ref[1, 2 * p]
        source = [table_ref[2, 2 * p + u] for u in range(2)]

        def part(half):
            rows = slice(half * TILE, (half + 1) * TILE)
            v = jnp.concatenate([values[b, rows, :] for b in source], axis=1)
            v = jnp.concatenate([v, ones], axis=0)
            both = jnp.dot(
                v, weights[:, half * 2 * TILE : (half + 1) * 2 * TILE],
                preferred_element_type=jnp.float32,
            )
            for side in range(2):
                start = half * TILE + side * HEAD
                num_acc[a, start : start + HEAD, :] += both[
                    side * HEAD : (side + 1) * HEAD, side * TILE : (side + 1) * TILE
                ]
            den_acc[a, half] += both[TILE : TILE + 8]

        return [functools.partial(part, half) for half in range(2)]

    def together(scored, mixed, weighed):
        for k in range(2):
            scored[k]()
            mixed[k]()
        for part in weighed:
            part()

    for part in score(0, even_scores):
        part()

    def turn(t, _):
        for u in range(0, UNROLL, 2):
            p = UNROLL * t + u
            together(
                score(p + 1, odd_scores), mix(jnp.maximum(p - 1, 0), odd_weights),
                weigh(p, even_scores, even_weights),
            )
            together(
                score(p + 2, even_scores), mix(p, even_weights),
                weigh(p + 1, odd_scores, odd_weights),
            )
        return 0

    turns = (pairs + UNROLL - 1) // UNROLL
    lax.fori_loop(0, turns, turn, 0)
    for part in mix(jnp.maximum(UNROLL * turns - 1, 0), odd_weights):
        part()
    num_ref[...] = (num_acc[...] * 0.5).astype(num_ref.dtype)
    for a in range(den_acc.shape[0]):
        for h in range(HEADS):
            lanes = slice(h % 2 * TILE, (h % 2 + 1) * TILE)
            den_ref[a, h : h + 1, :] = den_acc[a, h // 2, 0:1, lanes] * 0.5


def attention(table, bias, gathered, values, stationary, words):
    row_tiles = stationary.shape[0]
    smem = pl.BlockSpec(memory_space=pltpu.SMEM)
    vmem = pl.BlockSpec(memory_space=pltpu.VMEM)
    return pl.pallas_call(
        attention_kernel,
        out_shape=(
            jax.ShapeDtypeStruct((row_tiles, D, TILE), jnp.bfloat16),
            jax.ShapeDtypeStruct((row_tiles, HEADS, TILE), jnp.float32),
        ),
        in_specs=[smem] * 2 + [vmem] * 4,
        out_specs=(vmem, vmem),
        scratch_shapes=[
            pltpu.VMEM((row_tiles, D, TILE), jnp.float32),
            pltpu.VMEM((row_tiles, 2, 8, 2 * TILE), jnp.float32),
            pltpu.VMEM((2 * TILE, HEADS * TILE), jnp.float32),
            pltpu.VMEM((2 * TILE, HEADS * TILE), jnp.float32),
            pltpu.VMEM((2 * TILE, HEADS * TILE), jnp.bfloat16),
            pltpu.VMEM((2 * TILE, HEADS * TILE), jnp.bfloat16),
        ],
        compiler_params=pltpu.CompilerParams(vmem_limit_bytes=16 * 1024 * 1024),
        name="attention",
    )(table, bias, gathered, values, stationary, words)


def finish_kernel(
    features_ref, num_ref, den_ref, w_ref, gain_ref, out_ref,
    nums, dens, send, recv,
):
    z, x, y, core = position()
    y_lo = y % 2
    meet(site_partners(z, x, y, core))
    home = y_lo == core

    def part(d, src, dst, k):
        c = (y + d) % NY
        return pltpu.make_async_remote_copy(
            src_ref=src.at[c], dst_ref=dst.at[y], send_sem=send.at[k, d], recv_sem=recv.at[k, y],
            device_id=device(z, x, c // 2 * 2 + core, c % 2), device_id_type=MESH,
        )

    pairs = ((num_ref, nums), (den_ref, dens))
    for d in (1, 2, 3):
        for k, (src, dst) in enumerate(pairs):
            part(d, src, dst, k).start()
    for k, (src, dst) in enumerate(pairs):
        @pl.when(home)
        def _():
            pltpu.make_async_copy(src.at[y], dst.at[y], recv.at[k, y]).start()

        @pl.when(jnp.logical_not(home))
        def _():
            part(0, src, dst, k).start()

    for c in range(NY):
        for k, (src, dst) in enumerate(pairs):
            pltpu.make_async_copy(dst.at[c], dst.at[c], recv.at[k, c]).wait()
    total = sum(nums[c].astype(jnp.float32) for c in range(NY))
    weight = 1.0 + sum(dens[c] for c in range(NY))
    gain = gain_ref[...]
    node, lane_node = lane_order()
    to_nodes = jnp.transpose(jnp.where(node == lane_node, 1.0, 0.0)).astype(jnp.bfloat16)
    for t in range(NODES // TILE):
        mixed = total[t].reshape(HEADS, HEAD, TILE) / weight[t].reshape(HEADS, 1, TILE)
        mixed = mixed.reshape(D, TILE).astype(jnp.bfloat16)
        mixed = jnp.dot(mixed, to_nodes, preferred_element_type=jnp.float32).astype(jnp.bfloat16)
        projected = lax.dot_general(
            mixed, w_ref[...], (((0,), (0,)), ((), ())), preferred_element_type=jnp.float32
        )
        square = jnp.mean(projected * projected, axis=1, keepdims=True)
        here = pl.ds(t * TILE, TILE)
        out_ref[here, :] = features_ref[here, :] + gain * projected * lax.rsqrt(square + 1e-05)
    for d in range(NY):
        for k, (src, dst) in enumerate(pairs):
            if d:
                part(d, src, dst, k).wait_send()
            else:
                @pl.when(jnp.logical_not(home))
                def _():
                    part(d, src, dst, k).wait_send()


def finish(features, numerator, denominator, w_out, gain):
    vmem = pl.BlockSpec(memory_space=pltpu.VMEM)
    hbm = pl.BlockSpec(memory_space=pl.ANY)
    dma = pltpu.SemaphoreType.DMA
    return pl.pallas_call(
        finish_kernel,
        out_shape=jax.ShapeDtypeStruct(features.shape, jnp.float32),
        in_specs=[vmem, hbm, hbm, vmem, vmem],
        out_specs=vmem,
        scratch_shapes=[
            pltpu.VMEM(numerator.shape, numerator.dtype),
            pltpu.VMEM(denominator.shape, denominator.dtype),
            dma((2, NY)), dma((2, NY)),
        ],
        compiler_params=pltpu.CompilerParams(
            collective_id=1, has_side_effects=True, vmem_limit_bytes=32 * 1024 * 1024
        ),
        name="finish",
    )(features, numerator, denominator, w_out, gain)


def local(
    features, w_qkv, w_out, head_bias, out_gain, tile_rows, tile_cols, tile_masks, tile_count
):
    block_tiles = features.shape[0] // TILE
    gathered, values, stationary, words, table = exchange(
        features, tile_masks[0], tile_rows, tile_cols, tile_count, w_qkv
    )
    numerator, denominator = attention(
        table, head_bias, gathered, values, stationary, words
    )
    return finish(
        features,
        numerator.reshape(NY, block_tiles, D, TILE),
        denominator.reshape(NY, block_tiles, HEADS, TILE),
        w_out, out_gain[None, :],
    )


def solution(mesh):
    placed = (
        P(("row", "col"), None),
        P(),
        P(),
        P(),
        P(),
        P(("row", "col"), None),
        P(("row", "col"), None),
        P(("row", "col"), None, None),
        P(("row", "col")),
    )
    return jax.shard_map(
        local, mesh=mesh, in_specs=placed, out_specs=P(("row", "col"), None), check_vma=False
    )
```

```python
import functools

import jax
import jax.numpy as jnp
from jax import lax
from jax.experimental import pallas as pl
from jax.experimental.pallas import tpu as pltpu
from jax.sharding import PartitionSpec as P

TILE = 128
HEADS = 4
HEAD = 64
D = 256
STRIP = 16
UNROLL = 12
TABLE = 384
NX, NY, NZ = 4, 4, 8
SITES = NX * NZ
NODES = 384
FIRST = 160
SECOND = NODES - FIRST
BLOCK = NODES // TILE
MESH = pl.DeviceIdType.MESH
NT = (((1,), (1,)), ((), ()))


def position():
    row, col = lax.axis_index("row"), lax.axis_index("col")
    return row // 8, row // 2 % 4, col // 2 * 2 + row % 2, col % 2


def device(z, x, y, core):
    return ((z * NX + x) * 2 + y % 2, y // 2 * 2 + core)


def meet(partners, meanwhile=None):
    barrier = pltpu.get_barrier_semaphore()
    for partner in partners:
        pl.semaphore_signal(barrier, inc=1, device_id=partner, device_id_type=MESH)
    if meanwhile is not None:
        meanwhile()
    pl.semaphore_wait(barrier, len(partners))


def site_partners(z, x, y, core):
    found = [device(z, x, y, 1 - core)]
    for d in range(1, NY):
        found += [device(z, x, (y + d) % NY, core), device(z, x, (y + d) % NY, 1 - core)]
    return found


def lane_order():
    node = lax.broadcasted_iota(jnp.int32, (TILE, TILE), 0)
    lane = lax.broadcasted_iota(jnp.int32, (TILE, TILE), 1)
    return node, lane % 16 * 8 + lane // 16


def exchange_kernel(
    features_ref, masks_ref, lists_ref, count_ref, weights_ref,
    gathered, values, stationary, words, table,
    queries, own, own_queries, wq, wv, bits, landed, sorted_slots, diagonal,
    query_send, query_recv, list_send, list_recv,
    ring_send, first_x, first_z, second_z, second_x, sibling_send, sibling_recv,
):
    z, x, y, core = position()
    y_lo, y_hi = y % 2, y // 2
    site = z * NX + x

    def setup():
        own[...] = features_ref[...].astype(jnp.bfloat16)
        wq[...] = jnp.transpose(weights_ref[:, 0:D])
        wv[...] = jnp.transpose(weights_ref[:, 2 * D : 3 * D])
        bits[...] = masks_ref[...].astype(jnp.float32).astype(jnp.bfloat16)
        diagonal[...] = jnp.zeros_like(diagonal)

    meet(
        site_partners(z, x, y, core)
        + [device(z, (x + d) % NX, y, core) for d in (1, 2, 3)]
        + [device((z + d) % NZ, x, y, core) for d in (1, 7)],
        setup,
    )

    my_list = y_hi * 2 + core
    home = y_lo == core
    partner = device(z, x, y_hi * 2 + core, y_lo)

    def to_partner(src, dst, k):
        return pltpu.make_async_remote_copy(
            src_ref=src, dst_ref=dst, send_sem=list_send.at[k], recv_sem=list_recv.at[k],
            device_id=partner, device_id_type=MESH,
        )

    def hand_over(src, dst, k):
        @pl.when(home)
        def _():
            pltpu.make_async_copy(src, dst, list_recv.at[k]).start()

        @pl.when(jnp.logical_not(home))
        def _():
            to_partner(src, dst, k).start()

    def handed(ref, k):
        pltpu.make_async_copy(ref, ref, list_recv.at[k]).wait()

    def rows(a_site, parity, low, count):
        return pl.ds(pl.multiple_of((a_site * 2 + parity) * NODES + low, 16), count)

    def remote(src, dst, send, recv, target):
        pltpu.make_async_remote_copy(
            src_ref=src, dst_ref=dst, send_sem=send, recv_sem=recv,
            device_id=target, device_id_type=MESH,
        ).start()

    def arrived(a_site, low, count, sem):
        here = gathered.at[rows(a_site, core, low, count)]
        pltpu.make_async_copy(here, here, sem).wait()

    def forward(a_site, low, count, send, recv, target):
        here = gathered.at[rows(a_site, core, low, count)]
        remote(here, here, send, recv, target)

    up, down = device((z + 1) % NZ, x, y, core), device((z + 7) % NZ, x, y, core)
    right, left = device(z, (x + 1) % NX, y, core), device(z, (x + 3) % NX, y, core)
    across = device(z, (x + 2) % NX, y, core)
    other = device(z, x, y, 1 - core)
    z_to, x_to = (up, down), (right, left)

    def site_of(dz, dx):
        return (z + dz + NZ) % NZ * NX + (x + dx + NX) % NX

    def to_queries(d):
        return pltpu.make_async_remote_copy(
            src_ref=own_queries, dst_ref=queries.at[my_list],
            send_sem=query_send.at[d], recv_sem=query_recv.at[my_list],
            device_id=device(z, x, (y_hi * 2 + core + d) % NY, y_lo), device_id_type=MESH,
        )

    def prepare():
        node, lane_node = lane_order()
        to_lanes = jnp.where(node == lane_node, 1.0, 0.0).astype(jnp.bfloat16)
        q = lax.dot_general(wq[...], own[...], NT, preferred_element_type=jnp.float32)
        q = q.astype(jnp.bfloat16) * jnp.bfloat16(0.0625)
        for t in range(BLOCK):
            own_queries[t] = jnp.dot(
                q[:, t * TILE : (t + 1) * TILE], to_lanes, preferred_element_type=jnp.float32
            ).astype(jnp.bfloat16)
        sort_slots()

    def fold(c, t):
        if t == 0:
            pltpu.make_async_copy(queries.at[c], queries.at[c], query_recv.at[c]).wait()
        for h in range(HEADS):
            diagonal[h * HEAD : (h + 1) * HEAD, h * TILE : (h + 1) * TILE] = (
                queries[c, t, h * HEAD : (h + 1) * HEAD, :]
            )
        stationary[c * BLOCK + t] = jnp.dot(
            weights_ref[:, D : 2 * D], diagonal[...], preferred_element_type=jnp.float32
        ).astype(jnp.bfloat16)

    def spread(c):
        words[c] = landed[:, c * TILE : (c + 1) * TILE].astype(jnp.float32).astype(jnp.int32)

    def swap_bit(b):
        step = 1 << b
        slots = words.shape[1]
        upper = (lax.broadcasted_iota(jnp.int32, (slots, TILE), 1) // step) % 2 == 1
        for c in range(words.shape[0]):
            if c & step == 0:
                low, high = words[c], words[c + step]
                words[c] = jnp.where(upper, pltpu.roll(high, step, 1), low)
                words[c + step] = jnp.where(upper, high, pltpu.roll(low, TILE - step, 1))

    def start_words():
        handed(landed, 1)
        for c in range(words.shape[0]):
            spread(c)

    def sort_slots():
        slots = lists_ref.shape[1]
        row_tiles = NY * BLOCK
        to, source = (lists_ref[k : k + 1, :].astype(jnp.float32) for k in range(2))
        count = jnp.full((1, slots), count_ref[0], jnp.int32).astype(jnp.float32)
        slot = lax.broadcasted_iota(jnp.int32, (1, slots), 1).astype(jnp.float32)
        a = to - row_tiles * jnp.floor((to + 0.5) * (1.0 / row_tiles))
        b = BLOCK * jnp.floor((source + 0.5) * (1.0 / row_tiles)) + (
            source - BLOCK * jnp.floor((source + 0.5) * (1.0 / BLOCK))
        )
        a = jnp.where(slot < count, a, float(row_tiles))
        base = jnp.zeros_like(a)
        total = jnp.zeros((1, 1), jnp.float32)
        for tile in range(row_tiles):
            number = jnp.sum(jnp.where(a == tile, 1.0, 0.0), axis=1, keepdims=True)
            number = 2.0 * jnp.floor((number + 1.5) * 0.5)
            base += jnp.where(a > tile, number, 0.0)
            total += number
        across_lanes = jnp.broadcast_to(a, (slots, slots))
        down = jnp.transpose(across_lanes)
        earlier = lax.broadcasted_iota(jnp.int32, (slots, slots), 0) < lax.broadcasted_iota(
            jnp.int32, (slots, slots), 1
        )
        rank = jnp.sum(
            jnp.where((across_lanes == down) & earlier, 1.0, 0.0), axis=0, keepdims=True
        )
        at = jnp.where(a < row_tiles, base + rank, float(TABLE))
        at_down = jnp.transpose(jnp.broadcast_to(at, (TABLE, slots)))
        hit = at_down == lax.broadcasted_iota(jnp.int32, (slots, TABLE), 1).astype(jnp.float32)

        def pick(value):
            down = jnp.transpose(jnp.broadcast_to(value, (TABLE, slots)))
            return jnp.sum(jnp.where(hit, down, 0.0), axis=0, keepdims=True)

        sorted_slots[0:1, :] = (pick(slot + 1.0) - 1.0).astype(jnp.int32)
        sorted_slots[1:2, :] = pick(a).astype(jnp.int32)
        sorted_slots[2:3, :] = pick(b).astype(jnp.int32)
        sorted_slots[3:4, :] = jnp.broadcast_to(total * 0.5, (1, TABLE)).astype(jnp.int32)
        sorted_slots[4:8, :] = jnp.zeros((4, TABLE), jnp.int32)

    hand_over(own, gathered.at[rows(site, y_lo, 0, NODES)], 0)

    @pl.when(jnp.logical_not(home))
    def _():
        prepare()

    handed(gathered.at[rows(site, core, 0, NODES)], 0)
    for s in range(2):
        forward(site, FIRST, SECOND, ring_send.at[s], second_z.at[s, 0], z_to[s])
        forward(site, 0, FIRST, ring_send.at[2 + s], first_x.at[s], x_to[s])
    forward(site, 0, FIRST, ring_send.at[4], first_x.at[2], across)
    for s in range(2):
        forward(site, FIRST, SECOND, ring_send.at[2 + s], second_x.at[0, s, 0], x_to[s])
        forward(site, 0, FIRST, ring_send.at[s], first_z.at[s, 0, 0], z_to[s])

    @pl.when(home)
    def _():
        prepare()
        pltpu.make_async_copy(own_queries, queries.at[my_list], query_recv.at[my_list]).start()

    @pl.when(jnp.logical_not(home))
    def _():
        to_queries(0).start()

    for d in (1, 2, 3):
        to_queries(d).start()
    hand_over(bits, landed, 1)
    hand_over(sorted_slots, table, 2)

    X_OFF = (0, -1, 1, 2)
    Z_OFF = (0, -1, 1, -2, 2, -3, 3, 4)
    HALF1, HALF2 = FIRST // 2, SECOND // 2

    def second_z_step(t):
        for s in range(2):
            sign = -1 if s == 0 else 1
            if t < 4:
                a = site_of(sign * t, 0)
                arrived(a, FIRST, SECOND, second_z.at[s, t - 1])
                if t < 3:
                    forward(a, FIRST, SECOND, ring_send.at[s], second_z.at[s, t], z_to[s])
                else:
                    forward(a, FIRST + s * HALF2, HALF2, ring_send.at[s], second_z.at[s, 3], z_to[s])
                k = Z_OFF.index(sign * t)
                for e in range(2):
                    forward(a, FIRST, SECOND, ring_send.at[2 + e], second_x.at[k, e, 0], x_to[e])
        if t == 4:
            a = site_of(4, 0)
            for s in range(2):
                arrived(a, FIRST + s * HALF2, HALF2, second_z.at[s, 3])
            for e in range(2):
                forward(a, FIRST, SECOND, ring_send.at[2 + e], second_x.at[7, e, 0], x_to[e])

    def first_x_step(*which):
        for k in which:
            a = site_of(0, X_OFF[k + 1])
            arrived(a, 0, FIRST, first_x.at[k])
            for s in range(2):
                forward(a, 0, FIRST, ring_send.at[s], first_z.at[s, 0, k + 1], z_to[s])

    def first_z_step(t, k):
        if t < 4:
            for s in range(2):
                sign = -1 if s == 0 else 1
                a = site_of(sign * t, X_OFF[k])
                arrived(a, 0, FIRST, first_z.at[s, t - 1, k])
                if t < 3:
                    forward(a, 0, FIRST, ring_send.at[s], first_z.at[s, t, k], z_to[s])
                else:
                    forward(a, s * HALF1, HALF1, ring_send.at[s], first_z.at[s, 3, k], z_to[s])
        else:
            a = site_of(4, X_OFF[k])
            for s in range(2):
                arrived(a, s * HALF1, HALF1, first_z.at[s, 3, k])

    def second_x_step(k):
        for e in range(2):
            sign = -1 if e == 0 else 1
            a = site_of(Z_OFF[k], sign)
            arrived(a, FIRST, SECOND, second_x.at[k, e, 0])
            forward(a, FIRST + e * HALF2, HALF2, ring_send.at[2 + e], second_x.at[k, e, 1], x_to[e])

    def second_x_end(k):
        a = site_of(Z_OFF[k], 2)
        for e in range(2):
            arrived(a, FIRST + e * HALF2, HALF2, second_x.at[k, e, 1])

    def project(dz, k):
        a = site_of(dz, X_OFF[k])
        start = pl.multiple_of((a * 2 + core) * NODES, NODES)
        tile = (a * 2 + core) * BLOCK
        forward(a, 0, NODES, sibling_send.at[0], sibling_recv.at[0], other)
        v = lax.dot_general(
            wv[...], gathered[pl.ds(start, NODES), :], NT, preferred_element_type=jnp.float32
        ).astype(jnp.bfloat16)
        for t in range(BLOCK):
            values[tile + t] = v[:, t * TILE : (t + 1) * TILE]
        done = values.at[pl.ds(tile, BLOCK)]
        remote(done, done, sibling_send.at[1], sibling_recv.at[1], other)

    def drain(count, sem):
        pltpu.make_async_copy(gathered.at[pl.ds(0, count)], gathered.at[pl.ds(0, count)], sem).wait()

    order = [
        (project, 0, 0), (second_z_step, 1), (first_x_step, 0, 1), (second_z_step, 2), (second_x_step, 0),
        (fold, 0, 0), (fold, 0, 1), (first_z_step, 1, 0), (first_z_step, 1, 1), (project, 1, 0), (fold, 0, 2),
        (first_x_step, 2), (second_x_step, 1), (second_x_step, 2), (fold, 1, 0), (project, 0, 1),
        (fold, 1, 1), (fold, 1, 2), (fold, 2, 0), (second_z_step, 3), (fold, 2, 1), (fold, 2, 2),
        (project, 0, 2), (first_z_step, 1, 2), (project, -1, 1), (fold, 3, 0), (first_z_step, 1, 3),
        (second_x_step, 3), (first_z_step, 2, 0), (project, -2, 0), (second_x_end, 0), (start_words,),
        (swap_bit, 0), (swap_bit, 1), (first_z_step, 2, 2), (second_x_end, 1), (second_z_step, 4),
        (project, 1, 1), (swap_bit, 2), (first_z_step, 2, 1), (project, 2, 0), (fold, 3, 1),
        (second_x_step, 4), (project, 0, 3), (project, 1, 2), (first_z_step, 2, 3), (swap_bit, 3),
        (project, -1, 3), (second_x_step, 6), (project, -1, 0), (project, -1, 2), (project, 2, 1),
        (project, -2, 2), (first_z_step, 3, 0), (second_x_step, 5), (second_x_end, 3), (project, 3, 0),
        (project, -2, 1), (first_z_step, 3, 2), (project, -3, 0), (first_z_step, 3, 1), (project, -2, 3),
        (project, 2, 2), (second_x_step, 7), (project, 3, 2), (second_x_end, 2), (second_x_end, 4),
        (first_z_step, 3, 3), (project, -3, 2), (project, 2, 3), (second_x_end, 6), (project, 3, 1),
        (fold, 3, 2), (first_z_step, 4, 0), (project, -3, 1), (project, 1, 3), (second_x_end, 5),
        (project, -3, 3), (project, 4, 0), (project, 3, 3), (first_z_step, 4, 2), (first_z_step, 4, 1),
        (project, 4, 1), (project, 4, 2), (second_x_end, 7), (first_z_step, 4, 3), (project, 4, 3),
    ]
    for step in order:
        step[0](*step[1:])

    half_values = values.at[pl.ds(0, SITES * BLOCK)]
    pltpu.make_async_copy(half_values, half_values, sibling_recv.at[1]).wait()
    pltpu.make_async_copy(half_values, half_values, sibling_send.at[1]).wait()
    drain(SITES * NODES, sibling_recv.at[0])
    drain(SITES * NODES, sibling_send.at[0])
    z_rows = 3 * SECOND + HALF2 + NX * (3 * FIRST + HALF1)
    x_rows = FIRST + NZ * (SECOND + HALF2)
    for s in range(2):
        drain(z_rows, ring_send.at[s])
        drain(x_rows, ring_send.at[2 + s])
    drain(FIRST, ring_send.at[4])
    for d in range(1, NY):
        to_queries(d).wait_send()
    handed(table, 2)

    @pl.when(jnp.logical_not(home))
    def _():
        to_queries(0).wait_send()
        to_partner(own, gathered.at[rows(site, y_lo, 0, NODES)], 0).wait_send()
        to_partner(bits, landed, 1).wait_send()
        to_partner(sorted_slots, table, 2).wait_send()


def exchange(features, masks, lists, tile_count, weights):
    slots, length = masks.shape
    vmem = pl.BlockSpec(memory_space=pltpu.VMEM)
    smem = pl.BlockSpec(memory_space=pltpu.SMEM)
    dma = pltpu.SemaphoreType.DMA
    half = jnp.bfloat16
    return pl.pallas_call(
        exchange_kernel,
        out_shape=(
            jax.ShapeDtypeStruct((SITES * 2 * NODES, D), half),
            jax.ShapeDtypeStruct((SITES * 2 * BLOCK, D, TILE), half),
            jax.ShapeDtypeStruct((NY * BLOCK, D, HEADS * TILE), half),
            jax.ShapeDtypeStruct((length // TILE, slots, TILE), jnp.int32),
            jax.ShapeDtypeStruct((8, TABLE), jnp.int32),
        ),
        in_specs=[vmem, vmem, vmem, smem, vmem],
        out_specs=(vmem,) * 5,
        scratch_shapes=[
            pltpu.VMEM((NY, BLOCK, D, TILE), half),
            pltpu.VMEM((NODES, D), half),
            pltpu.VMEM((BLOCK, D, TILE), half),
            pltpu.VMEM((D, D), half),
            pltpu.VMEM((D, D), half),
            pltpu.VMEM((slots, length), half),
            pltpu.VMEM((slots, length), half),
            pltpu.VMEM((8, TABLE), jnp.int32),
            pltpu.VMEM((D, HEADS * TILE), half),
            dma((NY,)), dma((NY,)), dma((3,)), dma((3,)),
            dma((5,)), dma((3,)), dma((2, 4, NX)), dma((2, 4)), dma((NZ, 2, 2)), dma((2,)), dma((2,)),
        ],
        compiler_params=pltpu.CompilerParams(
            collective_id=0, has_side_effects=True, vmem_limit_bytes=16 * 1024 * 1024
        ),
        name="exchange",
    )(features, masks, lists, tile_count, weights)


def attention_kernel(
    table_ref, bias_ref, gathered, values, stationary, words,
    num_ref, den_ref, num_acc, den_acc, even_scores, odd_scores, even_weights, odd_weights,
):
    pairs = table_ref[3, 0]
    num_acc[...] = jnp.zeros_like(num_acc)
    den_acc[...] = jnp.zeros_like(den_acc)
    odd_weights[...] = jnp.zeros_like(odd_weights)
    bit_of = jnp.left_shift(jnp.int32(1), lax.broadcasted_iota(jnp.int32, (8, TILE), 0))
    half_bias = [bias_ref[h] * 0.5 for h in range(HEADS)]
    ones = jnp.ones((STRIP, 2 * TILE), jnp.bfloat16)

    def score(p, scores):
        a = table_ref[1, 2 * p]
        sources = jnp.concatenate(
            [
                gathered[pl.ds(pl.multiple_of(table_ref[2, 2 * p + u] * TILE, TILE), TILE), :]
                for u in range(2)
            ],
            axis=0,
        )

        def part(half):
            lanes = slice(half * 2 * TILE, (half + 1) * 2 * TILE)
            scores[:, lanes] = jnp.dot(
                sources, stationary[a, :, lanes], preferred_element_type=jnp.float32
            )

        return [functools.partial(part, half) for half in range(2)]

    def weigh(p, scores, weights):
        def part(u, groups):
            s = table_ref[0, 2 * p + u]
            live = jnp.where(s >= 0, bit_of, 0)
            s = jnp.maximum(s, 0)
            for g in groups:
                edge = [
                    jnp.where(
                        (jnp.broadcast_to(words[w, pl.ds(s, 1), :], (8, TILE)) & live) != 0, 1.0, 0.0
                    )
                    for w in (2 * g, 2 * g + 1)
                ]
                edge = jnp.concatenate(edge, axis=0).astype(jnp.bfloat16)
                here = slice(u * TILE + g * STRIP, u * TILE + (g + 1) * STRIP)
                for h in range(HEADS):
                    lanes = slice(h * TILE, (h + 1) * TILE)
                    twice = jnp.tanh(scores[here, lanes] + half_bias[h]) + 1.0
                    weights[here, lanes] = twice.astype(jnp.bfloat16) * edge

        half = TILE // STRIP // 2
        return [
            functools.partial(part, u, range(v * half, (v + 1) * half))
            for u in range(2) for v in range(2)
        ]

    def mix(p, weights):
        a = table_ref[1, 2 * p]
        source = [table_ref[2, 2 * p + u] for u in range(2)]

        def part(half):
            rows = slice(half * TILE, (half + 1) * TILE)
            v = jnp.concatenate([values[b, rows, :] for b in source], axis=1)
            v = jnp.concatenate([v, ones], axis=0)
            both = jnp.dot(
                v, weights[:, half * 2 * TILE : (half + 1) * 2 * TILE],
                preferred_element_type=jnp.float32,
            )
            for side in range(2):
                start = half * TILE + side * HEAD
                num_acc[a, start : start + HEAD, :] += both[
                    side * HEAD : (side + 1) * HEAD, side * TILE : (side + 1) * TILE
                ]
            den_acc[a, half] += both[TILE : TILE + 8]

        return [functools.partial(part, half) for half in range(2)]

    def together(scored, mixed, weighed):
        for k in range(2):
            scored[k]()
            mixed[k]()
        for part in weighed:
            part()

    for part in score(0, even_scores):
        part()

    def turn(t, _):
        for u in range(0, UNROLL, 2):
            p = UNROLL * t + u
            together(
                score(p + 1, odd_scores), mix(jnp.maximum(p - 1, 0), odd_weights),
                weigh(p, even_scores, even_weights),
            )
            together(
                score(p + 2, even_scores), mix(p, even_weights),
                weigh(p + 1, odd_scores, odd_weights),
            )
        return 0

    turns = (pairs + UNROLL - 1) // UNROLL
    lax.fori_loop(0, turns, turn, 0)
    for part in mix(jnp.maximum(UNROLL * turns - 1, 0), odd_weights):
        part()
    num_ref[...] = (num_acc[...] * 0.5).astype(num_ref.dtype)
    for a in range(den_acc.shape[0]):
        for h in range(HEADS):
            lanes = slice(h % 2 * TILE, (h % 2 + 1) * TILE)
            den_ref[a, h : h + 1, :] = den_acc[a, h // 2, 0:1, lanes] * 0.5


def attention(table, bias, gathered, values, stationary, words):
    row_tiles = stationary.shape[0]
    smem = pl.BlockSpec(memory_space=pltpu.SMEM)
    vmem = pl.BlockSpec(memory_space=pltpu.VMEM)
    return pl.pallas_call(
        attention_kernel,
        out_shape=(
            jax.ShapeDtypeStruct((row_tiles, D, TILE), jnp.bfloat16),
            jax.ShapeDtypeStruct((row_tiles, HEADS, TILE), jnp.float32),
        ),
        in_specs=[smem] * 2 + [vmem] * 4,
        out_specs=(vmem, vmem),
        scratch_shapes=[
            pltpu.VMEM((row_tiles, D, TILE), jnp.float32),
            pltpu.VMEM((row_tiles, 2, 8, 2 * TILE), jnp.float32),
            pltpu.VMEM((2 * TILE, HEADS * TILE), jnp.float32),
            pltpu.VMEM((2 * TILE, HEADS * TILE), jnp.float32),
            pltpu.VMEM((2 * TILE, HEADS * TILE), jnp.bfloat16),
            pltpu.VMEM((2 * TILE, HEADS * TILE), jnp.bfloat16),
        ],
        compiler_params=pltpu.CompilerParams(vmem_limit_bytes=16 * 1024 * 1024),
        name="attention",
    )(table, bias, gathered, values, stationary, words)


def finish_kernel(
    features_ref, num_ref, den_ref, w_ref, gain_ref, out_ref,
    nums, dens, send, recv,
):
    z, x, y, core = position()
    y_lo = y % 2
    meet(site_partners(z, x, y, core))
    home = y_lo == core

    tiles = NODES // TILE

    def part(d, t):
        c = (y + d) % NY
        if t < tiles:
            src, dst = num_ref.at[c, t], nums.at[y, t]
        else:
            src, dst = den_ref.at[c], dens.at[y]
        return pltpu.make_async_remote_copy(
            src_ref=src, dst_ref=dst, send_sem=send.at[d, t], recv_sem=recv.at[y, t],
            device_id=device(z, x, c // 2 * 2 + core, c % 2), device_id_type=MESH,
        )

    order = (tiles,) + tuple(range(tiles))
    for t in order:
        for d in (2, 1, 3):
            part(d, t).start()

        @pl.when(home)
        def _():
            if t < tiles:
                src, dst = num_ref.at[y, t], nums.at[y, t]
            else:
                src, dst = den_ref.at[y], dens.at[y]
            pltpu.make_async_copy(src, dst, recv.at[y, t]).start()

        @pl.when(jnp.logical_not(home))
        def _():
            part(0, t).start()

    def come(t):
        for c in range(NY):
            here = nums.at[c, t] if t < tiles else dens.at[c]
            pltpu.make_async_copy(here, here, recv.at[c, t]).wait()

    come(tiles)
    weight = 1.0 + sum(dens[c] for c in range(NY))
    gain = gain_ref[...]
    node, lane_node = lane_order()
    to_nodes = jnp.transpose(jnp.where(node == lane_node, 1.0, 0.0)).astype(jnp.bfloat16)
    for t in range(NODES // TILE):
        come(t)
        total = sum(nums[c, t].astype(jnp.float32) for c in range(NY))
        mixed = total.reshape(HEADS, HEAD, TILE) / weight[t].reshape(HEADS, 1, TILE)
        mixed = mixed.reshape(D, TILE).astype(jnp.bfloat16)
        mixed = jnp.dot(mixed, to_nodes, preferred_element_type=jnp.float32).astype(jnp.bfloat16)
        projected = lax.dot_general(
            mixed, w_ref[...], (((0,), (0,)), ((), ())), preferred_element_type=jnp.float32
        )
        square = jnp.mean(projected * projected, axis=1, keepdims=True)
        here = pl.ds(t * TILE, TILE)
        out_ref[here, :] = features_ref[here, :] + gain * projected * lax.rsqrt(square + 1e-05)
    for t in order:
        for d in (1, 2, 3):
            part(d, t).wait_send()

        @pl.when(jnp.logical_not(home))
        def _():
            part(0, t).wait_send()


def finish(features, numerator, denominator, w_out, gain):
    vmem = pl.BlockSpec(memory_space=pltpu.VMEM)
    hbm = pl.BlockSpec(memory_space=pl.ANY)
    dma = pltpu.SemaphoreType.DMA
    return pl.pallas_call(
        finish_kernel,
        out_shape=jax.ShapeDtypeStruct(features.shape, jnp.float32),
        in_specs=[vmem, hbm, hbm, vmem, vmem],
        out_specs=vmem,
        scratch_shapes=[
            pltpu.VMEM(numerator.shape, numerator.dtype),
            pltpu.VMEM(denominator.shape, denominator.dtype),
            dma((NY, 4)), dma((NY, 4)),
        ],
        compiler_params=pltpu.CompilerParams(
            collective_id=1, has_side_effects=True, vmem_limit_bytes=32 * 1024 * 1024
        ),
        name="finish",
    )(features, numerator, denominator, w_out, gain)


def local(
    features, w_qkv, w_out, head_bias, out_gain, tile_rows, tile_cols, tile_masks, tile_count
):
    block_tiles = features.shape[0] // TILE
    gathered, values, stationary, words, table = exchange(
        features, tile_masks[0], jnp.concatenate([tile_rows, tile_cols], axis=0), tile_count, w_qkv
    )
    numerator, denominator = attention(
        table, head_bias, gathered, values, stationary, words
    )
    return finish(
        features,
        numerator.reshape(NY, block_tiles, D, TILE),
        denominator.reshape(NY, block_tiles, HEADS, TILE),
        w_out, out_gain[None, :],
    )


def solution(mesh):
    placed = (
        P(("row", "col"), None),
        P(),
        P(),
        P(),
        P(),
        P(("row", "col"), None),
        P(("row", "col"), None),
        P(("row", "col"), None, None),
        P(("row", "col")),
    )
    return jax.shard_map(
        local, mesh=mesh, in_specs=placed, out_specs=P(("row", "col"), None), check_vma=False
    )
```

```python
import functools

import jax
import jax.numpy as jnp
from jax import lax
from jax.experimental import pallas as pl
from jax.experimental.pallas import tpu as pltpu
from jax.sharding import PartitionSpec as P

TILE = 128
HEADS = 4
HEAD = 64
D = 256
STRIP = 16
UNROLL = 12
TABLE = 384
NX, NY, NZ = 4, 4, 8
SITES = NX * NZ
NODES = 384
FIRST = 160
SECOND = NODES - FIRST
BLOCK = NODES // TILE
MESH = pl.DeviceIdType.MESH
NT = (((1,), (1,)), ((), ()))


def position():
    row, col = lax.axis_index("row"), lax.axis_index("col")
    return row // 8, row // 2 % 4, col // 2 * 2 + row % 2, col % 2


def device(z, x, y, core):
    return ((z * NX + x) * 2 + y % 2, y // 2 * 2 + core)


def meet(partners, meanwhile=None):
    barrier = pltpu.get_barrier_semaphore()
    for partner in partners:
        pl.semaphore_signal(barrier, inc=1, device_id=partner, device_id_type=MESH)
    if meanwhile is not None:
        meanwhile()
    pl.semaphore_wait(barrier, len(partners))


def site_partners(z, x, y, core):
    found = [device(z, x, y, 1 - core)]
    for d in range(1, NY):
        found += [device(z, x, (y + d) % NY, core), device(z, x, (y + d) % NY, 1 - core)]
    return found


def lane_order():
    node = lax.broadcasted_iota(jnp.int32, (TILE, TILE), 0)
    lane = lax.broadcasted_iota(jnp.int32, (TILE, TILE), 1)
    return node, lane % 16 * 8 + lane // 16


def exchange_kernel(
    features_ref, masks_ref, lists_ref, count_ref, weights_ref,
    gathered, values, stationary, words, table,
    queries, own, own_queries, wq, wv, bits, landed, sorted_slots, diagonal,
    query_send, query_recv, list_send, list_recv,
    ring_send, first_x, first_z, second_z, second_x, sibling_send, sibling_recv,
):
    z, x, y, core = position()
    y_lo, y_hi = y % 2, y // 2
    site = z * NX + x

    def setup():
        own[...] = features_ref[...].astype(jnp.bfloat16)
        wq[...] = jnp.transpose(weights_ref[:, 0:D])
        wv[...] = jnp.transpose(weights_ref[:, 2 * D : 3 * D])
        bits[...] = masks_ref[...].astype(jnp.float32).astype(jnp.bfloat16)
        diagonal[...] = jnp.zeros_like(diagonal)

    meet(
        site_partners(z, x, y, core)
        + [device(z, (x + d) % NX, y, core) for d in (1, 2, 3)]
        + [device((z + d) % NZ, x, y, core) for d in (1, 7)],
        setup,
    )

    my_list = y_hi * 2 + core
    home = y_lo == core
    partner = device(z, x, y_hi * 2 + core, y_lo)

    def to_partner(src, dst, k):
        return pltpu.make_async_remote_copy(
            src_ref=src, dst_ref=dst, send_sem=list_send.at[k], recv_sem=list_recv.at[k],
            device_id=partner, device_id_type=MESH,
        )

    def hand_over(src, dst, k):
        @pl.when(home)
        def _():
            pltpu.make_async_copy(src, dst, list_recv.at[k]).start()

        @pl.when(jnp.logical_not(home))
        def _():
            to_partner(src, dst, k).start()

    def handed(ref, k):
        pltpu.make_async_copy(ref, ref, list_recv.at[k]).wait()

    def rows(a_site, parity, low, count):
        return pl.ds(pl.multiple_of((a_site * 2 + parity) * NODES + low, 16), count)

    def remote(src, dst, send, recv, target):
        pltpu.make_async_remote_copy(
            src_ref=src, dst_ref=dst, send_sem=send, recv_sem=recv,
            device_id=target, device_id_type=MESH,
        ).start()

    def arrived(a_site, low, count, sem):
        here = gathered.at[rows(a_site, core, low, count)]
        pltpu.make_async_copy(here, here, sem).wait()

    def forward(a_site, low, count, send, recv, target):
        here = gathered.at[rows(a_site, core, low, count)]
        remote(here, here, send, recv, target)

    up, down = device((z + 1) % NZ, x, y, core), device((z + 7) % NZ, x, y, core)
    right, left = device(z, (x + 1) % NX, y, core), device(z, (x + 3) % NX, y, core)
    across = device(z, (x + 2) % NX, y, core)
    other = device(z, x, y, 1 - core)
    z_to, x_to = (up, down), (right, left)

    def site_of(dz, dx):
        return (z + dz + NZ) % NZ * NX + (x + dx + NX) % NX

    def to_queries(d):
        return pltpu.make_async_remote_copy(
            src_ref=own_queries, dst_ref=queries.at[my_list],
            send_sem=query_send.at[d], recv_sem=query_recv.at[my_list],
            device_id=device(z, x, (y_hi * 2 + core + d) % NY, y_lo), device_id_type=MESH,
        )

    def prepare():
        node, lane_node = lane_order()
        to_lanes = jnp.where(node == lane_node, 1.0, 0.0).astype(jnp.bfloat16)
        q = lax.dot_general(wq[...], own[...], NT, preferred_element_type=jnp.float32)
        q = q.astype(jnp.bfloat16) * jnp.bfloat16(0.0625)
        for t in range(BLOCK):
            own_queries[t] = jnp.dot(
                q[:, t * TILE : (t + 1) * TILE], to_lanes, preferred_element_type=jnp.float32
            ).astype(jnp.bfloat16)
        sort_slots()

    def fold(c, t):
        if t == 0:
            pltpu.make_async_copy(queries.at[c], queries.at[c], query_recv.at[c]).wait()
        for h in range(HEADS):
            diagonal[h * HEAD : (h + 1) * HEAD, h * TILE : (h + 1) * TILE] = (
                queries[c, t, h * HEAD : (h + 1) * HEAD, :]
            )
        stationary[c * BLOCK + t] = jnp.dot(
            weights_ref[:, D : 2 * D], diagonal[...], preferred_element_type=jnp.float32
        ).astype(jnp.bfloat16)

    def spread(c):
        words[c] = landed[:, c * TILE : (c + 1) * TILE].astype(jnp.float32).astype(jnp.int32)

    def swap_bit(b):
        step = 1 << b
        slots = words.shape[1]
        upper = (lax.broadcasted_iota(jnp.int32, (slots, TILE), 1) // step) % 2 == 1
        for c in range(words.shape[0]):
            if c & step == 0:
                low, high = words[c], words[c + step]
                words[c] = jnp.where(upper, pltpu.roll(high, step, 1), low)
                words[c + step] = jnp.where(upper, high, pltpu.roll(low, TILE - step, 1))

    def start_words():
        handed(landed, 1)
        for c in range(words.shape[0]):
            spread(c)

    def sort_slots():
        slots = lists_ref.shape[1]
        row_tiles = NY * BLOCK
        to, source = (lists_ref[k : k + 1, :].astype(jnp.float32) for k in range(2))
        count = jnp.full((1, slots), count_ref[0], jnp.int32).astype(jnp.float32)
        slot = lax.broadcasted_iota(jnp.int32, (1, slots), 1).astype(jnp.float32)
        a = to - row_tiles * jnp.floor((to + 0.5) * (1.0 / row_tiles))
        b = BLOCK * jnp.floor((source + 0.5) * (1.0 / row_tiles)) + (
            source - BLOCK * jnp.floor((source + 0.5) * (1.0 / BLOCK))
        )
        a = jnp.where(slot < count, a, float(row_tiles))
        base = jnp.zeros_like(a)
        total = jnp.zeros((1, 1), jnp.float32)
        for tile in range(row_tiles):
            number = jnp.sum(jnp.where(a == tile, 1.0, 0.0), axis=1, keepdims=True)
            number = 2.0 * jnp.floor((number + 1.5) * 0.5)
            base += jnp.where(a > tile, number, 0.0)
            total += number
        across_lanes = jnp.broadcast_to(a, (slots, slots))
        down = jnp.transpose(across_lanes)
        earlier = lax.broadcasted_iota(jnp.int32, (slots, slots), 0) < lax.broadcasted_iota(
            jnp.int32, (slots, slots), 1
        )
        rank = jnp.sum(
            jnp.where((across_lanes == down) & earlier, 1.0, 0.0), axis=0, keepdims=True
        )
        at = jnp.where(a < row_tiles, base + rank, float(TABLE))
        at_down = jnp.transpose(jnp.broadcast_to(at, (TABLE, slots)))
        hit = at_down == lax.broadcasted_iota(jnp.int32, (slots, TABLE), 1).astype(jnp.float32)

        def pick(value):
            down = jnp.transpose(jnp.broadcast_to(value, (TABLE, slots)))
            return jnp.sum(jnp.where(hit, down, 0.0), axis=0, keepdims=True)

        sorted_slots[0:1, :] = (pick(slot + 1.0) - 1.0).astype(jnp.int32)
        sorted_slots[1:2, :] = pick(a).astype(jnp.int32)
        sorted_slots[2:3, :] = pick(b).astype(jnp.int32)
        sorted_slots[3:4, :] = jnp.broadcast_to(total * 0.5, (1, TABLE)).astype(jnp.int32)
        sorted_slots[4:8, :] = jnp.zeros((4, TABLE), jnp.int32)

    hand_over(own, gathered.at[rows(site, y_lo, 0, NODES)], 0)

    @pl.when(jnp.logical_not(home))
    def _():
        prepare()

    handed(gathered.at[rows(site, core, 0, NODES)], 0)
    for s in range(2):
        forward(site, FIRST, SECOND, ring_send.at[s], second_z.at[s, 0], z_to[s])
        forward(site, 0, FIRST, ring_send.at[2 + s], first_x.at[s], x_to[s])
    forward(site, 0, FIRST, ring_send.at[4], first_x.at[2], across)
    for s in range(2):
        forward(site, FIRST, SECOND, ring_send.at[2 + s], second_x.at[0, s, 0], x_to[s])
        forward(site, 0, FIRST, ring_send.at[s], first_z.at[s, 0, 0], z_to[s])

    @pl.when(home)
    def _():
        prepare()
        pltpu.make_async_copy(own_queries, queries.at[my_list], query_recv.at[my_list]).start()

    @pl.when(jnp.logical_not(home))
    def _():
        to_queries(0).start()

    for d in (1, 2, 3):
        to_queries(d).start()
    hand_over(bits, landed, 1)
    hand_over(sorted_slots, table, 2)

    X_OFF = (0, -1, 1, 2)
    Z_OFF = (0, -1, 1, -2, 2, -3, 3, 4)
    HALF1, HALF2 = FIRST // 2, SECOND // 2

    def second_z_step(t):
        for s in range(2):
            sign = -1 if s == 0 else 1
            if t < 4:
                a = site_of(sign * t, 0)
                arrived(a, FIRST, SECOND, second_z.at[s, t - 1])
                if t < 3:
                    forward(a, FIRST, SECOND, ring_send.at[s], second_z.at[s, t], z_to[s])
                else:
                    forward(a, FIRST + s * HALF2, HALF2, ring_send.at[s], second_z.at[s, 3], z_to[s])
                k = Z_OFF.index(sign * t)
                for e in range(2):
                    forward(a, FIRST, SECOND, ring_send.at[2 + e], second_x.at[k, e, 0], x_to[e])
        if t == 4:
            a = site_of(4, 0)
            for s in range(2):
                arrived(a, FIRST + s * HALF2, HALF2, second_z.at[s, 3])
            for e in range(2):
                forward(a, FIRST, SECOND, ring_send.at[2 + e], second_x.at[7, e, 0], x_to[e])

    def first_x_step(*which):
        for k in which:
            a = site_of(0, X_OFF[k + 1])
            arrived(a, 0, FIRST, first_x.at[k])
            for s in range(2):
                forward(a, 0, FIRST, ring_send.at[s], first_z.at[s, 0, k + 1], z_to[s])

    def first_z_step(t, k):
        if t < 4:
            for s in range(2):
                sign = -1 if s == 0 else 1
                a = site_of(sign * t, X_OFF[k])
                arrived(a, 0, FIRST, first_z.at[s, t - 1, k])
                if t < 3:
                    forward(a, 0, FIRST, ring_send.at[s], first_z.at[s, t, k], z_to[s])
                else:
                    forward(a, s * HALF1, HALF1, ring_send.at[s], first_z.at[s, 3, k], z_to[s])
        else:
            a = site_of(4, X_OFF[k])
            for s in range(2):
                arrived(a, s * HALF1, HALF1, first_z.at[s, 3, k])

    def second_x_step(k):
        for e in range(2):
            sign = -1 if e == 0 else 1
            a = site_of(Z_OFF[k], sign)
            arrived(a, FIRST, SECOND, second_x.at[k, e, 0])
            forward(a, FIRST + e * HALF2, HALF2, ring_send.at[2 + e], second_x.at[k, e, 1], x_to[e])

    def second_x_end(k):
        a = site_of(Z_OFF[k], 2)
        for e in range(2):
            arrived(a, FIRST + e * HALF2, HALF2, second_x.at[k, e, 1])

    def project(*blocks):
        sites = [site_of(dz, X_OFF[k]) for dz, k in blocks]
        for a in sites:
            forward(a, 0, NODES, sibling_send.at[0], sibling_recv.at[0], other)
        found = [
            lax.dot_general(
                wv[...], gathered[rows(a, core, 0, NODES), :], NT, preferred_element_type=jnp.float32
            ).astype(jnp.bfloat16)
            for a in sites
        ]
        for a, v in zip(sites, found):
            for t in range(BLOCK):
                values[(a * 2 + core) * BLOCK + t] = v[:, t * TILE : (t + 1) * TILE]
        for a in sites:
            done = values.at[pl.ds((a * 2 + core) * BLOCK, BLOCK)]
            remote(done, done, sibling_send.at[1], sibling_recv.at[1], other)

    def drain(count, sem):
        pltpu.make_async_copy(gathered.at[pl.ds(0, count)], gathered.at[pl.ds(0, count)], sem).wait()

    order = [
        (second_z_step, 1), (first_x_step, 0, 1), (first_z_step, 1, 0), (second_z_step, 2), (fold, 0, 0),
        (second_x_step, 0), (fold, 0, 1), (first_x_step, 2), (fold, 0, 2), (project, (1, 0), (-1, 0)),
        (project, (0, 0), (0, 1)), (fold, 1, 0), (second_x_step, 2), (fold, 1, 1), (second_x_step, 1),
        (first_z_step, 1, 1), (fold, 1, 2), (first_z_step, 2, 0), (project, (2, 0), (-2, 0)), (fold, 2, 0),
        (first_z_step, 1, 2), (fold, 2, 1), (project, (1, 1), (-1, 1)), (second_z_step, 3), (start_words,),
        (first_z_step, 1, 3), (swap_bit, 0), (project, (1, 2), (-1, 2)), (swap_bit, 1), (fold, 2, 2),
        (fold, 3, 0), (second_x_step, 3), (second_x_end, 0), (second_x_end, 1), (second_x_step, 4),
        (swap_bit, 2), (first_z_step, 2, 1), (project, (0, 2), (0, 3)), (project, (2, 1), (-2, 1)),
        (first_z_step, 2, 2), (second_z_step, 4), (fold, 3, 1), (swap_bit, 3), (second_x_end, 2),
        (first_z_step, 2, 3), (fold, 3, 2), (project, (1, 3), (-1, 3)), (second_x_end, 3), (second_x_step, 6),
        (second_x_step, 5), (first_z_step, 3, 1), (project, (3, 1), (-3, 1)), (first_z_step, 3, 0),
        (second_x_end, 4), (project, (3, 0), (-3, 0)), (first_z_step, 3, 2), (project, (3, 2), (-3, 2)),
        (second_x_step, 7), (first_z_step, 3, 3), (project, (2, 3), (-2, 3)), (project, (2, 2), (-2, 2)),
        (second_x_end, 6), (second_x_end, 5), (project, (3, 3), (-3, 3)), (first_z_step, 4, 0),
        (first_z_step, 4, 1), (first_z_step, 4, 2), (project, (4, 0), (4, 1)), (first_z_step, 4, 3),
        (second_x_end, 7), (project, (4, 2), (4, 3)),
    ]
    for step in order:
        step[0](*step[1:])

    half_values = values.at[pl.ds(0, SITES * BLOCK)]
    pltpu.make_async_copy(half_values, half_values, sibling_recv.at[1]).wait()
    pltpu.make_async_copy(half_values, half_values, sibling_send.at[1]).wait()
    drain(SITES * NODES, sibling_recv.at[0])
    drain(SITES * NODES, sibling_send.at[0])
    z_rows = 3 * SECOND + HALF2 + NX * (3 * FIRST + HALF1)
    x_rows = FIRST + NZ * (SECOND + HALF2)
    for s in range(2):
        drain(z_rows, ring_send.at[s])
        drain(x_rows, ring_send.at[2 + s])
    drain(FIRST, ring_send.at[4])
    for d in range(1, NY):
        to_queries(d).wait_send()
    handed(table, 2)

    @pl.when(jnp.logical_not(home))
    def _():
        to_queries(0).wait_send()
        to_partner(own, gathered.at[rows(site, y_lo, 0, NODES)], 0).wait_send()
        to_partner(bits, landed, 1).wait_send()
        to_partner(sorted_slots, table, 2).wait_send()


def exchange(features, masks, lists, tile_count, weights):
    slots, length = masks.shape
    vmem = pl.BlockSpec(memory_space=pltpu.VMEM)
    smem = pl.BlockSpec(memory_space=pltpu.SMEM)
    dma = pltpu.SemaphoreType.DMA
    half = jnp.bfloat16
    return pl.pallas_call(
        exchange_kernel,
        out_shape=(
            jax.ShapeDtypeStruct((SITES * 2 * NODES, D), half),
            jax.ShapeDtypeStruct((SITES * 2 * BLOCK, D, TILE), half),
            jax.ShapeDtypeStruct((NY * BLOCK, D, HEADS * TILE), half),
            jax.ShapeDtypeStruct((length // TILE, slots, TILE), jnp.int32),
            jax.ShapeDtypeStruct((8, TABLE), jnp.int32),
        ),
        in_specs=[vmem, vmem, vmem, smem, vmem],
        out_specs=(vmem,) * 5,
        scratch_shapes=[
            pltpu.VMEM((NY, BLOCK, D, TILE), half),
            pltpu.VMEM((NODES, D), half),
            pltpu.VMEM((BLOCK, D, TILE), half),
            pltpu.VMEM((D, D), half),
            pltpu.VMEM((D, D), half),
            pltpu.VMEM((slots, length), half),
            pltpu.VMEM((slots, length), half),
            pltpu.VMEM((8, TABLE), jnp.int32),
            pltpu.VMEM((D, HEADS * TILE), half),
            dma((NY,)), dma((NY,)), dma((3,)), dma((3,)),
            dma((5,)), dma((3,)), dma((2, 4, NX)), dma((2, 4)), dma((NZ, 2, 2)), dma((2,)), dma((2,)),
        ],
        compiler_params=pltpu.CompilerParams(
            collective_id=0, has_side_effects=True, vmem_limit_bytes=16 * 1024 * 1024
        ),
        name="exchange",
    )(features, masks, lists, tile_count, weights)


def attention_kernel(
    table_ref, bias_ref, gathered, values, stationary, words,
    num_ref, den_ref, num_acc, den_acc, even_scores, odd_scores, even_weights, odd_weights,
):
    pairs = table_ref[3, 0]
    num_acc[...] = jnp.zeros_like(num_acc)
    den_acc[...] = jnp.zeros_like(den_acc)
    odd_weights[...] = jnp.zeros_like(odd_weights)
    bit_of = jnp.left_shift(jnp.int32(1), lax.broadcasted_iota(jnp.int32, (8, TILE), 0))
    half_bias = [bias_ref[h] * 0.5 for h in range(HEADS)]
    ones = jnp.ones((STRIP, 2 * TILE), jnp.bfloat16)

    def score(p, scores):
        a = table_ref[1, 2 * p]
        sources = jnp.concatenate(
            [
                gathered[pl.ds(pl.multiple_of(table_ref[2, 2 * p + u] * TILE, TILE), TILE), :]
                for u in range(2)
            ],
            axis=0,
        )

        def part(half):
            lanes = slice(half * 2 * TILE, (half + 1) * 2 * TILE)
            scores[:, lanes] = jnp.dot(
                sources, stationary[a, :, lanes], preferred_element_type=jnp.float32
            )

        return [functools.partial(part, half) for half in range(2)]

    def weigh(p, scores, weights):
        def part(u, groups):
            s = table_ref[0, 2 * p + u]
            live = jnp.where(s >= 0, bit_of, 0)
            s = jnp.maximum(s, 0)
            for g in groups:
                edge = [
                    jnp.where(
                        (jnp.broadcast_to(words[w, pl.ds(s, 1), :], (8, TILE)) & live) != 0, 1.0, 0.0
                    )
                    for w in (2 * g, 2 * g + 1)
                ]
                edge = jnp.concatenate(edge, axis=0).astype(jnp.bfloat16)
                here = slice(u * TILE + g * STRIP, u * TILE + (g + 1) * STRIP)
                for h in range(HEADS):
                    lanes = slice(h * TILE, (h + 1) * TILE)
                    twice = jnp.tanh(scores[here, lanes] + half_bias[h]) + 1.0
                    weights[here, lanes] = twice.astype(jnp.bfloat16) * edge

        half = TILE // STRIP // 2
        return [
            functools.partial(part, u, range(v * half, (v + 1) * half))
            for u in range(2) for v in range(2)
        ]

    def mix(p, weights):
        a = table_ref[1, 2 * p]
        source = [table_ref[2, 2 * p + u] for u in range(2)]

        def part(half):
            rows = slice(half * TILE, (half + 1) * TILE)
            v = jnp.concatenate([values[b, rows, :] for b in source], axis=1)
            v = jnp.concatenate([v, ones], axis=0)
            both = jnp.dot(
                v, weights[:, half * 2 * TILE : (half + 1) * 2 * TILE],
                preferred_element_type=jnp.float32,
            )
            for side in range(2):
                start = half * TILE + side * HEAD
                num_acc[a, start : start + HEAD, :] += both[
                    side * HEAD : (side + 1) * HEAD, side * TILE : (side + 1) * TILE
                ]
            den_acc[a, half] += both[TILE : TILE + 8]

        return [functools.partial(part, half) for half in range(2)]

    def together(scored, mixed, weighed):
        for k in range(2):
            scored[k]()
            mixed[k]()
        for part in weighed:
            part()

    for part in score(0, even_scores):
        part()

    def turn(t, _):
        for u in range(0, UNROLL, 2):
            p = UNROLL * t + u
            together(
                score(p + 1, odd_scores), mix(jnp.maximum(p - 1, 0), odd_weights),
                weigh(p, even_scores, even_weights),
            )
            together(
                score(p + 2, even_scores), mix(p, even_weights),
                weigh(p + 1, odd_scores, odd_weights),
            )
        return 0

    turns = (pairs + UNROLL - 1) // UNROLL
    lax.fori_loop(0, turns, turn, 0)
    for part in mix(jnp.maximum(UNROLL * turns - 1, 0), odd_weights):
        part()
    num_ref[...] = (num_acc[...] * 0.5).astype(num_ref.dtype)
    for a in range(den_acc.shape[0]):
        for h in range(HEADS):
            lanes = slice(h % 2 * TILE, (h % 2 + 1) * TILE)
            den_ref[a, h : h + 1, :] = den_acc[a, h // 2, 0:1, lanes] * 0.5


def attention(table, bias, gathered, values, stationary, words):
    row_tiles = stationary.shape[0]
    smem = pl.BlockSpec(memory_space=pltpu.SMEM)
    vmem = pl.BlockSpec(memory_space=pltpu.VMEM)
    return pl.pallas_call(
        attention_kernel,
        out_shape=(
            jax.ShapeDtypeStruct((row_tiles, D, TILE), jnp.bfloat16),
            jax.ShapeDtypeStruct((row_tiles, HEADS, TILE), jnp.float32),
        ),
        in_specs=[smem] * 2 + [vmem] * 4,
        out_specs=(vmem, vmem),
        scratch_shapes=[
            pltpu.VMEM((row_tiles, D, TILE), jnp.float32),
            pltpu.VMEM((row_tiles, 2, 8, 2 * TILE), jnp.float32),
            pltpu.VMEM((2 * TILE, HEADS * TILE), jnp.float32),
            pltpu.VMEM((2 * TILE, HEADS * TILE), jnp.float32),
            pltpu.VMEM((2 * TILE, HEADS * TILE), jnp.bfloat16),
            pltpu.VMEM((2 * TILE, HEADS * TILE), jnp.bfloat16),
        ],
        compiler_params=pltpu.CompilerParams(vmem_limit_bytes=16 * 1024 * 1024),
        name="attention",
    )(table, bias, gathered, values, stationary, words)


def finish_kernel(
    features_ref, num_ref, den_ref, w_ref, gain_ref, out_ref,
    nums, dens, send, recv,
):
    z, x, y, core = position()
    y_lo = y % 2
    meet(site_partners(z, x, y, core))
    home = y_lo == core

    def part(d, src, dst, k):
        c = (y + d) % NY
        return pltpu.make_async_remote_copy(
            src_ref=src.at[c], dst_ref=dst.at[y], send_sem=send.at[k, d], recv_sem=recv.at[k, y],
            device_id=device(z, x, c // 2 * 2 + core, c % 2), device_id_type=MESH,
        )

    pairs = ((num_ref, nums), (den_ref, dens))
    for d in (1, 2, 3):
        for k, (src, dst) in enumerate(pairs):
            part(d, src, dst, k).start()
    for k, (src, dst) in enumerate(pairs):
        @pl.when(home)
        def _():
            pltpu.make_async_copy(src.at[y], dst.at[y], recv.at[k, y]).start()

        @pl.when(jnp.logical_not(home))
        def _():
            part(0, src, dst, k).start()

    for c in range(NY):
        for k, (src, dst) in enumerate(pairs):
            pltpu.make_async_copy(dst.at[c], dst.at[c], recv.at[k, c]).wait()
    total = sum(nums[c].astype(jnp.float32) for c in range(NY))
    weight = 1.0 + sum(dens[c] for c in range(NY))
    gain = gain_ref[...]
    node, lane_node = lane_order()
    to_nodes = jnp.transpose(jnp.where(node == lane_node, 1.0, 0.0)).astype(jnp.bfloat16)
    for t in range(NODES // TILE):
        mixed = total[t].reshape(HEADS, HEAD, TILE) / weight[t].reshape(HEADS, 1, TILE)
        mixed = mixed.reshape(D, TILE).astype(jnp.bfloat16)
        mixed = jnp.dot(mixed, to_nodes, preferred_element_type=jnp.float32).astype(jnp.bfloat16)
        projected = lax.dot_general(
            mixed, w_ref[...], (((0,), (0,)), ((), ())), preferred_element_type=jnp.float32
        )
        square = jnp.mean(projected * projected, axis=1, keepdims=True)
        here = pl.ds(t * TILE, TILE)
        out_ref[here, :] = features_ref[here, :] + gain * projected * lax.rsqrt(square + 1e-05)
    for d in range(NY):
        for k, (src, dst) in enumerate(pairs):
            if d:
                part(d, src, dst, k).wait_send()
            else:
                @pl.when(jnp.logical_not(home))
                def _():
                    part(d, src, dst, k).wait_send()


def finish(features, numerator, denominator, w_out, gain):
    vmem = pl.BlockSpec(memory_space=pltpu.VMEM)
    hbm = pl.BlockSpec(memory_space=pl.ANY)
    dma = pltpu.SemaphoreType.DMA
    return pl.pallas_call(
        finish_kernel,
        out_shape=jax.ShapeDtypeStruct(features.shape, jnp.float32),
        in_specs=[vmem, hbm, hbm, vmem, vmem],
        out_specs=vmem,
        scratch_shapes=[
            pltpu.VMEM(numerator.shape, numerator.dtype),
            pltpu.VMEM(denominator.shape, denominator.dtype),
            dma((2, NY)), dma((2, NY)),
        ],
        compiler_params=pltpu.CompilerParams(
            collective_id=1, has_side_effects=True, vmem_limit_bytes=32 * 1024 * 1024
        ),
        name="finish",
    )(features, numerator, denominator, w_out, gain)


def local(
    features, w_qkv, w_out, head_bias, out_gain, tile_rows, tile_cols, tile_masks, tile_count
):
    block_tiles = features.shape[0] // TILE
    gathered, values, stationary, words, table = exchange(
        features, tile_masks[0], jnp.concatenate([tile_rows, tile_cols], axis=0), tile_count, w_qkv
    )
    numerator, denominator = attention(
        table, head_bias, gathered, values, stationary, words
    )
    return finish(
        features,
        numerator.reshape(NY, block_tiles, D, TILE),
        denominator.reshape(NY, block_tiles, HEADS, TILE),
        w_out, out_gain[None, :],
    )


def solution(mesh):
    placed = (
        P(("row", "col"), None),
        P(),
        P(),
        P(),
        P(),
        P(("row", "col"), None),
        P(("row", "col"), None),
        P(("row", "col"), None, None),
        P(("row", "col")),
    )
    return jax.shard_map(
        local, mesh=mesh, in_specs=placed, out_specs=P(("row", "col"), None), check_vma=False
    )
```

```python
import functools

import jax
import jax.numpy as jnp
from jax import lax
from jax.experimental import pallas as pl
from jax.experimental.pallas import tpu as pltpu
from jax.sharding import PartitionSpec as P

TILE = 128
HEADS = 4
HEAD = 64
D = 256
STRIP = 16
UNROLL = 22
TABLE = 384
NX, NY, NZ = 4, 4, 8
SITES = NX * NZ
NODES = 384
FIRST = 160
SECOND = NODES - FIRST
BLOCK = NODES // TILE
MESH = pl.DeviceIdType.MESH
NT = (((1,), (1,)), ((), ()))


def position():
    row, col = lax.axis_index("row"), lax.axis_index("col")
    return row // 8, row // 2 % 4, col // 2 * 2 + row % 2, col % 2


def device(z, x, y, core):
    return ((z * NX + x) * 2 + y % 2, y // 2 * 2 + core)


def meet(partners, meanwhile=None):
    barrier = pltpu.get_barrier_semaphore()
    for partner in partners:
        pl.semaphore_signal(barrier, inc=1, device_id=partner, device_id_type=MESH)
    if meanwhile is not None:
        meanwhile()
    pl.semaphore_wait(barrier, len(partners))


def site_partners(z, x, y, core):
    found = [device(z, x, y, 1 - core)]
    for d in range(1, NY):
        found += [device(z, x, (y + d) % NY, core), device(z, x, (y + d) % NY, 1 - core)]
    return found


def lane_order():
    node = lax.broadcasted_iota(jnp.int32, (TILE, TILE), 0)
    lane = lax.broadcasted_iota(jnp.int32, (TILE, TILE), 1)
    return node, lane % 16 * 8 + lane // 16


def exchange_kernel(
    features_ref, masks_ref, lists_ref, count_ref, weights_ref,
    gathered, values, stationary, words, table,
    queries, own, own_queries, wq, wv, bits, landed, sorted_slots, diagonal,
    query_send, query_recv, list_send, list_recv,
    ring_send, first_x, first_z, second_z, second_x, sibling_send, sibling_recv,
):
    z, x, y, core = position()
    y_lo, y_hi = y % 2, y // 2
    site = z * NX + x

    def setup():
        own[...] = features_ref[...].astype(jnp.bfloat16)
        wq[...] = jnp.transpose(weights_ref[:, 0:D])
        wv[...] = jnp.transpose(weights_ref[:, 2 * D : 3 * D])
        bits[...] = masks_ref[...].astype(jnp.float32).astype(jnp.bfloat16)
        diagonal[...] = jnp.zeros_like(diagonal)

    meet(
        site_partners(z, x, y, core)
        + [device(z, (x + d) % NX, y, core) for d in (1, 2, 3)]
        + [device((z + d) % NZ, x, y, core) for d in (1, 7)],
        setup,
    )

    my_list = y_hi * 2 + core
    home = y_lo == core
    partner = device(z, x, y_hi * 2 + core, y_lo)

    def to_partner(src, dst, k):
        return pltpu.make_async_remote_copy(
            src_ref=src, dst_ref=dst, send_sem=list_send.at[k], recv_sem=list_recv.at[k],
            device_id=partner, device_id_type=MESH,
        )

    def hand_over(src, dst, k):
        @pl.when(home)
        def _():
            pltpu.make_async_copy(src, dst, list_recv.at[k]).start()

        @pl.when(jnp.logical_not(home))
        def _():
            to_partner(src, dst, k).start()

    def handed(ref, k):
        pltpu.make_async_copy(ref, ref, list_recv.at[k]).wait()

    def rows(a_site, parity, low, count):
        return pl.ds(pl.multiple_of((a_site * 2 + parity) * NODES + low, 16), count)

    def remote(src, dst, send, recv, target):
        pltpu.make_async_remote_copy(
            src_ref=src, dst_ref=dst, send_sem=send, recv_sem=recv,
            device_id=target, device_id_type=MESH,
        ).start()

    def arrived(a_site, low, count, sem):
        here = gathered.at[rows(a_site, core, low, count)]
        pltpu.make_async_copy(here, here, sem).wait()

    def forward(a_site, low, count, send, recv, target):
        here = gathered.at[rows(a_site, core, low, count)]
        remote(here, here, send, recv, target)

    up, down = device((z + 1) % NZ, x, y, core), device((z + 7) % NZ, x, y, core)
    right, left = device(z, (x + 1) % NX, y, core), device(z, (x + 3) % NX, y, core)
    across = device(z, (x + 2) % NX, y, core)
    other = device(z, x, y, 1 - core)
    z_to, x_to = (up, down), (right, left)

    def site_of(dz, dx):
        return (z + dz + NZ) % NZ * NX + (x + dx + NX) % NX

    def to_queries(d):
        return pltpu.make_async_remote_copy(
            src_ref=own_queries, dst_ref=queries.at[my_list],
            send_sem=query_send.at[d], recv_sem=query_recv.at[my_list],
            device_id=device(z, x, (y_hi * 2 + core + d) % NY, y_lo), device_id_type=MESH,
        )

    def prepare():
        node, lane_node = lane_order()
        to_lanes = jnp.where(node == lane_node, 1.0, 0.0).astype(jnp.bfloat16)
        q = lax.dot_general(wq[...], own[...], NT, preferred_element_type=jnp.float32)
        q = q.astype(jnp.bfloat16) * jnp.bfloat16(0.0625)
        for t in range(BLOCK):
            own_queries[t] = jnp.dot(
                q[:, t * TILE : (t + 1) * TILE], to_lanes, preferred_element_type=jnp.float32
            ).astype(jnp.bfloat16)

    def fold(c, t):
        if t == 0:
            pltpu.make_async_copy(queries.at[c], queries.at[c], query_recv.at[c]).wait()
        for h in range(HEADS):
            diagonal[h * HEAD : (h + 1) * HEAD, h * TILE : (h + 1) * TILE] = (
                queries[c, t, h * HEAD : (h + 1) * HEAD, :]
            )
        stationary[c * BLOCK + t] = jnp.dot(
            weights_ref[:, D : 2 * D], diagonal[...], preferred_element_type=jnp.float32
        ).astype(jnp.bfloat16)

    def spread(c):
        words[c] = landed[:, c * TILE : (c + 1) * TILE].astype(jnp.float32).astype(jnp.int32)

    def swap_bit(b):
        step = 1 << b
        slots = words.shape[1]
        upper = (lax.broadcasted_iota(jnp.int32, (slots, TILE), 1) // step) % 2 == 1
        for c in range(words.shape[0]):
            if c & step == 0:
                low, high = words[c], words[c + step]
                words[c] = jnp.where(upper, pltpu.roll(high, step, 1), low)
                words[c + step] = jnp.where(upper, high, pltpu.roll(low, TILE - step, 1))

    def start_words():
        handed(landed, 1)
        for c in range(words.shape[0]):
            spread(c)

    placed = []

    def sort_slots():
        slots = lists_ref.shape[1]
        row_tiles = NY * BLOCK
        to, source = (lists_ref[k : k + 1, :].astype(jnp.float32) for k in range(2))
        count = jnp.full((1, slots), count_ref[0], jnp.int32).astype(jnp.float32)
        slot = lax.broadcasted_iota(jnp.int32, (1, slots), 1).astype(jnp.float32)
        a = to - row_tiles * jnp.floor((to + 0.5) * (1.0 / row_tiles))
        b = BLOCK * jnp.floor((source + 0.5) * (1.0 / row_tiles)) + (
            source - BLOCK * jnp.floor((source + 0.5) * (1.0 / BLOCK))
        )
        a = jnp.where(slot < count, a, float(row_tiles))
        base = jnp.zeros_like(a)
        total = jnp.zeros((1, 1), jnp.float32)
        for tile in range(row_tiles):
            number = jnp.sum(jnp.where(a == tile, 1.0, 0.0), axis=1, keepdims=True)
            number = 2.0 * jnp.floor((number + 1.5) * 0.5)
            base += jnp.where(a > tile, number, 0.0)
            total += number
        across_lanes = jnp.broadcast_to(a, (slots, slots))
        down = jnp.transpose(across_lanes)
        earlier = lax.broadcasted_iota(jnp.int32, (slots, slots), 0) < lax.broadcasted_iota(
            jnp.int32, (slots, slots), 1
        )
        rank = jnp.sum(
            jnp.where((across_lanes == down) & earlier, 1.0, 0.0), axis=0, keepdims=True
        )
        at = jnp.where(a < row_tiles, base + rank, float(TABLE))
        placed.extend([slots, row_tiles, slot, a, b, total, at])

    def list_slots():
        slots, row_tiles, slot, a, b, total, at = placed
        at_down = jnp.transpose(jnp.broadcast_to(at, (TABLE, slots)))
        hit = at_down == lax.broadcasted_iota(jnp.int32, (slots, TABLE), 1).astype(jnp.float32)

        def pick(value):
            down = jnp.transpose(jnp.broadcast_to(value, (TABLE, slots)))
            return jnp.sum(jnp.where(hit, down, 0.0), axis=0, keepdims=True)

        sorted_slots[0:1, :] = (pick(slot + 1.0) - 1.0).astype(jnp.int32)
        sorted_slots[1:2, :] = pick(a).astype(jnp.int32)
        sorted_slots[2:3, :] = pick(b).astype(jnp.int32)
        sorted_slots[3:4, :] = jnp.broadcast_to(total * 0.5, (1, TABLE)).astype(jnp.int32)
        sorted_slots[4:8, :] = jnp.zeros((4, TABLE), jnp.int32)
        hand_over(sorted_slots, table, 2)

    hand_over(own, gathered.at[rows(site, y_lo, 0, NODES)], 0)

    @pl.when(jnp.logical_not(home))
    def _():
        prepare()

    handed(gathered.at[rows(site, core, 0, NODES)], 0)
    for s in range(2):
        forward(site, FIRST, SECOND, ring_send.at[s], second_z.at[s, 0], z_to[s])
        forward(site, 0, FIRST, ring_send.at[2 + s], first_x.at[s], x_to[s])
    forward(site, 0, FIRST, ring_send.at[4], first_x.at[2], across)
    for s in range(2):
        forward(site, FIRST, SECOND, ring_send.at[2 + s], second_x.at[0, s, 0], x_to[s])
        forward(site, 0, FIRST, ring_send.at[s], first_z.at[s, 0, 0], z_to[s])

    @pl.when(home)
    def _():
        prepare()
        pltpu.make_async_copy(own_queries, queries.at[my_list], query_recv.at[my_list]).start()

    @pl.when(jnp.logical_not(home))
    def _():
        to_queries(0).start()

    for d in (1, 2, 3):
        to_queries(d).start()
    hand_over(bits, landed, 1)

    X_OFF = (0, -1, 1, 2)
    Z_OFF = (0, -1, 1, -2, 2, -3, 3, 4)
    HALF1, HALF2 = FIRST // 2, SECOND // 2

    def second_z_step(t):
        for s in range(2):
            sign = -1 if s == 0 else 1
            if t < 4:
                a = site_of(sign * t, 0)
                arrived(a, FIRST, SECOND, second_z.at[s, t - 1])
                if t < 3:
                    forward(a, FIRST, SECOND, ring_send.at[s], second_z.at[s, t], z_to[s])
                else:
                    forward(a, FIRST + s * HALF2, HALF2, ring_send.at[s], second_z.at[s, 3], z_to[s])
                k = Z_OFF.index(sign * t)
                for e in range(2):
                    forward(a, FIRST, SECOND, ring_send.at[2 + e], second_x.at[k, e, 0], x_to[e])
        if t == 4:
            a = site_of(4, 0)
            for s in range(2):
                arrived(a, FIRST + s * HALF2, HALF2, second_z.at[s, 3])
            for e in range(2):
                forward(a, FIRST, SECOND, ring_send.at[2 + e], second_x.at[7, e, 0], x_to[e])

    def first_x_step(*which):
        for k in which:
            a = site_of(0, X_OFF[k + 1])
            arrived(a, 0, FIRST, first_x.at[k])
            for s in range(2):
                forward(a, 0, FIRST, ring_send.at[s], first_z.at[s, 0, k + 1], z_to[s])

    def first_z_step(t, k):
        if t < 4:
            for s in range(2):
                sign = -1 if s == 0 else 1
                a = site_of(sign * t, X_OFF[k])
                arrived(a, 0, FIRST, first_z.at[s, t - 1, k])
                if t < 3:
                    forward(a, 0, FIRST, ring_send.at[s], first_z.at[s, t, k], z_to[s])
                else:
                    forward(a, s * HALF1, HALF1, ring_send.at[s], first_z.at[s, 3, k], z_to[s])
        else:
            a = site_of(4, X_OFF[k])
            for s in range(2):
                arrived(a, s * HALF1, HALF1, first_z.at[s, 3, k])

    def second_x_step(k):
        for e in range(2):
            sign = -1 if e == 0 else 1
            a = site_of(Z_OFF[k], sign)
            arrived(a, FIRST, SECOND, second_x.at[k, e, 0])
            forward(a, FIRST + e * HALF2, HALF2, ring_send.at[2 + e], second_x.at[k, e, 1], x_to[e])

    def second_x_end(k):
        a = site_of(Z_OFF[k], 2)
        for e in range(2):
            arrived(a, FIRST + e * HALF2, HALF2, second_x.at[k, e, 1])

    def project(*blocks):
        sites = [site_of(dz, X_OFF[k]) for dz, k in blocks]
        for a in sites:
            forward(a, 0, NODES, sibling_send.at[0], sibling_recv.at[0], other)
        found = [
            lax.dot_general(
                wv[...], gathered[rows(a, core, 0, NODES), :], NT, preferred_element_type=jnp.float32
            ).astype(jnp.bfloat16)
            for a in sites
        ]
        for a, v in zip(sites, found):
            for t in range(BLOCK):
                values[(a * 2 + core) * BLOCK + t] = v[:, t * TILE : (t + 1) * TILE]
        for a in sites:
            done = values.at[pl.ds((a * 2 + core) * BLOCK, BLOCK)]
            remote(done, done, sibling_send.at[1], sibling_recv.at[1], other)

    def drain(count, sem):
        pltpu.make_async_copy(gathered.at[pl.ds(0, count)], gathered.at[pl.ds(0, count)], sem).wait()

    order = [
        (second_z_step, 1), (first_x_step, 0, 1), (first_z_step, 1, 0), (fold, 0, 0), (second_z_step, 2),
        (fold, 0, 1), (second_x_step, 0), (first_x_step, 2), (fold, 0, 2), (project, (1, 0), (-1, 0)),
        (fold, 1, 0), (project, (0, 0), (0, 1)), (fold, 1, 1), (fold, 1, 2), (second_x_step, 1),
        (sort_slots,), (first_z_step, 1, 1), (second_x_step, 2), (first_z_step, 2, 0),
        (project, (2, 0), (-2, 0)), (list_slots,), (first_z_step, 1, 2), (fold, 2, 0), (fold, 2, 1),
        (project, (1, 1), (-1, 1)), (second_z_step, 3), (start_words,), (first_z_step, 1, 3),
        (project, (1, 2), (-1, 2)), (swap_bit, 0), (fold, 2, 2), (second_x_step, 3), (swap_bit, 1),
        (fold, 3, 0), (second_x_end, 0), (second_x_end, 1), (second_x_step, 4), (first_z_step, 2, 1),
        (swap_bit, 2), (project, (2, 1), (-2, 1)), (first_z_step, 2, 2), (project, (0, 2), (0, 3)),
        (second_z_step, 4), (fold, 3, 1), (second_x_end, 2), (project, (1, 3), (-1, 3)), (first_z_step, 2, 3),
        (fold, 3, 2), (swap_bit, 3), (second_x_end, 3), (first_z_step, 3, 0), (second_x_step, 5),
        (second_x_step, 6), (first_z_step, 3, 1), (project, (3, 1), (-3, 1)), (second_x_end, 4),
        (project, (3, 0), (-3, 0)), (first_z_step, 3, 2), (project, (3, 2), (-3, 2)), (second_x_step, 7),
        (first_z_step, 3, 3), (project, (2, 2), (-2, 2)), (project, (2, 3), (-2, 3)), (second_x_end, 5),
        (second_x_end, 6), (project, (3, 3), (-3, 3)), (first_z_step, 4, 0), (first_z_step, 4, 1),
        (first_z_step, 4, 2), (project, (4, 0), (4, 1)), (second_x_end, 7), (first_z_step, 4, 3),
        (project, (4, 2), (4, 3)),
    ]
    for step in order:
        step[0](*step[1:])

    half_values = values.at[pl.ds(0, SITES * BLOCK)]
    pltpu.make_async_copy(half_values, half_values, sibling_recv.at[1]).wait()
    pltpu.make_async_copy(half_values, half_values, sibling_send.at[1]).wait()
    drain(SITES * NODES, sibling_recv.at[0])
    drain(SITES * NODES, sibling_send.at[0])
    z_rows = 3 * SECOND + HALF2 + NX * (3 * FIRST + HALF1)
    x_rows = FIRST + NZ * (SECOND + HALF2)
    for s in range(2):
        drain(z_rows, ring_send.at[s])
        drain(x_rows, ring_send.at[2 + s])
    drain(FIRST, ring_send.at[4])
    for d in range(1, NY):
        to_queries(d).wait_send()
    handed(table, 2)

    @pl.when(jnp.logical_not(home))
    def _():
        to_queries(0).wait_send()
        to_partner(own, gathered.at[rows(site, y_lo, 0, NODES)], 0).wait_send()
        to_partner(bits, landed, 1).wait_send()
        to_partner(sorted_slots, table, 2).wait_send()


def exchange(features, masks, lists, tile_count, weights):
    slots, length = masks.shape
    vmem = pl.BlockSpec(memory_space=pltpu.VMEM)
    smem = pl.BlockSpec(memory_space=pltpu.SMEM)
    dma = pltpu.SemaphoreType.DMA
    half = jnp.bfloat16
    return pl.pallas_call(
        exchange_kernel,
        out_shape=(
            jax.ShapeDtypeStruct((SITES * 2 * NODES, D), half),
            jax.ShapeDtypeStruct((SITES * 2 * BLOCK, D, TILE), half),
            jax.ShapeDtypeStruct((NY * BLOCK, D, HEADS * TILE), half),
            jax.ShapeDtypeStruct((length // TILE, slots, TILE), jnp.int32),
            jax.ShapeDtypeStruct((8, TABLE), jnp.int32),
        ),
        in_specs=[vmem, vmem, vmem, smem, vmem],
        out_specs=(vmem,) * 5,
        scratch_shapes=[
            pltpu.VMEM((NY, BLOCK, D, TILE), half),
            pltpu.VMEM((NODES, D), half),
            pltpu.VMEM((BLOCK, D, TILE), half),
            pltpu.VMEM((D, D), half),
            pltpu.VMEM((D, D), half),
            pltpu.VMEM((slots, length), half),
            pltpu.VMEM((slots, length), half),
            pltpu.VMEM((8, TABLE), jnp.int32),
            pltpu.VMEM((D, HEADS * TILE), half),
            dma((NY,)), dma((NY,)), dma((3,)), dma((3,)),
            dma((5,)), dma((3,)), dma((2, 4, NX)), dma((2, 4)), dma((NZ, 2, 2)), dma((2,)), dma((2,)),
        ],
        compiler_params=pltpu.CompilerParams(
            collective_id=0, has_side_effects=True, vmem_limit_bytes=16 * 1024 * 1024
        ),
        name="exchange",
    )(features, masks, lists, tile_count, weights)


def attention_kernel(
    table_ref, bias_ref, gathered, values, stationary, words,
    num_ref, den_ref, num_acc, den_acc, even_scores, odd_scores, even_weights, odd_weights,
):
    pairs = table_ref[3, 0]
    num_acc[...] = jnp.zeros_like(num_acc)
    den_acc[...] = jnp.zeros_like(den_acc)
    odd_weights[...] = jnp.zeros_like(odd_weights)
    bit_of = jnp.left_shift(jnp.int32(1), lax.broadcasted_iota(jnp.int32, (8, TILE), 0))
    half_bias = [bias_ref[h] * 0.5 for h in range(HEADS)]
    ones = jnp.ones((STRIP, 2 * TILE), jnp.bfloat16)

    def score(p, scores):
        a = table_ref[1, 2 * p]
        sources = jnp.concatenate(
            [
                gathered[pl.ds(pl.multiple_of(table_ref[2, 2 * p + u] * TILE, TILE), TILE), :]
                for u in range(2)
            ],
            axis=0,
        )

        def part(half):
            lanes = slice(half * 2 * TILE, (half + 1) * 2 * TILE)
            scores[:, lanes] = jnp.dot(
                sources, stationary[a, :, lanes], preferred_element_type=jnp.float32
            )

        return [functools.partial(part, half) for half in range(2)]

    def weigh(p, scores, weights):
        def part(u, groups):
            s = table_ref[0, 2 * p + u]
            live = jnp.where(s >= 0, bit_of, 0)
            s = jnp.maximum(s, 0)
            for g in groups:
                edge = [
                    jnp.where(
                        (jnp.broadcast_to(words[w, pl.ds(s, 1), :], (8, TILE)) & live) != 0, 1.0, 0.0
                    )
                    for w in (2 * g, 2 * g + 1)
                ]
                edge = jnp.concatenate(edge, axis=0).astype(jnp.bfloat16)
                here = slice(u * TILE + g * STRIP, u * TILE + (g + 1) * STRIP)
                for h in range(HEADS):
                    lanes = slice(h * TILE, (h + 1) * TILE)
                    twice = jnp.tanh(scores[here, lanes] + half_bias[h]) + 1.0
                    weights[here, lanes] = twice.astype(jnp.bfloat16) * edge

        half = TILE // STRIP // 2
        return [
            functools.partial(part, u, range(v * half, (v + 1) * half))
            for u in range(2) for v in range(2)
        ]

    def mix(p, weights):
        a = table_ref[1, 2 * p]
        source = [table_ref[2, 2 * p + u] for u in range(2)]

        def part(half):
            rows = slice(half * TILE, (half + 1) * TILE)
            v = jnp.concatenate([values[b, rows, :] for b in source], axis=1)
            v = jnp.concatenate([v, ones], axis=0)
            both = jnp.dot(
                v, weights[:, half * 2 * TILE : (half + 1) * 2 * TILE],
                preferred_element_type=jnp.float32,
            )
            for side in range(2):
                start = half * TILE + side * HEAD
                num_acc[a, start : start + HEAD, :] += both[
                    side * HEAD : (side + 1) * HEAD, side * TILE : (side + 1) * TILE
                ]
            den_acc[a, half] += both[TILE : TILE + 8]

        return [functools.partial(part, half) for half in range(2)]

    def together(scored, mixed, weighed):
        for k in range(2):
            scored[k]()
            mixed[k]()
        for part in weighed:
            part()

    for part in score(0, even_scores):
        part()

    def turn(t, _):
        for u in range(0, UNROLL, 2):
            p = UNROLL * t + u
            together(
                score(p + 1, odd_scores), mix(jnp.maximum(p - 1, 0), odd_weights),
                weigh(p, even_scores, even_weights),
            )
            together(
                score(p + 2, even_scores), mix(p, even_weights),
                weigh(p + 1, odd_scores, odd_weights),
            )
        return 0

    turns = (pairs + UNROLL - 1) // UNROLL
    lax.fori_loop(0, turns, turn, 0)
    for part in mix(jnp.maximum(UNROLL * turns - 1, 0), odd_weights):
        part()
    num_ref[...] = (num_acc[...] * 0.5).astype(num_ref.dtype)
    for a in range(den_acc.shape[0]):
        for h in range(HEADS):
            lanes = slice(h % 2 * TILE, (h % 2 + 1) * TILE)
            den_ref[a, h : h + 1, :] = den_acc[a, h // 2, 0:1, lanes] * 0.5


def attention(table, bias, gathered, values, stationary, words):
    row_tiles = stationary.shape[0]
    smem = pl.BlockSpec(memory_space=pltpu.SMEM)
    vmem = pl.BlockSpec(memory_space=pltpu.VMEM)
    return pl.pallas_call(
        attention_kernel,
        out_shape=(
            jax.ShapeDtypeStruct((row_tiles, D, TILE), jnp.bfloat16),
            jax.ShapeDtypeStruct((row_tiles, HEADS, TILE), jnp.float32),
        ),
        in_specs=[smem] * 2 + [vmem] * 4,
        out_specs=(vmem, vmem),
        scratch_shapes=[
            pltpu.VMEM((row_tiles, D, TILE), jnp.float32),
            pltpu.VMEM((row_tiles, 2, 8, 2 * TILE), jnp.float32),
            pltpu.VMEM((2 * TILE, HEADS * TILE), jnp.float32),
            pltpu.VMEM((2 * TILE, HEADS * TILE), jnp.float32),
            pltpu.VMEM((2 * TILE, HEADS * TILE), jnp.bfloat16),
            pltpu.VMEM((2 * TILE, HEADS * TILE), jnp.bfloat16),
        ],
        compiler_params=pltpu.CompilerParams(vmem_limit_bytes=16 * 1024 * 1024),
        name="attention",
    )(table, bias, gathered, values, stationary, words)


def finish_kernel(
    features_ref, num_ref, den_ref, w_ref, gain_ref, out_ref,
    nums, dens, send, recv,
):
    z, x, y, core = position()
    y_lo = y % 2
    meet(site_partners(z, x, y, core))
    home = y_lo == core

    def part(d, src, dst, k):
        c = (y + d) % NY
        return pltpu.make_async_remote_copy(
            src_ref=src.at[c], dst_ref=dst.at[y], send_sem=send.at[k, d], recv_sem=recv.at[k, y],
            device_id=device(z, x, c // 2 * 2 + core, c % 2), device_id_type=MESH,
        )

    pairs = ((num_ref, nums), (den_ref, dens))
    for d in (1, 2, 3):
        for k, (src, dst) in enumerate(pairs):
            part(d, src, dst, k).start()
    for k, (src, dst) in enumerate(pairs):
        @pl.when(home)
        def _():
            pltpu.make_async_copy(src.at[y], dst.at[y], recv.at[k, y]).start()

        @pl.when(jnp.logical_not(home))
        def _():
            part(0, src, dst, k).start()

    for c in range(NY):
        for k, (src, dst) in enumerate(pairs):
            pltpu.make_async_copy(dst.at[c], dst.at[c], recv.at[k, c]).wait()
    total = sum(nums[c].astype(jnp.float32) for c in range(NY))
    weight = 1.0 + sum(dens[c] for c in range(NY))
    gain = gain_ref[...]
    node, lane_node = lane_order()
    to_nodes = jnp.transpose(jnp.where(node == lane_node, 1.0, 0.0)).astype(jnp.bfloat16)
    for t in range(NODES // TILE):
        mixed = total[t].reshape(HEADS, HEAD, TILE) / weight[t].reshape(HEADS, 1, TILE)
        mixed = mixed.reshape(D, TILE).astype(jnp.bfloat16)
        mixed = jnp.dot(mixed, to_nodes, preferred_element_type=jnp.float32).astype(jnp.bfloat16)
        projected = lax.dot_general(
            mixed, w_ref[...], (((0,), (0,)), ((), ())), preferred_element_type=jnp.float32
        )
        square = jnp.mean(projected * projected, axis=1, keepdims=True)
        here = pl.ds(t * TILE, TILE)
        out_ref[here, :] = features_ref[here, :] + gain * projected * lax.rsqrt(square + 1e-05)
    for d in range(NY):
        for k, (src, dst) in enumerate(pairs):
            if d:
                part(d, src, dst, k).wait_send()
            else:
                @pl.when(jnp.logical_not(home))
                def _():
                    part(d, src, dst, k).wait_send()


def finish(features, numerator, denominator, w_out, gain):
    vmem = pl.BlockSpec(memory_space=pltpu.VMEM)
    hbm = pl.BlockSpec(memory_space=pl.ANY)
    dma = pltpu.SemaphoreType.DMA
    return pl.pallas_call(
        finish_kernel,
        out_shape=jax.ShapeDtypeStruct(features.shape, jnp.float32),
        in_specs=[vmem, hbm, hbm, vmem, vmem],
        out_specs=vmem,
        scratch_shapes=[
            pltpu.VMEM(numerator.shape, numerator.dtype),
            pltpu.VMEM(denominator.shape, denominator.dtype),
            dma((2, NY)), dma((2, NY)),
        ],
        compiler_params=pltpu.CompilerParams(
            collective_id=1, has_side_effects=True, vmem_limit_bytes=32 * 1024 * 1024
        ),
        name="finish",
    )(features, numerator, denominator, w_out, gain)


def local(
    features, w_qkv, w_out, head_bias, out_gain, tile_rows, tile_cols, tile_masks, tile_count
):
    block_tiles = features.shape[0] // TILE
    gathered, values, stationary, words, table = exchange(
        features, tile_masks[0], jnp.concatenate([tile_rows, tile_cols], axis=0), tile_count, w_qkv
    )
    numerator, denominator = attention(
        table, head_bias, gathered, values, stationary, words
    )
    return finish(
        features,
        numerator.reshape(NY, block_tiles, D, TILE),
        denominator.reshape(NY, block_tiles, HEADS, TILE),
        w_out, out_gain[None, :],
    )


def solution(mesh):
    placed = (
        P(("row", "col"), None),
        P(),
        P(),
        P(),
        P(),
        P(("row", "col"), None),
        P(("row", "col"), None),
        P(("row", "col"), None, None),
        P(("row", "col")),
    )
    return jax.shard_map(
        local, mesh=mesh, in_specs=placed, out_specs=P(("row", "col"), None), check_vma=False
    )
```

```python
import functools

import jax
import jax.numpy as jnp
from jax import lax
from jax.experimental import pallas as pl
from jax.experimental.pallas import tpu as pltpu
from jax.sharding import PartitionSpec as P

TILE = 128
HEADS = 4
HEAD = 64
D = 256
STRIP = 16
UNROLL = 22
TABLE = 384
NX, NY, NZ = 4, 4, 8
SITES = NX * NZ
NODES = 384
FIRST = 160
SECOND = NODES - FIRST
BLOCK = NODES // TILE
MESH = pl.DeviceIdType.MESH
NT = (((1,), (1,)), ((), ()))


def position():
    row, col = lax.axis_index("row"), lax.axis_index("col")
    return row // 8, row // 2 % 4, col // 2 * 2 + row % 2, col % 2


def device(z, x, y, core):
    return ((z * NX + x) * 2 + y % 2, y // 2 * 2 + core)


def meet(partners, meanwhile=None):
    barrier = pltpu.get_barrier_semaphore()
    for partner in partners:
        pl.semaphore_signal(barrier, inc=1, device_id=partner, device_id_type=MESH)
    if meanwhile is not None:
        meanwhile()
    pl.semaphore_wait(barrier, len(partners))


def site_partners(z, x, y, core):
    found = [device(z, x, y, 1 - core)]
    for d in range(1, NY):
        found += [device(z, x, (y + d) % NY, core), device(z, x, (y + d) % NY, 1 - core)]
    return found


def lane_order():
    node = lax.broadcasted_iota(jnp.int32, (TILE, TILE), 0)
    lane = lax.broadcasted_iota(jnp.int32, (TILE, TILE), 1)
    return node, lane % 16 * 8 + lane // 16


def exchange_kernel(
    features_ref, masks_ref, lists_ref, count_ref, weights_ref,
    gathered, values, stationary, words, table,
    queries, own, own_queries, wq, wv, bits, landed, sorted_slots, diagonal,
    query_send, query_recv, list_send, list_recv,
    ring_send, first_x, first_z, second_z, second_x, sibling_send, sibling_recv,
):
    z, x, y, core = position()
    y_lo, y_hi = y % 2, y // 2
    site = z * NX + x

    def setup():
        own[...] = features_ref[...].astype(jnp.bfloat16)

    meet(
        site_partners(z, x, y, core)
        + [device(z, (x + d) % NX, y, core) for d in (1, 2, 3)]
        + [device((z + d) % NZ, x, y, core) for d in (1, 7)],
        setup,
    )

    my_list = y_hi * 2 + core
    home = y_lo == core
    partner = device(z, x, y_hi * 2 + core, y_lo)

    def to_partner(src, dst, k):
        return pltpu.make_async_remote_copy(
            src_ref=src, dst_ref=dst, send_sem=list_send.at[k], recv_sem=list_recv.at[k],
            device_id=partner, device_id_type=MESH,
        )

    def hand_over(src, dst, k):
        @pl.when(home)
        def _():
            pltpu.make_async_copy(src, dst, list_recv.at[k]).start()

        @pl.when(jnp.logical_not(home))
        def _():
            to_partner(src, dst, k).start()

    def handed(ref, k):
        pltpu.make_async_copy(ref, ref, list_recv.at[k]).wait()

    def rows(a_site, parity, low, count):
        return pl.ds(pl.multiple_of((a_site * 2 + parity) * NODES + low, 16), count)

    def remote(src, dst, send, recv, target):
        pltpu.make_async_remote_copy(
            src_ref=src, dst_ref=dst, send_sem=send, recv_sem=recv,
            device_id=target, device_id_type=MESH,
        ).start()

    def arrived(a_site, low, count, sem):
        here = gathered.at[rows(a_site, core, low, count)]
        pltpu.make_async_copy(here, here, sem).wait()

    def forward(a_site, low, count, send, recv, target):
        here = gathered.at[rows(a_site, core, low, count)]
        remote(here, here, send, recv, target)

    up, down = device((z + 1) % NZ, x, y, core), device((z + 7) % NZ, x, y, core)
    right, left = device(z, (x + 1) % NX, y, core), device(z, (x + 3) % NX, y, core)
    across = device(z, (x + 2) % NX, y, core)
    other = device(z, x, y, 1 - core)
    z_to, x_to = (up, down), (right, left)

    def site_of(dz, dx):
        return (z + dz + NZ) % NZ * NX + (x + dx + NX) % NX

    def to_queries(d):
        return pltpu.make_async_remote_copy(
            src_ref=own_queries, dst_ref=queries.at[my_list],
            send_sem=query_send.at[d], recv_sem=query_recv.at[my_list],
            device_id=device(z, x, (y_hi * 2 + core + d) % NY, y_lo), device_id_type=MESH,
        )

    def prepare():
        wq[...] = jnp.transpose(weights_ref[:, 0:D])
        wv[...] = jnp.transpose(weights_ref[:, 2 * D : 3 * D])
        diagonal[...] = jnp.zeros_like(diagonal)
        node, lane_node = lane_order()
        to_lanes = jnp.where(node == lane_node, 1.0, 0.0).astype(jnp.bfloat16)
        q = lax.dot_general(wq[...], own[...], NT, preferred_element_type=jnp.float32)
        q = q.astype(jnp.bfloat16) * jnp.bfloat16(0.0625)
        for t in range(BLOCK):
            own_queries[t] = jnp.dot(
                q[:, t * TILE : (t + 1) * TILE], to_lanes, preferred_element_type=jnp.float32
            ).astype(jnp.bfloat16)

    def fold(c, t):
        if t == 0:
            pltpu.make_async_copy(queries.at[c], queries.at[c], query_recv.at[c]).wait()
        for h in range(HEADS):
            diagonal[h * HEAD : (h + 1) * HEAD, h * TILE : (h + 1) * TILE] = (
                queries[c, t, h * HEAD : (h + 1) * HEAD, :]
            )
        stationary[c * BLOCK + t] = jnp.dot(
            weights_ref[:, D : 2 * D], diagonal[...], preferred_element_type=jnp.float32
        ).astype(jnp.bfloat16)

    def spread(c):
        words[c] = landed[:, c * TILE : (c + 1) * TILE].astype(jnp.float32).astype(jnp.int32)

    def swap_bit(b):
        step = 1 << b
        slots = words.shape[1]
        upper = (lax.broadcasted_iota(jnp.int32, (slots, TILE), 1) // step) % 2 == 1
        for c in range(words.shape[0]):
            if c & step == 0:
                low, high = words[c], words[c + step]
                words[c] = jnp.where(upper, pltpu.roll(high, step, 1), low)
                words[c + step] = jnp.where(upper, high, pltpu.roll(low, TILE - step, 1))

    def start_words():
        handed(landed, 1)
        for c in range(words.shape[0]):
            spread(c)

    placed = []

    def sort_slots():
        slots = lists_ref.shape[1]
        row_tiles = NY * BLOCK
        to, source = (lists_ref[k : k + 1, :].astype(jnp.float32) for k in range(2))
        count = jnp.full((1, slots), count_ref[0], jnp.int32).astype(jnp.float32)
        slot = lax.broadcasted_iota(jnp.int32, (1, slots), 1).astype(jnp.float32)
        a = to - row_tiles * jnp.floor((to + 0.5) * (1.0 / row_tiles))
        b = BLOCK * jnp.floor((source + 0.5) * (1.0 / row_tiles)) + (
            source - BLOCK * jnp.floor((source + 0.5) * (1.0 / BLOCK))
        )
        a = jnp.where(slot < count, a, float(row_tiles))
        base = jnp.zeros_like(a)
        total = jnp.zeros((1, 1), jnp.float32)
        for tile in range(row_tiles):
            number = jnp.sum(jnp.where(a == tile, 1.0, 0.0), axis=1, keepdims=True)
            number = 2.0 * jnp.floor((number + 1.5) * 0.5)
            base += jnp.where(a > tile, number, 0.0)
            total += number
        across_lanes = jnp.broadcast_to(a, (slots, slots))
        down = jnp.transpose(across_lanes)
        earlier = lax.broadcasted_iota(jnp.int32, (slots, slots), 0) < lax.broadcasted_iota(
            jnp.int32, (slots, slots), 1
        )
        rank = jnp.sum(
            jnp.where((across_lanes == down) & earlier, 1.0, 0.0), axis=0, keepdims=True
        )
        at = jnp.where(a < row_tiles, base + rank, float(TABLE))
        placed.extend([slots, row_tiles, slot, a, b, total, at])

    def list_slots():
        slots, row_tiles, slot, a, b, total, at = placed
        at_down = jnp.transpose(jnp.broadcast_to(at, (TABLE, slots)))
        hit = at_down == lax.broadcasted_iota(jnp.int32, (slots, TABLE), 1).astype(jnp.float32)

        def pick(value):
            down = jnp.transpose(jnp.broadcast_to(value, (TABLE, slots)))
            return jnp.sum(jnp.where(hit, down, 0.0), axis=0, keepdims=True)

        sorted_slots[0:1, :] = (pick(slot + 1.0) - 1.0).astype(jnp.int32)
        sorted_slots[1:2, :] = pick(a).astype(jnp.int32)
        sorted_slots[2:3, :] = pick(b).astype(jnp.int32)
        sorted_slots[3:4, :] = jnp.broadcast_to(total * 0.5, (1, TABLE)).astype(jnp.int32)
        sorted_slots[4:8, :] = jnp.zeros((4, TABLE), jnp.int32)
        hand_over(sorted_slots, table, 2)

    hand_over(own, gathered.at[rows(site, y_lo, 0, NODES)], 0)

    @pl.when(jnp.logical_not(home))
    def _():
        prepare()

    handed(gathered.at[rows(site, core, 0, NODES)], 0)
    for s in range(2):
        forward(site, FIRST, SECOND, ring_send.at[s], second_z.at[s, 0], z_to[s])
        forward(site, 0, FIRST, ring_send.at[2 + s], first_x.at[s], x_to[s])
    forward(site, 0, FIRST, ring_send.at[4], first_x.at[2], across)
    for s in range(2):
        forward(site, FIRST, SECOND, ring_send.at[2 + s], second_x.at[0, s, 0], x_to[s])
        forward(site, 0, FIRST, ring_send.at[s], first_z.at[s, 0, 0], z_to[s])

    @pl.when(home)
    def _():
        prepare()
        pltpu.make_async_copy(own_queries, queries.at[my_list], query_recv.at[my_list]).start()

    @pl.when(jnp.logical_not(home))
    def _():
        to_queries(0).start()

    for d in (1, 2, 3):
        to_queries(d).start()
    bits[...] = masks_ref[...].astype(jnp.float32).astype(jnp.bfloat16)
    hand_over(bits, landed, 1)

    X_OFF = (0, -1, 1, 2)
    Z_OFF = (0, -1, 1, -2, 2, -3, 3, 4)
    HALF1, HALF2 = FIRST // 2, SECOND // 2

    def second_z_step(t):
        for s in range(2):
            sign = -1 if s == 0 else 1
            if t < 4:
                a = site_of(sign * t, 0)
                arrived(a, FIRST, SECOND, second_z.at[s, t - 1])
                if t < 3:
                    forward(a, FIRST, SECOND, ring_send.at[s], second_z.at[s, t], z_to[s])
                else:
                    forward(a, FIRST + s * HALF2, HALF2, ring_send.at[s], second_z.at[s, 3], z_to[s])
                k = Z_OFF.index(sign * t)
                for e in range(2):
                    forward(a, FIRST, SECOND, ring_send.at[2 + e], second_x.at[k, e, 0], x_to[e])
        if t == 4:
            a = site_of(4, 0)
            for s in range(2):
                arrived(a, FIRST + s * HALF2, HALF2, second_z.at[s, 3])
            for e in range(2):
                forward(a, FIRST, SECOND, ring_send.at[2 + e], second_x.at[7, e, 0], x_to[e])

    def first_x_step(*which):
        for k in which:
            a = site_of(0, X_OFF[k + 1])
            arrived(a, 0, FIRST, first_x.at[k])
            for s in range(2):
                forward(a, 0, FIRST, ring_send.at[s], first_z.at[s, 0, k + 1], z_to[s])

    def first_z_step(t, k):
        if t < 4:
            for s in range(2):
                sign = -1 if s == 0 else 1
                a = site_of(sign * t, X_OFF[k])
                arrived(a, 0, FIRST, first_z.at[s, t - 1, k])
                if t < 3:
                    forward(a, 0, FIRST, ring_send.at[s], first_z.at[s, t, k], z_to[s])
                else:
                    forward(a, s * HALF1, HALF1, ring_send.at[s], first_z.at[s, 3, k], z_to[s])
        else:
            a = site_of(4, X_OFF[k])
            for s in range(2):
                arrived(a, s * HALF1, HALF1, first_z.at[s, 3, k])

    def second_x_step(k):
        for e in range(2):
            sign = -1 if e == 0 else 1
            a = site_of(Z_OFF[k], sign)
            arrived(a, FIRST, SECOND, second_x.at[k, e, 0])
            forward(a, FIRST + e * HALF2, HALF2, ring_send.at[2 + e], second_x.at[k, e, 1], x_to[e])

    def second_x_end(k):
        a = site_of(Z_OFF[k], 2)
        for e in range(2):
            arrived(a, FIRST + e * HALF2, HALF2, second_x.at[k, e, 1])

    def project(*blocks):
        sites = [site_of(dz, X_OFF[k]) for dz, k in blocks]
        for a in sites:
            forward(a, 0, NODES, sibling_send.at[0], sibling_recv.at[0], other)
        found = [
            lax.dot_general(
                wv[...], gathered[rows(a, core, 0, NODES), :], NT, preferred_element_type=jnp.float32
            ).astype(jnp.bfloat16)
            for a in sites
        ]
        for a, v in zip(sites, found):
            for t in range(BLOCK):
                values[(a * 2 + core) * BLOCK + t] = v[:, t * TILE : (t + 1) * TILE]
        for a in sites:
            done = values.at[pl.ds((a * 2 + core) * BLOCK, BLOCK)]
            remote(done, done, sibling_send.at[1], sibling_recv.at[1], other)

    def drain(count, sem):
        pltpu.make_async_copy(gathered.at[pl.ds(0, count)], gathered.at[pl.ds(0, count)], sem).wait()

    order = [
        (second_z_step, 1), (first_x_step, 0, 1), (first_z_step, 1, 0), (fold, 0, 0), (second_z_step, 2),
        (fold, 0, 1), (second_x_step, 0), (first_x_step, 2), (fold, 0, 2), (project, (1, 0), (-1, 0)),
        (fold, 1, 0), (project, (0, 0), (0, 1)), (fold, 1, 1), (fold, 1, 2), (second_x_step, 1),
        (sort_slots,), (first_z_step, 1, 1), (second_x_step, 2), (first_z_step, 2, 0),
        (project, (2, 0), (-2, 0)), (list_slots,), (first_z_step, 1, 2), (fold, 2, 0), (fold, 2, 1),
        (project, (1, 1), (-1, 1)), (second_z_step, 3), (start_words,), (first_z_step, 1, 3),
        (project, (1, 2), (-1, 2)), (swap_bit, 0), (fold, 2, 2), (second_x_step, 3), (swap_bit, 1),
        (fold, 3, 0), (second_x_end, 0), (second_x_end, 1), (second_x_step, 4), (first_z_step, 2, 1),
        (swap_bit, 2), (project, (2, 1), (-2, 1)), (first_z_step, 2, 2), (project, (0, 2), (0, 3)),
        (second_z_step, 4), (fold, 3, 1), (second_x_end, 2), (project, (1, 3), (-1, 3)), (first_z_step, 2, 3),
        (fold, 3, 2), (swap_bit, 3), (second_x_end, 3), (first_z_step, 3, 0), (second_x_step, 5),
        (second_x_step, 6), (first_z_step, 3, 1), (project, (3, 1), (-3, 1)), (second_x_end, 4),
        (project, (3, 0), (-3, 0)), (first_z_step, 3, 2), (project, (3, 2), (-3, 2)), (second_x_step, 7),
        (first_z_step, 3, 3), (project, (2, 2), (-2, 2)), (project, (2, 3), (-2, 3)), (second_x_end, 5),
        (second_x_end, 6), (project, (3, 3), (-3, 3)), (first_z_step, 4, 0), (first_z_step, 4, 1),
        (first_z_step, 4, 2), (project, (4, 0), (4, 1)), (second_x_end, 7), (first_z_step, 4, 3),
        (project, (4, 2), (4, 3)),
    ]
    for step in order:
        step[0](*step[1:])

    half_values = values.at[pl.ds(0, SITES * BLOCK)]
    pltpu.make_async_copy(half_values, half_values, sibling_recv.at[1]).wait()
    pltpu.make_async_copy(half_values, half_values, sibling_send.at[1]).wait()
    drain(SITES * NODES, sibling_recv.at[0])
    drain(SITES * NODES, sibling_send.at[0])
    z_rows = 3 * SECOND + HALF2 + NX * (3 * FIRST + HALF1)
    x_rows = FIRST + NZ * (SECOND + HALF2)
    for s in range(2):
        drain(z_rows, ring_send.at[s])
        drain(x_rows, ring_send.at[2 + s])
    drain(FIRST, ring_send.at[4])
    for d in range(1, NY):
        to_queries(d).wait_send()
    handed(table, 2)

    @pl.when(jnp.logical_not(home))
    def _():
        to_queries(0).wait_send()
        to_partner(own, gathered.at[rows(site, y_lo, 0, NODES)], 0).wait_send()
        to_partner(bits, landed, 1).wait_send()
        to_partner(sorted_slots, table, 2).wait_send()


def exchange(features, masks, lists, tile_count, weights):
    slots, length = masks.shape
    vmem = pl.BlockSpec(memory_space=pltpu.VMEM)
    smem = pl.BlockSpec(memory_space=pltpu.SMEM)
    dma = pltpu.SemaphoreType.DMA
    half = jnp.bfloat16
    return pl.pallas_call(
        exchange_kernel,
        out_shape=(
            jax.ShapeDtypeStruct((SITES * 2 * NODES, D), half),
            jax.ShapeDtypeStruct((SITES * 2 * BLOCK, D, TILE), half),
            jax.ShapeDtypeStruct((NY * BLOCK, D, HEADS * TILE), half),
            jax.ShapeDtypeStruct((length // TILE, slots, TILE), jnp.int32),
            jax.ShapeDtypeStruct((8, TABLE), jnp.int32),
        ),
        in_specs=[vmem, vmem, vmem, smem, vmem],
        out_specs=(vmem,) * 5,
        scratch_shapes=[
            pltpu.VMEM((NY, BLOCK, D, TILE), half),
            pltpu.VMEM((NODES, D), half),
            pltpu.VMEM((BLOCK, D, TILE), half),
            pltpu.VMEM((D, D), half),
            pltpu.VMEM((D, D), half),
            pltpu.VMEM((slots, length), half),
            pltpu.VMEM((slots, length), half),
            pltpu.VMEM((8, TABLE), jnp.int32),
            pltpu.VMEM((D, HEADS * TILE), half),
            dma((NY,)), dma((NY,)), dma((3,)), dma((3,)),
            dma((5,)), dma((3,)), dma((2, 4, NX)), dma((2, 4)), dma((NZ, 2, 2)), dma((2,)), dma((2,)),
        ],
        compiler_params=pltpu.CompilerParams(
            collective_id=0, has_side_effects=True, vmem_limit_bytes=16 * 1024 * 1024
        ),
        name="exchange",
    )(features, masks, lists, tile_count, weights)


def attention_kernel(
    table_ref, bias_ref, gathered, values, stationary, words,
    num_ref, den_ref, num_acc, den_acc, even_scores, odd_scores, even_weights, odd_weights,
):
    pairs = table_ref[3, 0]
    num_acc[...] = jnp.zeros_like(num_acc)
    den_acc[...] = jnp.zeros_like(den_acc)
    odd_weights[...] = jnp.zeros_like(odd_weights)
    bit_of = jnp.left_shift(jnp.int32(1), lax.broadcasted_iota(jnp.int32, (8, TILE), 0))
    half_bias = [bias_ref[h] * 0.5 for h in range(HEADS)]
    ones = jnp.ones((STRIP, 2 * TILE), jnp.bfloat16)

    def score(p, scores):
        a = table_ref[1, 2 * p]
        sources = jnp.concatenate(
            [
                gathered[pl.ds(pl.multiple_of(table_ref[2, 2 * p + u] * TILE, TILE), TILE), :]
                for u in range(2)
            ],
            axis=0,
        )

        def part(half):
            lanes = slice(half * 2 * TILE, (half + 1) * 2 * TILE)
            scores[:, lanes] = jnp.dot(
                sources, stationary[a, :, lanes], preferred_element_type=jnp.float32
            )

        return [functools.partial(part, half) for half in range(2)]

    def weigh(p, scores, weights):
        def part(u, groups):
            s = table_ref[0, 2 * p + u]
            live = jnp.where(s >= 0, bit_of, 0)
            s = jnp.maximum(s, 0)
            for g in groups:
                edge = [
                    jnp.where(
                        (jnp.broadcast_to(words[w, pl.ds(s, 1), :], (8, TILE)) & live) != 0, 1.0, 0.0
                    )
                    for w in (2 * g, 2 * g + 1)
                ]
                edge = jnp.concatenate(edge, axis=0).astype(jnp.bfloat16)
                here = slice(u * TILE + g * STRIP, u * TILE + (g + 1) * STRIP)
                for h in range(HEADS):
                    lanes = slice(h * TILE, (h + 1) * TILE)
                    twice = jnp.tanh(scores[here, lanes] + half_bias[h]) + 1.0
                    weights[here, lanes] = twice.astype(jnp.bfloat16) * edge

        half = TILE // STRIP // 2
        return [
            functools.partial(part, u, range(v * half, (v + 1) * half))
            for u in range(2) for v in range(2)
        ]

    def mix(p, weights):
        a = table_ref[1, 2 * p]
        source = [table_ref[2, 2 * p + u] for u in range(2)]

        def part(half):
            rows = slice(half * TILE, (half + 1) * TILE)
            v = jnp.concatenate([values[b, rows, :] for b in source], axis=1)
            v = jnp.concatenate([v, ones], axis=0)
            both = jnp.dot(
                v, weights[:, half * 2 * TILE : (half + 1) * 2 * TILE],
                preferred_element_type=jnp.float32,
            )
            for side in range(2):
                start = half * TILE + side * HEAD
                num_acc[a, start : start + HEAD, :] += both[
                    side * HEAD : (side + 1) * HEAD, side * TILE : (side + 1) * TILE
                ]
            den_acc[a, half] += both[TILE : TILE + 8]

        return [functools.partial(part, half) for half in range(2)]

    def together(scored, mixed, weighed):
        for k in range(2):
            scored[k]()
            mixed[k]()
        for part in weighed:
            part()

    for part in score(0, even_scores):
        part()

    def turn(t, _):
        for u in range(0, UNROLL, 2):
            p = UNROLL * t + u
            together(
                score(p + 1, odd_scores), mix(jnp.maximum(p - 1, 0), odd_weights),
                weigh(p, even_scores, even_weights),
            )
            together(
                score(p + 2, even_scores), mix(p, even_weights),
                weigh(p + 1, odd_scores, odd_weights),
            )
        return 0

    turns = (pairs + UNROLL - 1) // UNROLL
    lax.fori_loop(0, turns, turn, 0)
    for part in mix(jnp.maximum(UNROLL * turns - 1, 0), odd_weights):
        part()
    num_ref[...] = (num_acc[...] * 0.5).astype(num_ref.dtype)
    for a in range(den_acc.shape[0]):
        for h in range(HEADS):
            lanes = slice(h % 2 * TILE, (h % 2 + 1) * TILE)
            den_ref[a, h : h + 1, :] = den_acc[a, h // 2, 0:1, lanes] * 0.5


def attention(table, bias, gathered, values, stationary, words):
    row_tiles = stationary.shape[0]
    smem = pl.BlockSpec(memory_space=pltpu.SMEM)
    vmem = pl.BlockSpec(memory_space=pltpu.VMEM)
    return pl.pallas_call(
        attention_kernel,
        out_shape=(
            jax.ShapeDtypeStruct((row_tiles, D, TILE), jnp.bfloat16),
            jax.ShapeDtypeStruct((row_tiles, HEADS, TILE), jnp.float32),
        ),
        in_specs=[smem] * 2 + [vmem] * 4,
        out_specs=(vmem, vmem),
        scratch_shapes=[
            pltpu.VMEM((row_tiles, D, TILE), jnp.float32),
            pltpu.VMEM((row_tiles, 2, 8, 2 * TILE), jnp.float32),
            pltpu.VMEM((2 * TILE, HEADS * TILE), jnp.float32),
            pltpu.VMEM((2 * TILE, HEADS * TILE), jnp.float32),
            pltpu.VMEM((2 * TILE, HEADS * TILE), jnp.bfloat16),
            pltpu.VMEM((2 * TILE, HEADS * TILE), jnp.bfloat16),
        ],
        compiler_params=pltpu.CompilerParams(vmem_limit_bytes=16 * 1024 * 1024),
        name="attention",
    )(table, bias, gathered, values, stationary, words)


def finish_kernel(
    features_ref, num_ref, den_ref, w_ref, gain_ref, out_ref,
    nums, dens, send, recv,
):
    z, x, y, core = position()
    y_lo = y % 2
    meet(site_partners(z, x, y, core))
    home = y_lo == core

    def part(d, src, dst, k):
        c = (y + d) % NY
        return pltpu.make_async_remote_copy(
            src_ref=src.at[c], dst_ref=dst.at[y], send_sem=send.at[k, d], recv_sem=recv.at[k, y],
            device_id=device(z, x, c // 2 * 2 + core, c % 2), device_id_type=MESH,
        )

    pairs = ((num_ref, nums), (den_ref, dens))
    for d in (1, 2, 3):
        for k, (src, dst) in enumerate(pairs):
            part(d, src, dst, k).start()
    for k, (src, dst) in enumerate(pairs):
        @pl.when(home)
        def _():
            pltpu.make_async_copy(src.at[y], dst.at[y], recv.at[k, y]).start()

        @pl.when(jnp.logical_not(home))
        def _():
            part(0, src, dst, k).start()

    node, lane_node = lane_order()
    to_nodes = jnp.transpose(jnp.where(node == lane_node, 1.0, 0.0)).astype(jnp.bfloat16)
    for c in range(NY):
        for k, (src, dst) in enumerate(pairs):
            pltpu.make_async_copy(dst.at[c], dst.at[c], recv.at[k, c]).wait()
    total = sum(nums[c].astype(jnp.float32) for c in range(NY))
    weight = 1.0 + sum(dens[c] for c in range(NY))
    gain = gain_ref[...]
    for t in range(NODES // TILE):
        mixed = total[t].reshape(HEADS, HEAD, TILE) / weight[t].reshape(HEADS, 1, TILE)
        mixed = mixed.reshape(D, TILE).astype(jnp.bfloat16)
        mixed = jnp.dot(mixed, to_nodes, preferred_element_type=jnp.float32).astype(jnp.bfloat16)
        projected = lax.dot_general(
            mixed, w_ref[...], (((0,), (0,)), ((), ())), preferred_element_type=jnp.float32
        )
        square = jnp.mean(projected * projected, axis=1, keepdims=True)
        here = pl.ds(t * TILE, TILE)
        out_ref[here, :] = features_ref[here, :] + gain * projected * lax.rsqrt(square + 1e-05)
    for d in range(NY):
        for k, (src, dst) in enumerate(pairs):
            if d:
                part(d, src, dst, k).wait_send()
            else:
                @pl.when(jnp.logical_not(home))
                def _():
                    part(d, src, dst, k).wait_send()


def finish(features, numerator, denominator, w_out, gain):
    vmem = pl.BlockSpec(memory_space=pltpu.VMEM)
    hbm = pl.BlockSpec(memory_space=pl.ANY)
    dma = pltpu.SemaphoreType.DMA
    return pl.pallas_call(
        finish_kernel,
        out_shape=jax.ShapeDtypeStruct(features.shape, jnp.float32),
        in_specs=[vmem, hbm, hbm, vmem, vmem],
        out_specs=vmem,
        scratch_shapes=[
            pltpu.VMEM(numerator.shape, numerator.dtype),
            pltpu.VMEM(denominator.shape, denominator.dtype),
            dma((2, NY)), dma((2, NY)),
        ],
        compiler_params=pltpu.CompilerParams(
            collective_id=1, has_side_effects=True, vmem_limit_bytes=32 * 1024 * 1024
        ),
        name="finish",
    )(features, numerator, denominator, w_out, gain)


def local(
    features, w_qkv, w_out, head_bias, out_gain, tile_rows, tile_cols, tile_masks, tile_count
):
    block_tiles = features.shape[0] // TILE
    gathered, values, stationary, words, table = exchange(
        features, tile_masks[0], jnp.concatenate([tile_rows, tile_cols], axis=0), tile_count, w_qkv
    )
    numerator, denominator = attention(
        table, head_bias, gathered, values, stationary, words
    )
    return finish(
        features,
        numerator.reshape(NY, block_tiles, D, TILE),
        denominator.reshape(NY, block_tiles, HEADS, TILE),
        w_out, out_gain[None, :],
    )


def solution(mesh):
    placed = (
        P(("row", "col"), None),
        P(),
        P(),
        P(),
        P(),
        P(("row", "col"), None),
        P(("row", "col"), None),
        P(("row", "col"), None, None),
        P(("row", "col")),
    )
    return jax.shard_map(
        local, mesh=mesh, in_specs=placed, out_specs=P(("row", "col"), None), check_vma=False
    )
```
